32 devices in a mesh: dp: 2 (over core), region: 16 (over z, y, x).
Axes of the slice: x: 2, y: 2, z: 4, core: 2. Of those that a mesh axis runs over, the one named last changes fastest.
Arguments:
- cell_counts: int32 [16384], P('dp'), may hold values from 61 to 6144, as said below
- cell_seeds: int32 [16384], P('dp'), may hold values from 0 to 12287
- batch_ids: int32 [16384], P('dp'), may hold values from 0 to 7
- noise_draw: float32 [16384, 10], P('dp'), may hold values from -4 to 4
- cell_factor: float32 [16384], P('dp'), may hold values from 0.3 to 0.95
- enc_weight: float32 [12288, 128], P('region', 'dp'), may hold values from -0.0546875 to 0.0546875
- enc_first: float32 [12288, 128], P('region', 'dp'), may hold values from -1.1444092e-05 to 1.1444092e-05
- enc_second: float32 [12288, 128], P('region', 'dp'), may hold values from 3.4924596e-12 to 1.3969838e-11
- dec_weight: float32 [128, 12288], P('dp', 'region'), may hold values from -0.5 to 0.5
- dec_first: float32 [128, 12288], P('dp', 'region'), may hold values from -7.1525574e-07 to 7.1525574e-07
- dec_second: float32 [128, 12288], P('dp', 'region'), may hold values from 1.6168795e-14 to 6.467518e-14
- region_vecs: float32 [2, 12288], P('dp', 'region')
- vec_first: float32 [2, 12288], P('dp', 'region'), may hold values from -1.335144e-05 to 1.335144e-05
- vec_second: float32 [2, 12288], P('dp', 'region'), may hold values from 4.6566128e-12 to 1.8626451e-11
- trunk_rows: float32 [290, 128], replicated
- trunk_first: float32 [290, 128], replicated, may hold values from -1.5258789e-05 to 1.5258789e-05
- trunk_second: float32 [290, 128], replicated, may hold values from 6.2088173e-12 to 2.483527e-11
- head_rows: float32 [129, 20], replicated
- head_first: float32 [129, 20], replicated, may hold values from -1.5258789e-05 to 1.5258789e-05
- head_second: float32 [129, 20], replicated, may hold values from 6.2088173e-12 to 2.483527e-11
Outputs:
- loss: float32 [2], replicated
- enc_new: float32 [12288, 128], P('region', 'dp')
- enc_first_new: float32 [12288, 128], P('region', 'dp')
- enc_second_new: float32 [12288, 128], P('region', 'dp')
- enc_copy: bfloat16 [12288, 128], P('region', 'dp')
- dec_new: float32 [128, 12288], P('dp', 'region')
- dec_first_new: float32 [128, 12288], P('dp', 'region')
- dec_second_new: float32 [128, 12288], P('dp', 'region')
- dec_copy: bfloat16 [128, 12288], P('dp', 'region')
- vecs_new: float32 [2, 12288], P('dp', 'region')
- vec_first_new: float32 [2, 12288], P('dp', 'region')
- vec_second_new: float32 [2, 12288], P('dp', 'region')
- trunk_new: float32 [290, 128], replicated
- trunk_first_new: float32 [290, 128], replicated
- trunk_second_new: float32 [290, 128], replicated
- head_new: float32 [129, 20], replicated
- head_first_new: float32 [129, 20], replicated
- head_second_new: float32 [129, 20], replicated
- norms: float32 [2, 10], replicated
The draws below stay inside these ranges and needn't reach their ends.
Inputs may be any that keep to these rules, and one draw needn't show every extreme that they name: Each cell opens exactly cell_counts regions, given by the rule of the first step; some cell holds the smallest and some the largest count.
All inputs are finite; a program needn't handle non-finite values.
Results may differ from the reference program's by a relative error of at most 0.002.
The reference program's roundings to bfloat16 on the way count: a program that leaves them out, or rounds other values in their place, can miss the bound.
Values may be sent and summed in bfloat16 or wider, within the bound.
No kernel may reach another device: no remote copies, remote signals or barrier semaphores. Data moves between devices by JAX's collectives and lax.ppermute only.
A program may use at most 128 MiB of HBM per device.

```python
import math
import jax
import jax.numpy as jnp
from jax import lax

H = 128
L = 10
BATCHES = 8
R = 12288
CELLS = 16384
TR = 290


def draw_cell_counts(key, part):
    lowest = R // 200
    highest_count = R // 2
    counts = jax.random.randint(key, (CELLS,), lowest, highest_count + 1)
    positions = jnp.arange(CELLS, dtype=jnp.int32)
    counts = jnp.where(positions == 0, highest_count, counts)
    counts = jnp.where(positions == CELLS - 1, lowest, counts)
    return counts.astype(jnp.int32)


def draw_region_vecs(key, part):
    bias_key = jax.random.fold_in(key, 11)
    logit_key = jax.random.fold_in(key, 12)
    bias_row = 0.3 * jax.random.normal(bias_key, (1, R), jnp.float32)
    placement = jnp.arange(R, dtype=jnp.float32) / (R - 1.0)
    rough = jax.random.uniform(logit_key, (1, R), jnp.float32, -1.0, 1.0)
    logit_row = -2.5 + 5.0 * placement[None, :] + rough
    return jnp.concatenate([bias_row, logit_row], axis=0)


def draw_trunk_rows(key, part):
    weight_key = jax.random.fold_in(key, 21)
    gain_key = jax.random.fold_in(key, 22)
    shift_key = jax.random.fold_in(key, 23)
    weight_count = 2 * BATCHES + 2 * H + L
    scales = jnp.concatenate([jnp.full((BATCHES,), 0.3, jnp.float32), jnp.full((H,), H ** (-0.5), jnp.float32), jnp.full((L + BATCHES,), (L + BATCHES) ** (-0.5), jnp.float32), jnp.full((H,), H ** (-0.5), jnp.float32)])
    weights = jax.random.normal(weight_key, (weight_count, H), jnp.float32) * scales[:, None]
    gains = jax.random.uniform(gain_key, (4, H), jnp.float32, 0.7, 1.3)
    shifts = jax.random.uniform(shift_key, (4, H), jnp.float32, -0.3, 0.3)
    return jnp.concatenate([weights, gains, shifts], axis=0)


def draw_head_rows(key, part):
    weight_key = jax.random.fold_in(key, 31)
    centre_key = jax.random.fold_in(key, 32)
    spread_key = jax.random.fold_in(key, 33)
    column_scale = jnp.concatenate([jnp.full((L,), H ** (-0.5), jnp.float32), jnp.full((L,), 0.3 * H ** (-0.5), jnp.float32)])
    weights = jax.random.normal(weight_key, (H, 2 * L), jnp.float32) * column_scale[None, :]
    centre_bias = 0.3 * jax.random.normal(centre_key, (1, L), jnp.float32)
    spread_bias = jax.random.uniform(spread_key, (1, L), jnp.float32, -1.5, -0.5)
    return jnp.concatenate([weights, jnp.concatenate([centre_bias, spread_bias], axis=1)], axis=0)


def with_ends(values, stream_key, low, largest):
    shape = values.shape
    place = [jax.random.randint(jax.random.fold_in(stream_key, axis), (), 0, shape[axis]) for axis in range(len(shape))]
    values = values.at[tuple(place)].set(low)
    longest = shape.index(max(shape))
    place[longest] = (place[longest] + 1) % shape[longest]
    return values.at[tuple(place)].set(largest)


def steps_of(stream_key, extent, cuts, smallest, largest):
    def one(position, shards_of):
        heights = jax.random.uniform(jax.random.fold_in(jax.random.fold_in(stream_key, 6), position), (shards_of,), jnp.float32, smallest / len(cuts), largest / len(cuts))
        return jnp.repeat(jnp.exp(heights), extent[position] // shards_of).reshape((-1,) + (1,) * (len(extent) - position - 1))

    level = one(*cuts[0])
    for cut in cuts[1:]:
        level = level * one(*cut)
    return level


def noise(stream_key, shape, scale, limit, split=(), held_as=jnp.bfloat16):
    array = scale * jax.random.normal(stream_key, shape, jnp.float32)
    if split:
        array = array * steps_of(stream_key, shape, split, -0.22, 0.18)
    return jnp.clip(array, -limit, limit).astype(held_as)


def setup_inputs(seed: int = 0) -> dict:
    keys = jax.random.split(jax.random.key(seed), 21)
    return {
        "cell_counts": draw_cell_counts(jax.random.fold_in(keys[20], 71), 0),
        "cell_seeds": with_ends(jax.random.randint(keys[1], (CELLS,), 0, R), jax.random.fold_in(keys[1], 1), 0, R - 1).astype(jnp.int32),
        "batch_ids": with_ends(jax.random.randint(keys[2], (CELLS,), 0, BATCHES), jax.random.fold_in(keys[2], 1), 0, BATCHES - 1).astype(jnp.int32),
        "noise_draw": noise(keys[3], (CELLS, L), 1.0, 4.0, ((0, 2),), jnp.float32),
        "cell_factor": jnp.clip(0.3 + 0.65 * jax.random.uniform(keys[4], (CELLS,), jnp.float32) ** steps_of(keys[4], (CELLS,), ((0, 2),), -0.2, 0.2), 0.3, 0.95),
        "enc_weight": noise(keys[5], (R, H), R ** -0.5, 0.0546875, ((0, 16), (1, 2)), jnp.float32),
        "enc_first": noise(keys[6], (R, H), (0.3 * (CELLS * R * H) ** -0.5), 1.1444091796875e-05, ((0, 16), (1, 2)), jnp.float32),
        "enc_second": jnp.clip(jnp.exp(math.log(1.3969838306981952e-11) - 1.3862944 * jax.random.uniform(keys[7], (R, H), jnp.float32) ** steps_of(keys[7], (R, H), ((0, 16), (1, 2)), -0.2, 0.2)), 3.492459576745488e-12, 1.3969838306981952e-11),
        "dec_weight": noise(keys[8], (H, R), H ** -0.5, 0.5, ((0, 2), (1, 16)), jnp.float32),
        "dec_first": noise(keys[9], (H, R), (0.2 / (CELLS ** 0.5 * R)), 7.152557373046875e-07, ((0, 2), (1, 16)), jnp.float32),
        "dec_second": jnp.clip(jnp.exp(math.log(6.467518035881137e-14) - 1.3862944 * jax.random.uniform(keys[10], (H, R), jnp.float32) ** steps_of(keys[10], (H, R), ((0, 2), (1, 16)), -0.2, 0.2)), 1.6168795089702842e-14, 6.467518035881137e-14),
        "region_vecs": draw_region_vecs(jax.random.fold_in(keys[20], 71), 0),
        "vec_first": noise(keys[12], (2, R), (0.3 / (CELLS ** 0.25 * R)), 1.33514404296875e-05, ((0, 2), (1, 16)), jnp.float32),
        "vec_second": jnp.clip(jnp.exp(math.log(1.8626451075975936e-11) - 1.3862944 * jax.random.uniform(keys[13], (2, R), jnp.float32) ** steps_of(keys[13], (2, R), ((0, 2), (1, 16)), -0.2, 0.2)), 4.656612768993984e-12, 1.8626451075975936e-11),
        "trunk_rows": draw_trunk_rows(jax.random.fold_in(keys[20], 71), 0),
        "trunk_first": noise(keys[15], (TR, H), (0.4 * (CELLS * R * H) ** -0.5), 1.52587890625e-05, (), jnp.float32),
        "trunk_second": jnp.clip(jnp.exp(jax.random.uniform(keys[16], (TR, H), jnp.float32, math.log(6.208817314445891e-12), math.log(2.4835269257783565e-11))), 6.208817314445891e-12, 2.4835269257783565e-11),
        "head_rows": draw_head_rows(jax.random.fold_in(keys[20], 71), 0),
        "head_first": noise(keys[18], (H + 1, 2 * L), (0.4 * (CELLS * R * H) ** -0.5), 1.52587890625e-05, (), jnp.float32),
        "head_second": jnp.clip(jnp.exp(jax.random.uniform(keys[19], (H + 1, 2 * L), jnp.float32, math.log(6.208817314445891e-12), math.log(2.4835269257783565e-11))), 6.208817314445891e-12, 2.4835269257783565e-11),
    }


highest = lax.Precision.HIGHEST
norm_eps = 1e-05
leak_slope = 0.01
decay_rate = 0.5
weight_decay = 0.01
learn_rate = 0.5
lamb_eps = 1e-12

@jax.custom_vjp
def low(v):
    return lax.optimization_barrier(v.astype(jnp.bfloat16)).astype(jnp.float32)

@jax.custom_vjp
def low_back(v):
    return v

def low_keep(v):
    return (low(v), None)

def low_pass(kept, grad):
    return (grad,)

def back_keep(v):
    return (v, None)

def back_low(kept, grad):
    return (low(grad),)
low.defvjp(low_keep, low_pass)
low_back.defvjp(back_keep, back_low)

def matmul(left, right):
    return jnp.dot(left, right, precision=highest, preferred_element_type=jnp.float32)

def layer_norm(values, gain_row, shift_row):
    centre = values - lax.optimization_barrier(jnp.mean(values, axis=-1, keepdims=True))
    spread = lax.optimization_barrier(jnp.mean(centre * centre, axis=-1, keepdims=True))
    return centre * lax.rsqrt(spread + norm_eps) * gain_row + shift_row

def leaky_relu(values):
    return jnp.where(values >= 0, values, leak_slope * values)

def region_masks(counts, seed_rows, first_region, width, total):
    regions = first_region + jnp.arange(width, dtype=jnp.int32)
    stride = 6 * (seed_rows % (total // 6)) + 1
    upper = stride[:, None] * (regions[None, :] // 256) % total
    hashed = (upper * 256 + stride[:, None] * (regions[None, :] % 256) + seed_rows[:, None]) % total
    return hashed < counts[:, None]

def trunk_forward(pre_in, trunk_part, head_part, noise_rows, onehot):
    hidden = trunk_part.shape[1]
    latent = head_part.shape[1] // 2
    batches = onehot.shape[1]
    enc_two = trunk_part[batches:batches + hidden]
    dec_one = trunk_part[batches + hidden:2 * batches + hidden + latent]
    dec_two = trunk_part[2 * batches + hidden + latent:2 * batches + 2 * hidden + latent]
    base_row = 2 * batches + 2 * hidden + latent
    gain_rows = trunk_part[base_row:base_row + 4]
    shift_rows = trunk_part[base_row + 4:base_row + 8]
    first = leaky_relu(layer_norm(pre_in, gain_rows[0], shift_rows[0]))
    second = leaky_relu(layer_norm(matmul(first, enc_two), gain_rows[1], shift_rows[1]))
    moments = matmul(second, head_part[:hidden]) + head_part[hidden]
    centre_lat = moments[:, :latent]
    log_var = moments[:, latent:]
    sample = centre_lat + jnp.exp(0.5 * log_var) * noise_rows
    third_in = matmul(sample, dec_one[:latent]) + matmul(onehot, dec_one[latent:])
    third = leaky_relu(layer_norm(third_in, gain_rows[2], shift_rows[2]))
    fourth = leaky_relu(layer_norm(matmul(third, dec_two), gain_rows[3], shift_rows[3]))
    diverge = 0.5 * jnp.sum(jnp.exp(log_var) + centre_lat * centre_lat - 1.0 - log_var)
    return (fourth, diverge)

def lamb_moments(weight, grad, first, second):
    first_new = decay_rate * first + (1.0 - decay_rate) * grad
    second_new = decay_rate * second + (1.0 - decay_rate) * grad * grad
    update = first_new / (jnp.sqrt(second_new) + lamb_eps) + weight_decay * weight
    return (first_new, second_new, update)

def square_norm(values):
    return jnp.sqrt(jnp.sum(values * values))

def lamb_groups(weight, update, row_edges):
    pieces = []
    weight_list = []
    update_list = []
    for group_index in range(len(row_edges) - 1):
        start_row = row_edges[group_index]
        end_row = row_edges[group_index + 1]
        weight_part = weight[start_row:end_row]
        update_part = update[start_row:end_row]
        weight_norm = square_norm(weight_part)
        update_norm = square_norm(update_part)
        weight_list.append(weight_norm)
        update_list.append(update_norm)
        pieces.append(weight_part - learn_rate * (weight_norm / update_norm) * update_part)
    return (jnp.concatenate(pieces, axis=0), jnp.stack(weight_list), jnp.stack(update_list))

def trunk_edges(hidden, latent, batches):
    return [0, batches, batches + hidden, 2 * batches + hidden + latent, 2 * batches + 2 * hidden + latent, 2 * batches + 2 * hidden + latent + 8]

def reference(cell_counts, cell_seeds, batch_ids, noise_draw, cell_factor, enc_weight, enc_first, enc_second, dec_weight, dec_first, dec_second, region_vecs, vec_first, vec_second, trunk_rows, trunk_first, trunk_second, head_rows, head_first, head_second):
    block_rows = min(512, CELLS)
    blocks = CELLS // block_rows
    loss_scale = 1.0 / (CELLS * R)
    onehot = (batch_ids[:, None] == jnp.arange(BATCHES, dtype=jnp.int32)[None, :]).astype(jnp.float32)
    block_inputs = (cell_counts.reshape(blocks, block_rows), cell_seeds.reshape(blocks, block_rows), onehot.reshape(blocks, block_rows, BATCHES), noise_draw.reshape(blocks, block_rows, L), cell_factor.reshape(blocks, block_rows))

    def block_loss(enc_low, dec_low, vec_low, trunk_part, head_part, counts, seed_rows, hot_rows, noise_rows, factors):
        mask_rows = region_masks(counts, seed_rows, 0, R, R).astype(jnp.float32)
        pre_in = low_back(matmul(mask_rows, enc_low) + matmul(hot_rows, trunk_part[:BATCHES]))
        decoded, diverge = trunk_forward(pre_in, trunk_part, head_part, noise_rows, hot_rows)
        logits = low_back(matmul(low(decoded), dec_low) + vec_low[0])
        log_prob = jax.nn.log_sigmoid(logits) + jnp.log(factors)[:, None] + jax.nn.log_sigmoid(vec_low[1])[None, :]
        probability = jnp.exp(log_prob)
        recon_sum = -jnp.sum(mask_rows * log_prob + (1.0 - mask_rows) * jnp.log1p(-probability))
        return jnp.stack([recon_sum, diverge])
    checked = jax.checkpoint(block_loss)

    def total_loss(enc_part, dec_part, vec_part, trunk_part, head_part):
        enc_low = low(enc_part)
        dec_low = low(dec_part)
        vec_low = low(vec_part)

        def scan_step(carried, inputs):
            return (carried + checked(enc_low, dec_low, vec_low, trunk_part, head_part, *inputs), None)
        total, _ = lax.scan(scan_step, jnp.zeros((2,), jnp.float32), block_inputs)
        return ((total[0] + total[1]) * loss_scale, total)
    objective, pull_back, totals = jax.vjp(total_loss, enc_weight, dec_weight, region_vecs, trunk_rows, head_rows, has_aux=True)
    grads = pull_back(jnp.ones_like(objective))
    loss = jnp.stack([totals[0] * loss_scale, totals[1] / CELLS])
    enc_first_new, enc_second_new, enc_update = lamb_moments(enc_weight, grads[0], enc_first, enc_second)
    dec_first_new, dec_second_new, dec_update = lamb_moments(dec_weight, grads[1], dec_first, dec_second)
    vec_first_new, vec_second_new, vec_update = lamb_moments(region_vecs, grads[2], vec_first, vec_second)
    trunk_first_new, trunk_second_new, trunk_update = lamb_moments(trunk_rows, grads[3], trunk_first, trunk_second)
    head_first_new, head_second_new, head_update = lamb_moments(head_rows, grads[4], head_first, head_second)
    enc_new, enc_wn, enc_un = lamb_groups(enc_weight, enc_update, [0, R])
    dec_new, dec_wn, dec_un = lamb_groups(dec_weight, dec_update, [0, H])
    vecs_new, vec_wn, vec_un = lamb_groups(region_vecs, vec_update, [0, 1, 2])
    trunk_new, trunk_wn, trunk_un = lamb_groups(trunk_rows, trunk_update, trunk_edges(H, L, BATCHES))
    head_new, head_wn, head_un = lamb_groups(head_rows, head_update, [0, H + 1])
    norms = jnp.stack([jnp.concatenate([enc_wn, dec_wn, vec_wn, trunk_wn, head_wn]), jnp.concatenate([enc_un, dec_un, vec_un, trunk_un, head_un])])
    return (loss, enc_new, enc_first_new, enc_second_new, enc_new.astype(jnp.bfloat16), dec_new, dec_first_new, dec_second_new, dec_new.astype(jnp.bfloat16), vecs_new, vec_first_new, vec_second_new, trunk_new, trunk_first_new, trunk_second_new, head_new, head_first_new, head_second_new, norms)
```

```python
import functools

import jax
import jax.numpy as jnp
from jax import lax
from jax.experimental import pallas as pl
from jax.experimental.pallas import tpu as pltpu
from jax.sharding import Mesh
from jax.sharding import PartitionSpec as P

BATCHES = 8
COLUMNS = 4

norm_eps = 1e-05
leak_slope = 0.01
decay_rate = 0.5
weight_decay = 0.01
learn_rate = 0.5
lamb_eps = 1e-12

f32 = jnp.float32
bf16 = jnp.bfloat16
VMEM = pl.BlockSpec(memory_space=pltpu.VMEM)
SMEM = pl.BlockSpec(memory_space=pltpu.SMEM)
MEGA = 1024 * 1024


def params(mib=48):
    return pltpu.CompilerParams(vmem_limit_bytes=mib * MEGA)


def cost(flops, moved, transcendentals=0):
    return pl.CostEstimate(flops=flops, bytes_accessed=moved, transcendentals=transcendentals)


def exact(left, right, contract=((1,), (0,))):
    return lax.dot_general(
        left, right, (contract, ((), ())), precision=lax.Precision.HIGHEST, preferred_element_type=f32
    )


def wide(left, right, contract=((1,), (0,))):
    return lax.dot_general(left, right, (contract, ((), ())), preferred_element_type=f32)


def remainder(values, divisor):
    guess = jnp.floor(values.astype(f32) * (1.0 / divisor)).astype(jnp.int32)
    rest = values - guess * divisor
    rest = jnp.where(rest < 0, rest + divisor, rest)
    return jnp.where(rest >= divisor, rest - divisor, rest)


def turns(values, total):
    whole = 2**32 // total
    part = (2**32 % total) / total
    return values * whole + (values.astype(f32) * part + 0.5).astype(jnp.int32)


def mask_kernel(total, width, base_ref, cells_ref, mask_ref, factor_ref):
    step = pl.program_id(0)
    counts = cells_ref[0, pl.ds(step, 1), :].astype(jnp.int32)
    seeds = cells_ref[1, pl.ds(step, 1), :].astype(jnp.int32)
    factors = cells_ref[2, pl.ds(step, 1), :]
    stride = 6 * remainder(seeds, total // 6) + 1
    rows = []
    for column in range(COLUMNS):
        base = base_ref[column]
        upper = remainder(stride * (base // 256), total)
        rows.append(remainder(upper * 256 + stride * (base % 256) + seeds, total))
    low_end = jnp.int32(-(2**31))
    rows.append(stride)
    rows.append(turns(remainder(stride * 128, total), total))
    rows.append(turns(counts, total) + low_end)
    rows.append(counts)
    table = jnp.concatenate(rows, axis=0).T
    factor_ref[...] = jnp.broadcast_to(
        jnp.broadcast_to(factors, (8, 128)).T[:, 0:1], (128, 128)
    )
    half = 2**31 // total
    for part in range(2):
        lines = slice(part * 64, part * 64 + 64)
        shape = (64, 128)
        lane = lax.broadcasted_iota(jnp.int32, shape, 1)
        span = jnp.broadcast_to(table[lines, 4:5], shape) * lane
        advance = jnp.broadcast_to(table[lines, 5:6], shape)
        limit = jnp.broadcast_to(table[lines, 6:7], shape)
        for column in range(COLUMNS):
            start = remainder(jnp.broadcast_to(table[lines, column : column + 1], shape) + span, total)
            place = turns(start, total) + (low_end + jnp.int32(half))
            for group in range(width // 128):
                at = column * width + group * 128
                mask_ref[lines, at : at + 128] = jnp.where(place < limit, 1.0, 0.0).astype(bf16)
                place = place + advance


def encode_kernel(width, mask_ref, *refs):
    out_ref = refs[-1]
    total = None
    for column in range(COLUMNS):
        block = jnp.concatenate([refs[2 * column][...], refs[2 * column + 1][...]], axis=0)
        term = wide(mask_ref[:, column * width : (column + 1) * width], block, ((1,), (1,)))
        total = term if total is None else total + term
    out_ref[...] = total


def pack_kernel(info_ref, *refs):
    weight_ref, line_ref = refs[-2:]
    is_first = info_ref[0] == 0
    for column in range(COLUMNS):
        mine = refs[2 * column][...]
        other = refs[2 * column + 1][...]
        mine_line = mine[64:80].astype(f32)[0:1]
        other_line = other[64:80].astype(f32)[0:1]
        bias = jnp.where(is_first, mine_line, other_line)
        logit = jnp.where(is_first, other_line, mine_line)
        width = mine.shape[1]
        row = lax.broadcasted_iota(jnp.int32, (16, width), 0)
        weight_ref[column, 0:64] = mine[0:64]
        weight_ref[column, 64:128] = other[0:64]
        weight_ref[column, 128:144] = jnp.where(row == 0, bias, 0.0).astype(bf16)
        weight_ref[column, 144:256] = jnp.zeros((112, width), bf16)
        spread = jnp.exp(-jnp.abs(logit))
        chance = jnp.where(logit >= 0, 1.0, spread) / (1.0 + spread)
        logs = jnp.minimum(logit, 0.0) - jnp.log(1.0 + spread)
        line_ref[column, 0:16] = jnp.broadcast_to(chance, (16, width))
        line_ref[column, 16:32] = jnp.broadcast_to(logs, (16, width))


def normalize(values):
    centre = values - jnp.mean(values, axis=-1, keepdims=True)
    spread = jnp.mean(centre * centre, axis=-1, keepdims=True)
    scale = lax.rsqrt(spread + norm_eps)
    return centre * scale, scale


def leaky(values):
    return jnp.where(values >= 0, values, leak_slope * values)


def swap_halves(values, is_first):
    return jnp.where(is_first, values, pltpu.roll(values, 64, 1))


class Rows:
    def __init__(self, hidden, latent):
        self.enc_two = BATCHES
        self.dec_one = BATCHES + hidden
        self.dec_two = 2 * BATCHES + hidden + latent
        self.gain = 2 * BATCHES + 2 * hidden + latent
        self.shift = self.gain + 4
        self.end = self.gain + 8


def forward_kernel(parts, latent, own, *refs):
    info_ref, ids_ref, noise_ref, trunk_ref, head_ref, cells_ref = refs[:6]
    part_refs = refs[6 : 6 + parts]
    low_ref, norm_ref, scale_ref, left_ref, moment_ref, stat_ref = refs[6 + parts :]
    is_first = info_ref[0] == 0
    rows = Rows(128, latent)
    total = part_refs[0][...]
    for ref in part_refs[1:]:
        total = total + ref[...]
    total = swap_halves(total, is_first)
    lane = lax.broadcasted_iota(jnp.int32, total.shape, 1)
    ids = ids_ref[...]
    hot = jnp.where(lane == ids, 1.0, 0.0)
    gains = trunk_ref[rows.gain : rows.gain + 4, :]
    shifts = trunk_ref[rows.shift : rows.shift + 4, :]

    def act(index, values):
        normal, scale = normalize(values)
        norm_ref[index] = normal
        return leaky(normal * gains[index : index + 1] + shifts[index : index + 1]), scale

    first, scale0 = act(0, total + exact(hot, trunk_ref[0:128, :]))
    second, scale1 = act(1, exact(first, trunk_ref[rows.enc_two : rows.enc_two + 128, :]))
    moments = exact(second, head_ref[0:128, :]) + head_ref[128:129, :]
    inside = lane < latent
    centre = jnp.where(inside, moments, 0.0)
    log_var = jnp.where(inside, pltpu.roll(moments, 128 - latent, 1), 0.0)
    sample = centre + jnp.exp(0.5 * log_var) * noise_ref[...]
    left = sample + jnp.where(lane == ids + latent, 1.0, 0.0)
    third, scale2 = act(2, exact(left, trunk_ref[rows.dec_one : rows.dec_one + 128, :]))
    fourth, scale3 = act(3, exact(third, trunk_ref[rows.dec_two : rows.dec_two + 128, :]))
    low_ref[...] = swap_halves(fourth, is_first).astype(bf16)
    left_ref[...] = left
    moment_ref[0] = centre
    moment_ref[1] = log_var
    scale_ref[...] = jnp.where(
        lane == 0, scale0, jnp.where(lane == 1, scale1, jnp.where(lane == 2, scale2, scale3))
    )
    diverge = 0.5 * jnp.sum(jnp.exp(log_var) + centre * centre - 1.0 - log_var)
    lines = cells_ref.shape[1]
    place = lax.broadcasted_iota(jnp.int32, (lines, 128), 0) * 128 + lax.broadcasted_iota(
        jnp.int32, (lines, 128), 1
    )
    known = jnp.sum(jnp.where(place < own, cells_ref[0] * jnp.log(cells_ref[2]), 0.0))
    stat_lane = lax.broadcasted_iota(jnp.int32, (8, 128), 1)
    stat_row = lax.broadcasted_iota(jnp.int32, (8, 128), 0)
    stats = jnp.where(stat_lane == 8, known, jnp.where(stat_lane == 9, diverge, 0.0))
    stat_ref[...] = jnp.where(stat_row == 0, stats, 0.0)


def decode_kernel(loss_scale, has_sum, *refs):
    info_ref, low_ref, mask_ref, factor_ref, weight_ref, line_ref = refs[:6]
    refs = refs[6:]
    if has_sum:
        mine_in, other_in = refs[:2]
        refs = refs[2:]
    mine_ref, other_ref, back_ref, loss_ref, logit_ref, grad_ref, left_ref, turned_ref = refs
    column = pl.program_id(0)
    cells, width = grad_ref.shape
    is_first = info_ref[0] == 0

    @pl.when(column == 0)
    def _():
        low = low_ref[...]
        left_ref[:, 0:128] = low
        lane = lax.broadcasted_iota(jnp.int32, (cells, 128), 1)
        left_ref[:, 128:256] = jnp.where(lane == 0, 1.0, 0.0).astype(bf16)
        turned_ref[0:128, :] = low.astype(f32).T.astype(bf16)
        row = lax.broadcasted_iota(jnp.int32, (16, cells), 0)
        turned_ref[128:144, :] = jnp.where(row == 0, 1.0, 0.0).astype(bf16)

    logit_ref[...] = wide(left_ref[...], weight_ref[0])

    def step(index, carried):
        loss_sum, *signals = carried
        at = pl.ds(pl.multiple_of(index * 16, 16), 16)
        factor = factor_ref[at, :]
        top = bottom = held = None
        result = []
        for group in range(width // 128):
            lanes = slice(group * 128, group * 128 + 128)
            logits = logit_ref[at, lanes]
            spread = jnp.exp(-jnp.abs(logits))
            whole = 1.0 + spread
            positive = logits >= 0
            chance = factor * line_ref[0, 0:16, lanes]
            taken = chance * jnp.where(positive, 1.0, spread)
            opened = mask_ref[at, lanes].astype(f32) > 0.5
            rest = jnp.where(opened, 1.0, whole - taken)
            inverse = pl.reciprocal(whole * rest, approx=False)
            small = spread * loss_scale
            numerator = jnp.where(opened, jnp.where(positive, -small, -loss_scale), small * chance)
            grad_ref[at, lanes] = (numerator * inverse).astype(bf16)
            signal = jnp.where(opened, -1.0, taken * whole * inverse)
            result.append(signals[group] - (signal[0:8] + signal[8:16]))
            likely = jnp.where(opened, jnp.minimum(logits, 0.0) + line_ref[0, 16:32, lanes], 0.0)
            held = likely if held is None else held + likely
            top = rest if top is None else top * rest
            bottom = whole if bottom is None else bottom * whole
        held = held + (jnp.log(top) - jnp.log(bottom))
        return (loss_sum + (held[0:8] + held[8:16]), *result)

    zero = jnp.zeros((8, 128), f32)
    loss_sum, *signals = lax.fori_loop(0, cells // 16, step, (zero,) * (1 + width // 128))
    signal_line = jnp.sum(jnp.concatenate(signals, axis=1), axis=0, keepdims=True)
    product = wide(turned_ref[...], grad_ref[...])
    bias_line = product[128:129]
    mine_line = jnp.where(is_first, bias_line, signal_line)
    other_line = jnp.where(is_first, signal_line, bias_line)
    row = lax.broadcasted_iota(jnp.int32, (8, width), 0)
    mine_tail = jnp.where(row == 0, mine_line, 0.0)
    other_tail = jnp.where(row == 0, other_line, 0.0)
    if has_sum:
        mine_ref[0, 0:64] = mine_in[0, 0:64] + product[0:64]
        other_ref[0, 0:64] = other_in[0, 0:64] + product[64:128]
        mine_ref[0, 64:72] = mine_in[0, 64:72] + mine_tail
        other_ref[0, 64:72] = other_in[0, 64:72] + other_tail
    else:
        mine_ref[0, 0:64] = product[0:64]
        other_ref[0, 0:64] = product[64:128]
        mine_ref[0, 64:72] = mine_tail
        other_ref[0, 64:72] = other_tail
    back = wide(grad_ref[...], weight_ref[0, 0:128], ((1,), (1,)))

    @pl.when(column == 0)
    def _():
        back_ref[...] = back
        loss_ref[...] = loss_sum

    @pl.when(column > 0)
    def _():
        back_ref[...] += back
        loss_ref[...] += loss_sum


def backward_kernel(parts, latent, loss_scale, *refs):
    info_ref, ids_ref, noise_ref, trunk_ref, head_ref = refs[:5]
    norm_ref, scale_ref, left_ref, moment_ref = refs[5:9]
    part_refs = refs[9 : 9 + parts]
    low_ref, mine_ref, other_ref, sum_ref = refs[9 + parts :]
    is_first = info_ref[0] == 0
    rows = Rows(128, latent)
    total = part_refs[0][...]
    for ref in part_refs[1:]:
        total = total + ref[...]
    total = swap_halves(total, is_first)
    lane = lax.broadcasted_iota(jnp.int32, total.shape, 1)
    ids = ids_ref[...]
    gains = trunk_ref[rows.gain : rows.gain + 4, :]
    shifts = trunk_ref[rows.shift : rows.shift + 4, :]
    sum_ref[...] = jnp.zeros_like(sum_ref)
    rows_in, rows_out = ((0,), (0,)), ((1,), (1,))

    def output(index):
        return leaky(norm_ref[index] * gains[index : index + 1] + shifts[index : index + 1])

    def pull(index, grad):
        normal = norm_ref[index]
        gain = gains[index : index + 1]
        before = normal * gain + shifts[index : index + 1]
        grad = jnp.where(before >= 0, grad, leak_slope * grad)
        at = rows.gain + index
        sum_ref[at : at + 1, :] = jnp.sum(grad * normal, axis=0, keepdims=True)
        at = rows.shift + index
        sum_ref[at : at + 1, :] = jnp.sum(grad, axis=0, keepdims=True)
        grad = grad * gain
        plain = jnp.mean(grad, axis=-1, keepdims=True)
        along = jnp.mean(grad * normal, axis=-1, keepdims=True)
        return (grad - plain - normal * along) * scale_ref[:, index : index + 1]

    grad = pull(3, total)
    sum_ref[rows.dec_two : rows.dec_two + 128, :] = exact(output(2), grad, rows_in)
    grad = pull(2, exact(grad, trunk_ref[rows.dec_two : rows.dec_two + 128, :], rows_out))
    one = exact(left_ref[...], grad, rows_in)
    sum_ref[rows.dec_one : rows.dec_two, :] = one[0 : rows.dec_two - rows.dec_one]
    grad = exact(grad, trunk_ref[rows.dec_one : rows.dec_one + 128, :], rows_out)
    inside = lane < latent
    grad = jnp.where(inside, grad, 0.0)
    centre, log_var = moment_ref[0], moment_ref[1]
    grad_centre = grad + loss_scale * centre
    grad_log = grad * 0.5 * jnp.exp(0.5 * log_var) * noise_ref[...] + (0.5 * loss_scale) * (
        jnp.exp(log_var) - 1.0
    )
    both = jnp.where(inside, grad_centre, pltpu.roll(jnp.where(inside, grad_log, 0.0), latent, 1))
    head = exact(both, output(1), rows_in)
    sum_ref[296 : 296 + 24, :] = head[0:24]
    sum_ref[296 + 2 * latent : 297 + 2 * latent, :] = jnp.sum(both, axis=0, keepdims=True)
    grad = pull(1, exact(both, head_ref[0:128, :], rows_out))
    sum_ref[rows.enc_two : rows.enc_two + 128, :] = exact(output(0), grad, rows_in)
    grad = pull(0, exact(grad, trunk_ref[rows.enc_two : rows.enc_two + 128, :], rows_out))
    low = grad.astype(bf16)
    hot = jnp.where(lane == ids, 1.0, 0.0).astype(bf16)
    sum_ref[0:BATCHES, :] = wide(hot, low, rows_in)[0:BATCHES]
    low_ref[...] = swap_halves(low.astype(f32), is_first).astype(bf16)
    middle = sum_ref.shape[0] // 2
    upper, lower = sum_ref[0:middle, :], sum_ref[middle:, :]
    mine_ref[...] = jnp.where(is_first, upper, lower)
    other_ref[...] = jnp.where(is_first, lower, upper)


def encode_back_kernel(groups, mask_ref, *refs):
    low_refs = refs[:groups]
    mine_ref, other_ref, turned_ref = refs[groups:]
    cells = low_refs[0].shape[0]

    @pl.when(pl.program_id(0) == 0)
    def _():
        for group in range(groups):
            turned_ref[:, group * cells : (group + 1) * cells] = (
                low_refs[group][...].astype(f32).T.astype(bf16)
            )

    product = wide(turned_ref[...], mask_ref[...])
    mine_ref[0] = product[0:64]
    other_ref[0] = product[64:128]


def stat_tile(pairs):
    lane = lax.broadcasted_iota(jnp.int32, (8, 128), 1)
    row = lax.broadcasted_iota(jnp.int32, (8, 128), 0)
    tile = jnp.zeros((8, 128), f32)
    for index, value in pairs:
        tile = jnp.where(lane == index, value, tile)
    return jnp.where(row == 0, tile, 0.0)


def moments_of(weight, grad, first, second):
    first_new = decay_rate * first + (1.0 - decay_rate) * grad
    second_new = decay_rate * second + (1.0 - decay_rate) * grad * grad
    update = first_new / (jnp.sqrt(second_new) + lamb_eps) + weight_decay * weight
    return first_new, second_new, update


def enc_lamb_kernel(parts, *refs):
    weight_ref, first_ref, second_ref = refs[:3]
    part_refs = refs[3 : 3 + parts]
    first_out, second_out, update_out, stat_out = refs[3 + parts :]
    grad = part_refs[0][...]
    for ref in part_refs[1:]:
        grad = grad + ref[...]
    weight = weight_ref[...]
    first, second, update = moments_of(weight, grad.T, first_ref[...], second_ref[...])
    first_out[...] = first
    second_out[...] = second
    update_out[...] = update
    stat_out[...] = stat_tile([(0, jnp.sum(weight * weight)), (4, jnp.sum(update * update))])


def dec_lamb_kernel(parts, loss_scale, *refs):
    info_ref, weight_ref, first_ref, second_ref, vec_ref, vec_first_ref, vec_second_ref = refs[:7]
    part_refs = refs[7 : 7 + parts]
    first_out, second_out, update_out, vec_first_out, vec_second_out, vec_update_out, stat_out = refs[
        7 + parts :
    ]
    grad = part_refs[0][...]
    for ref in part_refs[1:]:
        grad = grad + ref[...]
    weight = weight_ref[...]
    first, second, update = moments_of(weight, grad[0:64], first_ref[...], second_ref[...])
    first_out[...] = first
    second_out[...] = second
    update_out[...] = update
    is_first = info_ref[0] == 0
    vec = vec_ref[...]
    low = vec.astype(bf16).astype(f32)
    line = grad[64:65]
    keep = 1.0 / (1.0 + jnp.exp(low))
    line = jnp.where(is_first, line, -keep * (line * loss_scale))
    vec_one, vec_two, vec_update = moments_of(vec, line, vec_first_ref[...], vec_second_ref[...])
    vec_first_out[...] = vec_one
    vec_second_out[...] = vec_two
    vec_update_out[...] = vec_update
    vec_square = jnp.sum(vec * vec)
    update_square = jnp.sum(vec_update * vec_update)
    stat_out[...] = stat_tile(
        [
            (1, jnp.sum(weight * weight)),
            (2, jnp.where(is_first, vec_square, 0.0)),
            (3, jnp.where(is_first, 0.0, vec_square)),
            (5, jnp.sum(update * update)),
            (6, jnp.where(is_first, update_square, 0.0)),
            (7, jnp.where(is_first, 0.0, update_square)),
        ]
    )


def trunk_lamb_kernel(latent, *refs):
    info_ref, mine_ref, other_ref = refs[:3]
    weight_ref, first_ref, second_ref, head_ref, head_first_ref, head_second_ref = refs[3:9]
    new_out, first_out, second_out, head_out, head_first_out, head_second_out, stat_out = refs[9:16]
    sum_ref = refs[16]
    is_first = info_ref[0] == 0
    rows = Rows(128, latent)
    mine, other = mine_ref[...], other_ref[...]
    middle = mine.shape[0]
    sum_ref[0:middle] = jnp.where(is_first, mine, other)
    sum_ref[middle : 2 * middle] = jnp.where(is_first, other, mine)
    weight = weight_ref[...]
    count = weight.shape[0]
    first, second, update = moments_of(weight, sum_ref[0:count], first_ref[...], second_ref[...])
    first_out[...] = first
    second_out[...] = second
    edges = [0, rows.enc_two, rows.dec_one, rows.dec_two, rows.gain, rows.end]
    row = lax.broadcasted_iota(jnp.int32, (count, 1), 0)
    weight_lines = jnp.sum(weight * weight, axis=1, keepdims=True)
    update_lines = jnp.sum(update * update, axis=1, keepdims=True)
    ratio = jnp.zeros((count, 1), f32)
    pairs = []
    for index in range(5):
        chosen = (row >= edges[index]) & (row < edges[index + 1])
        weight_norm = jnp.sqrt(jnp.sum(jnp.where(chosen, weight_lines, 0.0), keepdims=True))
        update_norm = jnp.sqrt(jnp.sum(jnp.where(chosen, update_lines, 0.0), keepdims=True))
        ratio = jnp.where(chosen, learn_rate * (weight_norm / update_norm), ratio)
        pairs += [(index, weight_norm), (8 + index, update_norm)]
    new_out[...] = weight - ratio * update
    size = 2 * latent
    head = head_ref[...]
    block = sum_ref[296:320]
    turned = jnp.concatenate([block, jnp.zeros((104, 128), f32)], axis=0).T[:, 0:size]
    grad_head = jnp.concatenate([turned, block[size : size + 1, 0:size]], axis=0)
    first, second, update = moments_of(head, grad_head, head_first_ref[...], head_second_ref[...])
    head_first_out[...] = first
    head_second_out[...] = second
    weight_norm = jnp.sqrt(jnp.sum(head * head, keepdims=True))
    update_norm = jnp.sqrt(jnp.sum(update * update, keepdims=True))
    head_out[...] = head - learn_rate * (weight_norm / update_norm) * update
    pairs += [(5, weight_norm), (13, update_norm)]
    stat_out[...] = stat_tile(pairs)


def final_kernel(parts, loss_scale, all_cells, *refs):
    info_ref, trunk_stat_ref = refs[:2]
    part_refs = refs[2 : 2 + parts]
    enc_ref, enc_update_ref, dec_ref, dec_update_ref, vec_ref, vec_update_ref = refs[2 + parts : 8 + parts]
    loss_out, enc_out, enc_copy, dec_out, dec_copy, vec_out, norm_out = refs[8 + parts :]
    stats = part_refs[0][...]
    for ref in part_refs[1:]:
        stats = stats + ref[...]
    trunk_stats = trunk_stat_ref[...]
    roots = jnp.sqrt(stats[0:1])

    def ratio(index):
        return learn_rate * (roots[:, index : index + 1] / roots[:, index + 4 : index + 5])

    enc_new = enc_ref[...] - ratio(0) * enc_update_ref[...]
    enc_out[...] = enc_new
    enc_copy[...] = enc_new.astype(bf16)
    dec_new = dec_ref[...] - ratio(1) * dec_update_ref[...]
    dec_out[...] = dec_new
    dec_copy[...] = dec_new.astype(bf16)
    vec_ratio = jnp.where(info_ref[0] == 0, ratio(2), ratio(3))
    vec_out[...] = vec_ref[...] - vec_ratio * vec_update_ref[...]
    norm_out[0:1, 0:4] = roots[:, 0:4]
    norm_out[1:2, 0:4] = roots[:, 4:8]
    norm_out[0:1, 4:10] = trunk_stats[0:1, 0:6]
    norm_out[1:2, 4:10] = trunk_stats[0:1, 8:14]
    lane = lax.broadcasted_iota(jnp.int32, (1, 128), 1)
    loss_out[0] = jnp.sum(jnp.where(lane == 8, -stats[0:1], 0.0)) * loss_scale
    loss_out[1] = jnp.sum(jnp.where(lane == 9, stats[0:1], 0.0)) / all_cells


def shaped(*shapes):
    return tuple(jax.ShapeDtypeStruct(shape, kind) for shape, kind in shapes)


def on_device(
    cell_counts,
    cell_seeds,
    batch_ids,
    noise_draw,
    cell_factor,
    enc_weight,
    enc_first,
    enc_second,
    dec_weight,
    dec_first,
    dec_second,
    region_vecs,
    vec_first,
    vec_second,
    trunk_rows,
    trunk_first,
    trunk_second,
    head_rows,
    head_first,
    head_second,
):
    cells_here = cell_counts.shape[0]
    width = enc_weight.shape[0]
    latent = head_rows.shape[1] // 2
    plane = lax.axis_size("plane")
    total = width * COLUMNS * plane
    all_cells = cells_here * lax.axis_size("dp")
    loss_scale = 1.0 / (all_cells * total)
    share = cells_here // COLUMNS
    own = share // plane
    groups = min(4, plane)
    each = plane // groups
    block = own * each
    dp = lax.axis_index("dp")
    column = lax.axis_index("column")
    spot = lax.axis_index("plane")
    info = jnp.stack([dp]).astype(jnp.int32)
    bases = jnp.stack(
        [((column + j) % COLUMNS * plane + spot) * width for j in range(COLUMNS)]
    ).astype(jnp.int32)

    def over_dp(value):
        return lax.ppermute(value, "dp", [(0, 1), (1, 0)])

    def from_column(value, j):
        return lax.ppermute(value, "column", [(i, (i - j) % COLUMNS) for i in range(COLUMNS)])

    def to_column(value, j):
        return lax.ppermute(value, "column", [(i, (i + j) % COLUMNS) for i in range(COLUMNS)])

    def over_plane(value, k):
        return lax.ppermute(value, "plane", [(i, i ^ k) for i in range(plane)])

    def gather_column(value):
        blocks = []
        for j in range(COLUMNS):
            mine = value if j == 0 else from_column(value, j)
            blocks += [mine, over_dp(mine)]
        return blocks

    def gather_plane(value):
        blocks = [value] + [over_plane(value, k) for k in range(1, plane)]
        if each == 1:
            return blocks
        return [jnp.concatenate(blocks[g * each : (g + 1) * each], axis=0) for g in range(groups)]

    def scatter_plane(values):
        received = []
        for g in range(groups):
            for e in range(each):
                k = g * each + e
                piece = values[g] if each == 1 else values[g][e * own : (e + 1) * own]
                received.append(piece if k == 0 else over_plane(piece, k))
        return received

    enc_blocks = gather_column(enc_weight.T.astype(bf16))

    stacked = jnp.stack([cell_counts.astype(f32), cell_seeds.astype(f32), cell_factor])
    stacked = stacked.reshape(3, COLUMNS * plane, own)
    cells = jnp.concatenate(
        [
            lax.dynamic_slice_in_dim(stacked, column * plane + (spot ^ k), 1, axis=1)
            for k in range(plane)
        ],
        axis=1,
    ).reshape(3, share // 128, 128)
    at = (column * plane + spot) * own
    ids = lax.dynamic_slice_in_dim(batch_ids, at, own).reshape(own, 1)
    noise = jnp.pad(lax.dynamic_slice_in_dim(noise_draw, at, own), ((0, 0), (0, 128 - latent)))
    head_wide = jnp.pad(head_rows, ((0, 7), (0, 128 - 2 * latent)))

    regions = COLUMNS * width
    masks, factors = pl.pallas_call(
        functools.partial(mask_kernel, total, width),
        grid=(share // 128,),
        in_specs=[SMEM, pl.BlockSpec(cells.shape, lambda i: (0, 0, 0))],
        out_specs=(
            pl.BlockSpec((128, regions), lambda i: (i, 0)),
            pl.BlockSpec((128, 128), lambda i: (i, 0)),
        ),
        out_shape=shaped(((share, regions), bf16), ((share, 128), f32)),
        compiler_params=params(),
        cost_estimate=cost(6 * share * regions, 2 * share * regions),
        name="masks",
    )(bases, cells)

    def encode(group):
        return pl.pallas_call(
            functools.partial(encode_kernel, width),
            grid=(1,),
            in_specs=[pl.BlockSpec((block, regions), lambda i: (group, 0))]
            + [pl.BlockSpec((64, width), lambda i: (0, 0))] * (2 * COLUMNS),
            out_specs=pl.BlockSpec((block, 128), lambda i: (0, 0)),
            out_shape=jax.ShapeDtypeStruct((block, 128), f32),
            compiler_params=params(),
            cost_estimate=cost(2 * block * regions * 256, 2 * block * regions),
            name="encode",
        )(masks, *enc_blocks)

    partial_pre = [None] * groups
    for g in [*range(1, groups), 0]:
        partial_pre[g] = encode(g)
    pre_parts = scatter_plane(partial_pre)

    dec_send = jnp.concatenate(
        [dec_weight.astype(bf16), region_vecs.astype(bf16), jnp.zeros((15, width), bf16)], axis=0
    )
    dec_send, _ = lax.optimization_barrier((dec_send, partial_pre[1 % groups]))
    dec_blocks = gather_column(dec_send)
    dec_pack, lines = pl.pallas_call(
        pack_kernel,
        in_specs=[SMEM] + [VMEM] * (2 * COLUMNS),
        out_specs=(VMEM, VMEM),
        out_shape=shaped(((COLUMNS, 256, width), bf16), ((COLUMNS, 32, width), f32)),
        compiler_params=params(),
        name="pack",
    )(info, *dec_blocks)

    saved_shapes = shaped(
        ((own, 128), bf16),
        ((4, own, 128), f32),
        ((own, 128), f32),
        ((own, 128), f32),
        ((2, own, 128), f32),
        ((8, 128), f32),
    )
    decoded_low, *saved, trunk_stats = pl.pallas_call(
        functools.partial(forward_kernel, plane, latent, own),
        in_specs=[SMEM] + [VMEM] * (5 + plane),
        out_specs=(VMEM,) * 6,
        out_shape=saved_shapes,
        compiler_params=params(),
        cost_estimate=cost(2 * 30 * own * 128 * 128, 4 * own * 128 * 10),
        name="forward",
    )(info, ids, noise, trunk_rows, head_wide, cells, *pre_parts)

    low_groups = gather_plane(decoded_low)

    def decode(group, low, sums):
        specs = [
            SMEM,
            pl.BlockSpec((block, 128), lambda j: (0, 0)),
            pl.BlockSpec((block, width), lambda j: (group, j)),
            pl.BlockSpec((block, 128), lambda j: (group, 0)),
            pl.BlockSpec((1, 256, width), lambda j: (j, 0, 0)),
            pl.BlockSpec((1, 32, width), lambda j: (j, 0, 0)),
        ]
        sum_spec = pl.BlockSpec((1, 72, width), lambda j: (j, 0, 0))
        return pl.pallas_call(
            functools.partial(decode_kernel, loss_scale, sums is not None),
            grid=(COLUMNS,),
            in_specs=specs + ([] if sums is None else [sum_spec] * 2),
            out_specs=(
                sum_spec,
                sum_spec,
                pl.BlockSpec((block, 128), lambda j: (0, 0)),
                pl.BlockSpec((8, 128), lambda j: (0, 0)),
            ),
            out_shape=shaped(
                ((COLUMNS, 72, width), f32),
                ((COLUMNS, 72, width), f32),
                ((block, 128), f32),
                ((8, 128), f32),
            ),
            scratch_shapes=[
                pltpu.VMEM((block, width), f32),
                pltpu.VMEM((block, width), bf16),
                pltpu.VMEM((block, 256), bf16),
                pltpu.VMEM((144, block), bf16),
            ],
            input_output_aliases={} if sums is None else {6: 0, 7: 1},
            compiler_params=params(),
            cost_estimate=cost(60 * block * regions * 10, 6 * block * regions, 3 * block * regions),
            name="decode",
        )(info, low, masks, factors, dec_pack, lines, *([] if sums is None else sums))

    sums = None
    backs, losses = [], []
    for g in range(groups):
        *sums, back, loss_tile = decode(g, low_groups[g], sums)
        backs.append(back)
        losses.append(loss_tile)
    back_parts = scatter_plane(backs)

    dec_other = over_dp(sums[1])
    dec_parts = [sums[0][0], dec_other[0]]
    for j in range(1, COLUMNS):
        dec_parts.append(to_column(sums[0][j] + dec_other[j], j))

    pre_low, trunk_mine, trunk_other = pl.pallas_call(
        functools.partial(backward_kernel, plane, latent, loss_scale),
        in_specs=[SMEM] + [VMEM] * (8 + plane),
        out_specs=(VMEM,) * 3,
        out_shape=shaped(((own, 128), bf16), ((160, 128), f32), ((160, 128), f32)),
        scratch_shapes=[pltpu.VMEM((320, 128), f32)],
        compiler_params=params(),
        cost_estimate=cost(2 * 60 * own * 128 * 128, 4 * own * 128 * 10),
        name="backward",
    )(info, ids, noise, trunk_rows, head_wide, *saved, *back_parts)

    pre_groups = gather_plane(pre_low)
    enc_sums = pl.pallas_call(
        functools.partial(encode_back_kernel, groups),
        grid=(COLUMNS,),
        in_specs=[pl.BlockSpec((share, width), lambda j: (0, j))]
        + [pl.BlockSpec((block, 128), lambda j: (0, 0))] * groups,
        out_specs=(pl.BlockSpec((1, 64, width), lambda j: (j, 0, 0)),) * 2,
        out_shape=shaped(((COLUMNS, 64, width), f32), ((COLUMNS, 64, width), f32)),
        scratch_shapes=[pltpu.VMEM((128, share), bf16)],
        compiler_params=params(),
        cost_estimate=cost(2 * share * regions * 256, 2 * share * regions),
        name="encode_back",
    )(masks, *pre_groups)
    enc_other = over_dp(enc_sums[1])
    enc_parts = [enc_sums[0][0], enc_other[0]]
    for j in range(1, COLUMNS):
        enc_parts.append(to_column(enc_sums[0][j] + enc_other[j], j))

    trunk_half = trunk_mine + over_dp(trunk_other)
    trunk_half = trunk_half + sum(from_column(trunk_half, j) for j in range(1, COLUMNS))
    trunk_half = trunk_half + sum(over_plane(trunk_half, k) for k in range(1, plane))
    trunk_rest = over_dp(trunk_half)

    like = lambda *arrays: shaped(*((x.shape, f32) for x in arrays))
    tile = jax.ShapeDtypeStruct((8, 128), f32)
    dec_first_new, dec_second_new, dec_update, vec_first_new, vec_second_new, vec_update, dec_stats = (
        pl.pallas_call(
            functools.partial(dec_lamb_kernel, len(dec_parts), loss_scale),
            in_specs=[SMEM] + [VMEM] * (6 + len(dec_parts)),
            out_specs=(VMEM,) * 7,
            out_shape=like(dec_weight, dec_weight, dec_weight, region_vecs, region_vecs, region_vecs)
            + (tile,),
            compiler_params=params(),
            name="dec_lamb",
        )(info, dec_weight, dec_first, dec_second, region_vecs, vec_first, vec_second, *dec_parts)
    )
    (
        trunk_new,
        trunk_first_new,
        trunk_second_new,
        head_new,
        head_first_new,
        head_second_new,
        trunk_norms,
    ) = pl.pallas_call(
        functools.partial(trunk_lamb_kernel, latent),
        in_specs=[SMEM] + [VMEM] * 8,
        out_specs=(VMEM,) * 7,
        out_shape=like(trunk_rows, trunk_rows, trunk_rows, head_rows, head_rows, head_rows) + (tile,),
        scratch_shapes=[pltpu.VMEM((320, 128), f32)],
        compiler_params=params(),
        name="trunk_lamb",
    )(
        info,
        trunk_half,
        trunk_rest,
        trunk_rows,
        trunk_first,
        trunk_second,
        head_rows,
        head_first,
        head_second,
    )
    enc_first_new, enc_second_new, enc_update, enc_stats = pl.pallas_call(
        functools.partial(enc_lamb_kernel, len(enc_parts)),
        in_specs=[VMEM] * (3 + len(enc_parts)),
        out_specs=(VMEM,) * 4,
        out_shape=like(enc_weight, enc_weight, enc_weight) + (tile,),
        compiler_params=params(),
        name="enc_lamb",
    )(enc_weight, enc_first, enc_second, *enc_parts)

    lane = lax.broadcasted_iota(jnp.int32, (8, 128), 1)
    row = lax.broadcasted_iota(jnp.int32, (8, 128), 0)
    loss_sum = jnp.sum(sum(losses))
    stats = enc_stats + dec_stats + trunk_stats
    stats = stats + jnp.where((lane == 8) & (row == 0), loss_sum, 0.0)
    stats = stats + over_dp(stats)
    stats = stats + sum(over_plane(stats, k) for k in range(1, plane))
    stat_parts = [stats] + [from_column(stats, j) for j in range(1, COLUMNS)]
    loss, enc_new, enc_copy, dec_new, dec_copy, vecs_new, norms = pl.pallas_call(
        functools.partial(final_kernel, len(stat_parts), loss_scale, all_cells),
        in_specs=[SMEM] + [VMEM] * (7 + len(stat_parts)),
        out_specs=(SMEM,) + (VMEM,) * 6,
        out_shape=shaped(
            ((2,), f32),
            (enc_weight.shape, f32),
            (enc_weight.shape, bf16),
            (dec_weight.shape, f32),
            (dec_weight.shape, bf16),
            (region_vecs.shape, f32),
            ((2, 10), f32),
        ),
        compiler_params=params(),
        name="final",
    )(
        info,
        trunk_norms,
        *stat_parts,
        enc_weight,
        enc_update,
        dec_weight,
        dec_update,
        region_vecs,
        vec_update,
    )
    return (
        loss,
        enc_new,
        enc_first_new,
        enc_second_new,
        enc_copy,
        dec_new,
        dec_first_new,
        dec_second_new,
        dec_copy,
        vecs_new,
        vec_first_new,
        vec_second_new,
        trunk_new,
        trunk_first_new,
        trunk_second_new,
        head_new,
        head_first_new,
        head_second_new,
        norms,
    )


def solution(mesh):
    regions = mesh.shape["region"]
    devices = mesh.devices.reshape(mesh.shape["dp"], COLUMNS, regions // COLUMNS)
    inner = Mesh(devices, ("dp", "column", "plane"))
    across = ("column", "plane")
    by_row, by_line = P(across, "dp"), P("dp", across)
    return jax.shard_map(
        on_device,
        mesh=inner,
        in_specs=(P("dp"), P("dp"), P("dp"), P("dp", None), P("dp"))
        + (by_row,) * 3
        + (by_line,) * 6
        + (P(),) * 6,
        out_specs=(P(),) + (by_row,) * 4 + (by_line,) * 7 + (P(),) * 7,
        check_vma=False,
    )
```

```python
import functools

import jax
import jax.numpy as jnp
from jax import lax
from jax.experimental import pallas as pl
from jax.experimental.pallas import tpu as pltpu
from jax.sharding import Mesh
from jax.sharding import PartitionSpec as P

BATCHES = 8
COLUMNS = 4
PIECE = 40
SAFE = 40.0
HOT, NOISE, LEFT, CENTRE, LOG_VAR, SCALE = range(4, 10)
LOG2_E = 1.4426950408889634
LN_2 = 0.6931471805599453

norm_eps = 1e-05
leak_slope = 0.01
decay_rate = 0.5
weight_decay = 0.01
learn_rate = 0.5
lamb_eps = 1e-12

f32 = jnp.float32
bf16 = jnp.bfloat16
VMEM = pl.BlockSpec(memory_space=pltpu.VMEM)
SMEM = pl.BlockSpec(memory_space=pltpu.SMEM)
MEGA = 1024 * 1024


def params(mib=16):
    return pltpu.CompilerParams(vmem_limit_bytes=mib * MEGA)


def place():
    return tuple(lax.axis_index(name) for name in ("dp", "column", "plane"))


def exact(left, right, contract=((1,), (0,))):
    return lax.dot_general(
        left, right, (contract, ((), ())), precision=lax.Precision.HIGHEST, preferred_element_type=f32
    )


def wide(left, right, contract=((1,), (0,))):
    return lax.dot_general(left, right, (contract, ((), ())), preferred_element_type=f32)


def remainder(values, divisor):
    guess = jnp.floor(values.astype(f32) * (1.0 / divisor)).astype(jnp.int32)
    rest = values - guess * divisor
    rest = jnp.where(rest < 0, rest + divisor, rest)
    return jnp.where(rest >= divisor, rest - divisor, rest)


def turns(values, total):
    whole = 2**32 // total
    part = (2**32 % total) / total
    return values * whole + (values.astype(f32) * part + 0.5).astype(jnp.int32)


def mask_kernel(total, width, plane, own, in_order, counts_ref, seeds_ref, factors_ref, *refs):
    mask_ref, factor_ref, table_ref, held_ref = refs
    step = pl.program_id(0)
    lines_here = table_ref.shape[1]

    @pl.when(step == 0)
    def _():
        _, column, spot = place()
        if in_order:
            counts, seeds, factors = counts_ref[...], seeds_ref[...], factors_ref[...]
        else:
            each = own // 128
            starts = [
                (column * plane + (spot ^ k)) * each + i for k in range(plane) for i in range(each)
            ]
            counts, seeds, factors = (
                jnp.concatenate([ref[pl.ds(at, 1), :] for at in starts], axis=0)
                for ref in (counts_ref, seeds_ref, factors_ref)
            )
        stride = 6 * remainder(seeds, total // 6) + 1
        low_end = jnp.int32(-(2**31))
        half = jnp.int32(2**31 // total)
        for j in range(COLUMNS):
            base = (lax.rem(column + j, COLUMNS) * plane + spot) * width
            upper = remainder(stride * (base // 256), total)
            start = remainder(upper * 256 + stride * (base % 256) + seeds, total)
            table_ref[j] = turns(start, total) + (low_end + half)
        table_ref[4] = turns(stride, total)
        table_ref[5] = turns(remainder(stride * 128, total), total)
        table_ref[6] = turns(counts, total) + low_end
        cell = lax.broadcasted_iota(jnp.int32, (lines_here, 128), 0) * 128
        cell = cell + lax.broadcasted_iota(jnp.int32, (lines_here, 128), 1)
        known = jnp.where(cell < own, counts.astype(f32) * jnp.log(factors), 0.0)
        row = lax.broadcasted_iota(jnp.int32, (8, 128), 0)
        known = jnp.where(row == 0, jnp.sum(known, axis=0, keepdims=True), 0.0)
        factor_ref[128 * lines_here : 128 * lines_here + 8, :] = known
        held_ref[...] = factors

    at = pl.ds(step, 1)
    rows = [table_ref[j, at, :] for j in range(7)]
    table = jnp.concatenate(rows + rows[:1], axis=0).T
    factor_ref[pl.ds(pl.multiple_of(step * 128, 128), 128), :] = jnp.broadcast_to(held_ref[at, :], (128, 128)).T
    for part in range(4):
        lines = slice(part * 32, part * 32 + 32)
        shape = (32, 128)
        lane = lax.broadcasted_iota(jnp.int32, shape, 1)
        span = jnp.broadcast_to(table[lines, 4:5], shape) * lane
        advance = jnp.broadcast_to(table[lines, 5:6], shape)
        limit = jnp.broadcast_to(table[lines, 6:7], shape)
        for column in range(COLUMNS):
            value = jnp.broadcast_to(table[lines, column : column + 1], shape) + span
            for group in range(width // 128):
                here = column * width + group * 128
                mask_ref[lines, here : here + 128] = jnp.where(value < limit, 1.0, 0.0).astype(bf16)
                value = value + advance


def encode_kernel(width, group, own, mask_ref, *refs):
    out_ref = refs[-1]
    cells = out_ref.shape[0]
    lines = slice(group * cells, (group + 1) * cells)
    total = None
    for column in range(COLUMNS):
        block = jnp.concatenate([refs[2 * column][...], refs[2 * column + 1][...]], axis=0)
        term = wide(mask_ref[lines, column * width : (column + 1) * width], block, ((1,), (1,)))
        total = term if total is None else total + term
    out_ref[...] = total
    for ref in refs[2 * COLUMNS : -1]:
        out_ref[0:own] += ref[...]


def pack_kernel(gain_row, trunk_ref, *refs):
    weight_ref, line_ref, small_ref = refs[-3:]
    is_first = place()[0] == 0
    longest = largest = jnp.zeros((1, 1), f32)
    for column in range(COLUMNS):
        mine = refs[2 * column][...]
        other = refs[2 * column + 1][...]
        mine_line = mine[64:80].astype(f32)[0:1]
        other_line = other[64:80].astype(f32)[0:1]
        bias = jnp.where(is_first, mine_line, other_line)
        logit = jnp.where(is_first, other_line, mine_line)
        width = mine.shape[1]
        row = lax.broadcasted_iota(jnp.int32, (16, width), 0)
        weight_ref[column, 0:64] = mine[0:64]
        weight_ref[column, 64:128] = other[0:64]
        weight_ref[column, 128:144] = jnp.where(row == 0, bias, 0.0).astype(bf16)
        weight_ref[column, 144:256] = jnp.zeros((112, width), bf16)
        spread = jnp.exp(-jnp.abs(logit))
        chance = jnp.where(logit >= 0, 1.0, spread) / (1.0 + spread)
        logs = jnp.minimum(logit, 0.0) - jnp.log(1.0 + spread)
        line_ref[column, 0:16] = jnp.broadcast_to(chance, (16, width))
        line_ref[column, 16:32] = jnp.broadcast_to(logs, (16, width))
        one, two = mine[0:64].astype(f32), other[0:64].astype(f32)
        squares = jnp.sum(one * one + two * two, axis=0, keepdims=True)
        longest = jnp.maximum(longest, jnp.max(squares, axis=1, keepdims=True))
        largest = jnp.maximum(largest, jnp.max(jnp.abs(bias), axis=1, keepdims=True))
    gain = jnp.max(jnp.abs(trunk_ref[gain_row + 3 : gain_row + 4, :]), axis=1, keepdims=True)
    shift = trunk_ref[gain_row + 7 : gain_row + 8, :]
    reach = gain * (128.0**0.5) + jnp.sqrt(jnp.sum(shift * shift, axis=1, keepdims=True))
    bound = 1.02 * reach * jnp.sqrt(longest) + largest
    small_ref[0] = jnp.sum(jnp.where(bound < SAFE, 1, 0))


def normalize(values):
    centre = values - jnp.mean(values, axis=-1, keepdims=True)
    spread = jnp.mean(centre * centre, axis=-1, keepdims=True)
    scale = lax.rsqrt(spread + norm_eps)
    return centre * scale, scale


def leaky(values):
    return jnp.where(values >= 0, values, leak_slope * values)


def swap_halves(values, is_first):
    return jnp.where(is_first, values, pltpu.roll(values, 64, 1))


class Rows:
    def __init__(self, hidden, latent):
        self.enc_two = BATCHES
        self.dec_one = BATCHES + hidden
        self.dec_two = 2 * BATCHES + hidden + latent
        self.gain = 2 * BATCHES + 2 * hidden + latent
        self.shift = self.gain + 4
        self.end = self.gain + 8


def turned_rows(ref, own):
    values = ref[...].astype(f32)
    rows, spare = values.shape[0], -own % 128
    if spare:
        values = jnp.concatenate([values, jnp.zeros((rows, spare), f32)], axis=1)
    if rows == 1:
        full = jnp.broadcast_to(values, (128, own + spare))
    else:
        full = jnp.concatenate([values, jnp.zeros((128 - rows, own + spare), f32)], axis=0)
    return full.T[0:own]


def forward_kernel(parts, latent, own, _, ids_ref, noise_ref, trunk_ref, head_ref, *refs):
    part_refs = refs[:parts]
    low_ref, saved_ref, stat_ref = refs[parts:]
    is_first = place()[0] == 0
    rows = Rows(128, latent)
    total = part_refs[0][0:own]
    for ref in part_refs[1:]:
        total = total + ref[...]
    total = swap_halves(total, is_first)
    lane = lax.broadcasted_iota(jnp.int32, total.shape, 1)
    ids = turned_rows(ids_ref, own).astype(jnp.int32)
    noise = turned_rows(noise_ref, own)
    saved_ref[NOISE] = noise
    hot = jnp.where(lane == ids, 1.0, 0.0)
    saved_ref[HOT] = hot
    gains = trunk_ref[rows.gain : rows.gain + 4, :]
    shifts = trunk_ref[rows.shift : rows.shift + 4, :]

    def act(index, values):
        normal, scale = normalize(values)
        saved_ref[index] = normal
        return leaky(normal * gains[index : index + 1] + shifts[index : index + 1]), scale

    first, scale0 = act(0, total + exact(hot, trunk_ref[0:128, :]))
    second, scale1 = act(1, exact(first, trunk_ref[rows.enc_two : rows.enc_two + 128, :]))
    moments = exact(second, head_ref[0:128, :]) + head_ref[128:129, :]
    inside = lane < latent
    centre = jnp.where(inside, moments, 0.0)
    log_var = jnp.where(inside, pltpu.roll(moments, 128 - latent, 1), 0.0)
    sample = centre + jnp.exp(0.5 * log_var) * noise
    left = sample + jnp.where(lane == ids + latent, 1.0, 0.0)
    third, scale2 = act(2, exact(left, trunk_ref[rows.dec_one : rows.dec_one + 128, :]))
    fourth, scale3 = act(3, exact(third, trunk_ref[rows.dec_two : rows.dec_two + 128, :]))
    low_ref[...] = swap_halves(fourth, is_first).astype(bf16)
    saved_ref[LEFT] = left
    saved_ref[CENTRE] = centre
    saved_ref[LOG_VAR] = log_var
    saved_ref[SCALE] = jnp.where(
        lane == 0, scale0, jnp.where(lane == 1, scale1, jnp.where(lane == 2, scale2, scale3))
    )
    diverge = 0.5 * jnp.sum(jnp.exp(log_var) + centre * centre - 1.0 - log_var)
    stat_ref[...] = stat_tile([(9, diverge)])


def decode_kernel(loss_scale, group, parts, small_ref, low_ref, mask_ref, factor_ref, weight_ref, line_ref, *refs):
    saved_ref, loss_in, *refs = refs
    has_sum = group != 1
    if has_sum:
        refs = refs[2:]
    part_refs, refs = refs[:parts], refs[parts:]
    mine_ref, other_ref, back_ref, loss_ref, logit_ref, grad_ref, left_ref, turned_ref = refs
    cells, width = grad_ref.shape
    half = cells // 2
    halves = (slice(0, half), slice(half, cells))
    blocks = width // 128
    first_row = group * cells
    zero = jnp.zeros((8, 128), f32)

    low = low_ref[...]
    left_ref[:, 0:128] = low
    lane = lax.broadcasted_iota(jnp.int32, (cells, 128), 1)
    left_ref[:, 128:256] = jnp.where(lane == 0, 1.0, 0.0).astype(bf16)
    turned_ref[0:128, :] = low.astype(f32).T.astype(bf16)
    row = lax.broadcasted_iota(jnp.int32, (16, cells), 0)
    turned_ref[128:144, :] = jnp.where(row == 0, 1.0, 0.0).astype(bf16)
    back_ref[...] = jnp.zeros_like(back_ref)
    grad_ref[halves[1], :] = jnp.zeros((half, width), bf16)
    if not has_sum:
        mine_ref[...] = jnp.zeros_like(mine_ref)
        other_ref[...] = jnp.zeros_like(other_ref)

    def logits_of(lines, column):
        logit_ref[lines, :] = wide(left_ref[lines, :], weight_ref[column])

    def add_sums(lines, column):
        product = wide(turned_ref[:, lines], grad_ref[lines, :])
        tail = product[128:136]
        mine_ref[column, 0:72] += jnp.concatenate([product[0:64], tail], axis=0)
        other_ref[column, 0:72] += jnp.concatenate([product[64:128], tail], axis=0)

    def add_back(lines, column):
        back_ref[lines, :] += wide(grad_ref[lines, :], weight_ref[column, 0:128], ((1,), (1,)))

    def add_odds(column, odds):
        line = jnp.sum(jnp.concatenate(odds, axis=1), axis=0, keepdims=True)
        place = lax.broadcasted_iota(jnp.int32, (8, width), 0)
        line = jnp.where(place == 1, line, 0.0)
        mine_ref[column, 64:72] += line
        other_ref[column, 64:72] += line

    def finish(loss_sum):
        if group == 0:
            loss_sum = loss_sum + factor_ref[-8:, :]
        loss_ref[...] = loss_in[...] + stat_tile([(8, jnp.sum(loss_sum))])
        for ref in part_refs:
            back_ref[0 : ref.shape[0]] += ref[...]

    def quick(column, at, odds, loss_sum):
        factor = factor_ref[first_row + at : first_row + at + 16, :]
        held = None
        for block in range(blocks):
            lanes = slice(block * 128, block * 128 + 128)
            far = slice(column * width + block * 128, column * width + block * 128 + 128)
            ratio = jnp.exp2(logit_ref[at : at + 16, lanes] * -LOG2_E)
            whole = 1.0 + ratio
            chance = factor * line_ref[column, 0:16, lanes]
            opened = mask_ref[first_row + at : first_row + at + 16, far].astype(f32) > 0.5
            rest = jnp.where(opened, 1.0, whole - chance)
            inverse = pl.reciprocal(whole * rest)
            part = jnp.where(opened, -1.0, chance) * inverse
            grad_ref[at : at + 16, lanes] = ((ratio * part) * loss_scale).astype(bf16)
            odds[block] = odds[block] + part[0:8] + part[8:16]
            likely = rest * (rest * inverse)
            held = likely if held is None else held * likely
            if block % 2 == 1 or block == blocks - 1:
                logs = jnp.log2(held)
                loss_sum = loss_sum + logs[0:8] + logs[8:16]
                held = None
        return loss_sum

    @pl.when(small_ref[0] == 1)
    def _():
        logits_of(halves[0], 0)
        loss_sum = zero
        for column in range(COLUMNS):
            odds = [zero] * blocks
            for at in range(0, half, 16):
                loss_sum = quick(column, at, odds, loss_sum)
            logits_of(halves[1], column)
            if column > 0:
                add_sums(halves[1], column - 1)
                add_back(halves[1], column - 1)
            for at in range(half, cells, 16):
                loss_sum = quick(column, at, odds, loss_sum)
            if column + 1 < COLUMNS:
                logits_of(halves[0], column + 1)
            add_sums(halves[0], column)
            add_back(halves[0], column)
            add_odds(column, odds)
        add_sums(halves[1], COLUMNS - 1)
        add_back(halves[1], COLUMNS - 1)
        finish(loss_sum * LN_2)

    def steady(column, loss_sum):
        logits_of(slice(None), column)

        def step(index, carried):
            loss_sum, *odds = carried
            here = pl.multiple_of(index * 16, 16)
            at = pl.ds(here, 16)
            far_at = pl.ds(pl.multiple_of(first_row + here, 16), 16)
            factor = factor_ref[far_at, :]
            top = bottom = held = None
            for block in range(blocks):
                lanes = slice(block * 128, block * 128 + 128)
                far = pl.ds(pl.multiple_of(column * width + block * 128, 128), 128)
                logits = logit_ref[at, lanes]
                spread = jnp.exp(-jnp.abs(logits))
                whole = 1.0 + spread
                positive = logits >= 0
                chance = factor * line_ref[column, 0:16, lanes]
                taken = chance * jnp.where(positive, 1.0, spread)
                opened = mask_ref[far_at, far].astype(f32) > 0.5
                rest = jnp.where(opened, 1.0, whole - taken)
                inverse = pl.reciprocal(whole * rest)
                upper = jnp.where(opened, jnp.where(positive, -spread, -1.0), spread * chance)
                slope = upper * inverse
                grad_ref[at, lanes] = (slope * loss_scale).astype(bf16)
                part = jnp.where(opened, -1.0, taken * whole * inverse) - slope
                odds[block] = odds[block] + part[0:8] + part[8:16]
                likely = jnp.where(opened, jnp.minimum(logits, 0.0), 0.0)
                held = likely if held is None else held + likely
                top = rest if top is None else top * rest
                bottom = whole if bottom is None else bottom * whole
            held = held + (jnp.log(top) - jnp.log(bottom))
            return (loss_sum + held[0:8] + held[8:16], *odds)

        loss_sum, *odds = lax.fori_loop(0, cells // 16, step, (loss_sum,) + (zero,) * blocks)
        add_sums(slice(None), column)
        add_back(slice(None), column)
        add_odds(column, odds)
        return loss_sum

    @pl.when(small_ref[0] != 1)
    def _():
        finish(lax.fori_loop(0, COLUMNS, steady, zero))


def backward_kernel(parts, latent, loss_scale, _, trunk_ref, head_ref, saved_ref, *refs):
    part_refs = refs[:parts]
    low_ref, mine_ref, other_ref, sum_ref = refs[parts:]
    dp, own_column, _ = place()
    is_first = dp == 0
    own = low_ref.shape[0]
    rows = Rows(128, latent)
    total = part_refs[0][0:own]
    for ref in part_refs[1:]:
        total = total + ref[...]
    total = swap_halves(total, is_first)
    lane = lax.broadcasted_iota(jnp.int32, total.shape, 1)
    gains = trunk_ref[rows.gain : rows.gain + 4, :]
    shifts = trunk_ref[rows.shift : rows.shift + 4, :]
    sum_ref[...] = jnp.zeros_like(sum_ref)
    rows_in, rows_out = ((0,), (0,)), ((1,), (1,))

    def output(index):
        return leaky(saved_ref[index] * gains[index : index + 1] + shifts[index : index + 1])

    def pull(index, grad):
        normal = saved_ref[index]
        gain = gains[index : index + 1]
        before = normal * gain + shifts[index : index + 1]
        grad = jnp.where(before >= 0, grad, leak_slope * grad)
        at = rows.gain + index
        sum_ref[at : at + 1, :] = jnp.sum(grad * normal, axis=0, keepdims=True)
        at = rows.shift + index
        sum_ref[at : at + 1, :] = jnp.sum(grad, axis=0, keepdims=True)
        grad = grad * gain
        plain = jnp.mean(grad, axis=-1, keepdims=True)
        along = jnp.mean(grad * normal, axis=-1, keepdims=True)
        return (grad - plain - normal * along) * saved_ref[SCALE][:, index : index + 1]

    grad = pull(3, total)
    sum_ref[rows.dec_two : rows.dec_two + 128, :] = exact(output(2), grad, rows_in)
    grad = pull(2, exact(grad, trunk_ref[rows.dec_two : rows.dec_two + 128, :], rows_out))
    one = exact(saved_ref[LEFT], grad, rows_in)
    sum_ref[rows.dec_one : rows.dec_two, :] = one[0 : rows.dec_two - rows.dec_one]
    grad = exact(grad, trunk_ref[rows.dec_one : rows.dec_one + 128, :], rows_out)
    inside = lane < latent
    grad = jnp.where(inside, grad, 0.0)
    centre, log_var = saved_ref[CENTRE], saved_ref[LOG_VAR]
    grad_centre = grad + loss_scale * centre
    grad_log = grad * 0.5 * jnp.exp(0.5 * log_var) * saved_ref[NOISE] + (0.5 * loss_scale) * (
        jnp.exp(log_var) - 1.0
    )
    both = jnp.where(inside, grad_centre, pltpu.roll(jnp.where(inside, grad_log, 0.0), latent, 1))
    head = exact(both, output(1), rows_in)
    sum_ref[296 : 296 + 24, :] = head[0:24]
    sum_ref[296 + 2 * latent : 297 + 2 * latent, :] = jnp.sum(both, axis=0, keepdims=True)
    grad = pull(1, exact(both, head_ref[0:128, :], rows_out))
    sum_ref[rows.enc_two : rows.enc_two + 128, :] = exact(output(0), grad, rows_in)
    grad = pull(0, exact(grad, trunk_ref[rows.enc_two : rows.enc_two + 128, :], rows_out))
    low = grad.astype(bf16)
    hot = saved_ref[HOT].astype(bf16)
    sum_ref[0:BATCHES, :] = wide(hot, low, rows_in)[0:BATCHES]
    low_ref[...] = swap_halves(low.astype(f32), is_first).astype(bf16)
    for j in range(COLUMNS):
        start = lax.rem(own_column + j, COLUMNS) * PIECE
        for ref, half in ((mine_ref, dp), (other_ref, 1 - dp)):
            at = pl.multiple_of(half * (COLUMNS * PIECE) + start, 8)
            ref[j] = sum_ref[pl.ds(at, PIECE), :]


def encode_back_kernel(groups, mask_ref, line_ref, loss_in, trunk_mine_ref, trunk_other_ref, *refs):
    low_refs = refs[:groups]
    mine_ref, other_ref, known_ref, turned_ref = refs[groups:]
    cells = low_refs[0].shape[0]
    share = turned_ref.shape[1]
    width = mine_ref.shape[2]
    for group in range(groups):
        turned_ref[0:128, group * cells : (group + 1) * cells] = (
            low_refs[group][...].astype(f32).T.astype(bf16)
        )
    row = lax.broadcasted_iota(jnp.int32, (16, share), 0)
    turned_ref[128:144, :] = jnp.where(row == 0, 1.0, 0.0).astype(bf16)
    known = jnp.zeros((8, width), f32)
    for column in range(COLUMNS):
        product = wide(turned_ref[...], mask_ref[:, column * width : (column + 1) * width])
        mine_ref[column, 0:64] = product[0:64]
        other_ref[column, 0:64] = product[64:128]
        known = known + product[128:136] * line_ref[column, 16:24, :]
        for ref, trunk_ref in ((mine_ref, trunk_mine_ref), (other_ref, trunk_other_ref)):
            ref[column, 64:72] = jnp.zeros((8, width), f32)
            for part in range(PIECE // 8):
                lanes = slice(part * 128, part * 128 + 128)
                ref[column, 64:72, lanes] = trunk_ref[column, part * 8 : part * 8 + 8, :]
    known_ref[...] = loss_in[...] + stat_tile([(8, jnp.sum(known))])


def sum_kernel(mine_ref, other_ref, *out_refs):
    for j in range(1, COLUMNS):
        total = mine_ref[j] + other_ref[j]
        tail = total[64:72]
        high = tail.astype(bf16)
        low = (tail - high.astype(f32)).astype(bf16)
        out_refs[j - 1][0:64] = total[0:64].astype(bf16)
        out_refs[j - 1][64:80] = jnp.concatenate([high.astype(f32), low.astype(f32)], axis=0).astype(bf16)


def stat_tile(pairs):
    lane = lax.broadcasted_iota(jnp.int32, (8, 128), 1)
    row = lax.broadcasted_iota(jnp.int32, (8, 128), 0)
    tile = jnp.zeros((8, 128), f32)
    for index, value in pairs:
        tile = jnp.where(lane == index, value, tile)
    return jnp.where(row == 0, tile, 0.0)


def moments_of(weight, grad, first, second):
    first_new = decay_rate * first + (1.0 - decay_rate) * grad
    second_new = decay_rate * second + (1.0 - decay_rate) * grad * grad
    update = first_new / (jnp.sqrt(second_new) + lamb_eps) + weight_decay * weight
    return first_new, second_new, update


def enc_lamb_kernel(*refs):
    weight_ref, first_ref, second_ref, mine_ref, other_ref, *part_refs = refs[: 4 + COLUMNS]
    stat_refs = refs[4 + COLUMNS : -4]
    first_out, second_out, update_out, tile_out = refs[-4:]
    grad = mine_ref[0] + other_ref[0]
    tail = grad[64:72]
    grad = grad[0:64]
    for ref in part_refs:
        grad = grad + ref[0:64].astype(f32)
        extra = ref[64:80].astype(f32)
        tail = tail + (extra[0:8] + extra[8:16])
    weight = weight_ref[...]
    first, second, update = moments_of(weight, grad, first_ref[...], second_ref[...])
    first_out[...] = first
    second_out[...] = second
    update_out[...] = update
    others = sum(ref[...] for ref in stat_refs)
    stats = stat_tile(
        [
            (0, jnp.sum(weight * weight)),
            (4, jnp.sum(update * update)),
        ]
    )
    tile_out[0:8] = stats + others
    for part in range(PIECE // 8):
        tile_out[8 + part * 8 : 16 + part * 8] = tail[:, part * 128 : part * 128 + 128]


def dec_lamb_kernel(loss_scale, *refs):
    weight_ref, first_ref, second_ref, vec_ref, vec_first_ref, vec_second_ref, mine_ref, other_ref = refs[:8]
    part_refs, refs = refs[8 : 7 + COLUMNS], refs[-7:]
    first_out, second_out, update_out, vec_first_out, vec_second_out, vec_update_out, stat_out = refs
    grad = mine_ref[0] + other_ref[0]
    tail = grad[64:72]
    grad = grad[0:64]
    for ref in part_refs:
        grad = grad + ref[0:64].astype(f32)
        extra = ref[64:80].astype(f32)
        tail = tail + (extra[0:8] + extra[8:16])
    weight = weight_ref[...]
    first, second, update = moments_of(weight, grad, first_ref[...], second_ref[...])
    first_out[...] = first
    second_out[...] = second
    update_out[...] = update
    is_first = place()[0] == 0
    vec = vec_ref[...]
    low = vec.astype(bf16).astype(f32)
    keep = 1.0 / (1.0 + jnp.exp(low))
    line = tail[0:1]
    line = jnp.where(is_first, line, keep * (tail[1:2] * loss_scale + line))
    vec_one, vec_two, vec_update = moments_of(vec, line, vec_first_ref[...], vec_second_ref[...])
    vec_first_out[...] = vec_one
    vec_second_out[...] = vec_two
    vec_update_out[...] = vec_update
    vec_square = jnp.sum(vec * vec)
    update_square = jnp.sum(vec_update * vec_update)
    stat_out[...] = stat_tile(
        [
            (1, jnp.sum(weight * weight)),
            (2, jnp.where(is_first, vec_square, 0.0)),
            (3, jnp.where(is_first, 0.0, vec_square)),
            (5, jnp.sum(update * update)),
            (6, jnp.where(is_first, update_square, 0.0)),
            (7, jnp.where(is_first, 0.0, update_square)),
        ]
    )


def trunk_lamb(latent, weight_refs, head_refs, outs, sum_ref):
    rows = Rows(128, latent)
    weight = weight_refs[0][...]
    count = weight.shape[0]
    first, second, update = moments_of(weight, sum_ref[0:count], weight_refs[1][...], weight_refs[2][...])
    outs[1][...] = first
    outs[2][...] = second
    edges = [0, rows.enc_two, rows.dec_one, rows.dec_two, rows.gain, rows.end]
    row = lax.broadcasted_iota(jnp.int32, (count, 1), 0)
    weight_lines = jnp.sum(weight * weight, axis=1, keepdims=True)
    update_lines = jnp.sum(update * update, axis=1, keepdims=True)
    ratio = jnp.zeros((count, 1), f32)
    norms = []
    for index in range(5):
        chosen = (row >= edges[index]) & (row < edges[index + 1])
        weight_norm = jnp.sqrt(jnp.sum(jnp.where(chosen, weight_lines, 0.0), keepdims=True))
        update_norm = jnp.sqrt(jnp.sum(jnp.where(chosen, update_lines, 0.0), keepdims=True))
        ratio = jnp.where(chosen, learn_rate * (weight_norm / update_norm), ratio)
        norms.append((weight_norm, update_norm))
    outs[0][...] = weight - ratio * update
    size = 2 * latent
    head = head_refs[0][...]
    bias = jnp.broadcast_to(sum_ref[296 + size : 297 + size, :], (128, 128)).T[0:size, 0:1]
    grad_head = jnp.concatenate([sum_ref[296 : 296 + size, :], bias], axis=1)
    first, second, update = moments_of(head, grad_head, head_refs[1][...], head_refs[2][...])
    outs[4][...] = first
    outs[5][...] = second
    weight_norm = jnp.sqrt(jnp.sum(head * head, keepdims=True))
    update_norm = jnp.sqrt(jnp.sum(update * update, keepdims=True))
    outs[3][...] = head - learn_rate * (weight_norm / update_norm) * update
    return norms + [(weight_norm, update_norm)]


def final_kernel(latent, loss_scale, all_cells, *refs):
    part_refs, refs = refs[:COLUMNS], refs[COLUMNS:]
    dp, own_column, _ = place()
    enc_ref, enc_update_ref, dec_ref, dec_update_ref, vec_ref, vec_update_ref = refs[:6]
    trunk_refs, head_refs = refs[6:9], refs[9:12]
    loss_out, enc_out, enc_copy, dec_out, dec_copy, vec_out, norm_out = refs[12:19]
    trunk_outs = refs[19:25]
    sum_ref = refs[25]
    stats = part_refs[0][0:8]
    for ref in part_refs[1:]:
        stats = stats + ref[0:8]
    roots = jnp.sqrt(jnp.abs(stats[0:1]))

    def ratio(index):
        return learn_rate * (roots[:, index : index + 1] / roots[:, index + 4 : index + 5])

    enc_new = enc_ref[...] - ratio(0) * enc_update_ref[...]
    enc_out[...] = enc_new
    enc_copy[...] = enc_new.astype(bf16)
    dec_new = dec_ref[...] - ratio(1) * dec_update_ref[...]
    dec_out[...] = dec_new
    dec_copy[...] = dec_new.astype(bf16)
    vec_ratio = jnp.where(dp == 0, ratio(2), ratio(3))
    vec_out[...] = vec_ref[...] - vec_ratio * vec_update_ref[...]
    for j in range(COLUMNS):
        start = lax.rem(own_column + j, COLUMNS) * PIECE
        for part, half in ((0, dp), (1, 1 - dp)):
            at = pl.multiple_of(half * (COLUMNS * PIECE) + start, 8)
            sum_ref[pl.ds(at, PIECE), :] = part_refs[j][8 + part * PIECE : 8 + (part + 1) * PIECE, :]
    norms = trunk_lamb(latent, trunk_refs, head_refs, trunk_outs, sum_ref)
    norm_out[0:1, 0:4] = roots[:, 0:4]
    norm_out[1:2, 0:4] = roots[:, 4:8]
    for index, (weight_norm, update_norm) in enumerate(norms):
        norm_out[0:1, 4 + index : 5 + index] = weight_norm
        norm_out[1:2, 4 + index : 5 + index] = update_norm
    lane = lax.broadcasted_iota(jnp.int32, (1, 128), 1)
    loss_out[0] = jnp.sum(jnp.where(lane == 8, -stats[0:1], 0.0)) * loss_scale
    loss_out[1] = jnp.sum(jnp.where(lane == 9, stats[0:1], 0.0)) / all_cells


def on_device(
    cell_counts,
    cell_seeds,
    batch_ids,
    noise_draw,
    cell_factor,
    enc_weight,
    enc_first,
    enc_second,
    dec_weight,
    dec_first,
    dec_second,
    region_vecs,
    vec_first,
    vec_second,
    trunk_rows,
    trunk_first,
    trunk_second,
    head_rows,
    head_first,
    head_second,
):
    cells_here = cell_counts.shape[0]
    enc_weight, enc_first, enc_second = enc_weight.T, enc_first.T, enc_second.T
    head_across, head_first, head_second = head_rows.T, head_first.T, head_second.T
    width = enc_weight.shape[1]
    latent = head_rows.shape[1] // 2
    plane = lax.axis_size("plane")
    total = width * COLUMNS * plane
    all_cells = cells_here * lax.axis_size("dp")
    loss_scale = 1.0 / (all_cells * total)
    share = cells_here // COLUMNS
    own = share // plane
    groups = min(4, plane)
    each = plane // groups
    block = own * each
    regions = COLUMNS * width
    rows = Rows(128, latent)
    column = lax.axis_index("column")
    spot = lax.axis_index("plane")
    tile = jax.ShapeDtypeStruct((8, 128), f32)

    def over_dp(value):
        return lax.ppermute(value, "dp", [(0, 1), (1, 0)])

    def from_column(value, j):
        return lax.ppermute(value, "column", [(i, (i - j) % COLUMNS) for i in range(COLUMNS)])

    def to_column(value, j):
        return lax.ppermute(value, "column", [(i, (i + j) % COLUMNS) for i in range(COLUMNS)])

    def over_plane(value, k):
        return lax.ppermute(value, "plane", [(i, i ^ k) for i in range(plane)])

    def gather_column(value, after=None):
        blocks = []
        for j in range(COLUMNS):
            mine = value if j == 0 else from_column(value, j)
            if j and after is not None:
                mine, _ = lax.optimization_barrier((mine, after))
            blocks += [mine, over_dp(mine)]
        return blocks

    def gather_plane(value):
        blocks = [value] + [over_plane(value, k) for k in range(1, plane)]
        if each == 1:
            return blocks
        return [jnp.concatenate(blocks[g * each : (g + 1) * each], axis=0) for g in range(groups)]

    def scatter_group(values, g):
        received = []
        for e in range(each):
            k = g * each + e
            piece = values if each == 1 else values[e * own : (e + 1) * own]
            received.append(piece if k == 0 else over_plane(piece, k))
        return received

    def call(kernel, name, ins, outs, args, mib=16, scratch=(), grid=(), aliases={}):
        return pl.pallas_call(
            kernel,
            grid=grid,
            in_specs=ins,
            out_specs=tuple(spec for spec, _ in outs),
            out_shape=tuple(shape for _, shape in outs),
            scratch_shapes=list(scratch),
            input_output_aliases=aliases,
            compiler_params=params(mib),
            name=name,
        )(*args)

    def whole(shape, kind=f32):
        return (VMEM, jax.ShapeDtypeStruct(shape, kind))

    in_order = own % 128 != 0
    per_cell = [cell_counts, cell_seeds, cell_factor]
    if in_order:
        per_cell = [
            jnp.concatenate(
                [
                    lax.dynamic_slice_in_dim(x, (column * plane + (spot ^ k)) * own, own)
                    for k in range(plane)
                ]
            )
            for x in per_cell
        ]
    per_cell = [x.reshape(-1, 128) for x in per_cell]
    masks, factors = call(
        functools.partial(mask_kernel, total, width, plane, own, in_order),
        "masks",
        [pl.BlockSpec(x.shape, lambda i: (0, 0)) for x in per_cell],
        [
            (pl.BlockSpec((128, regions), lambda i: (i, 0)), jax.ShapeDtypeStruct((share, regions), bf16)),
            (pl.BlockSpec((share + 8, 128), lambda i: (0, 0)), jax.ShapeDtypeStruct((share + 8, 128), f32)),
        ],
        per_cell,
        scratch=[
            pltpu.VMEM((7, share // 128, 128), jnp.int32),
            pltpu.VMEM((share // 128, 128), f32),
        ],
        grid=(share // 128,),
    )

    enc_blocks = gather_column(enc_weight.astype(bf16), factors)
    ready, pre_parts = None, []
    for g in [*range(1, groups), 0]:
        early = pre_parts[: (groups - 2) * each] if g == 0 else []
        (partial,) = call(
            functools.partial(encode_kernel, width, g, own),
            "encode",
            [VMEM] * (1 + 2 * COLUMNS + len(early)),
            [whole((block, 128))],
            [masks, *enc_blocks, *early],
        )
        if g == 0:
            pre_parts = [partial] + pre_parts[len(early) :]
            if each > 1:
                pre_parts += scatter_group(partial, 0)[1:]
        else:
            ready = partial if ready is None else ready
            pre_parts += scatter_group(partial, g)

    dec_send = jnp.concatenate(
        [dec_weight.astype(bf16), region_vecs.astype(bf16), jnp.zeros((15, width), bf16)], axis=0
    )
    dec_send, _ = lax.optimization_barrier((dec_send, ready))
    dec_blocks = gather_column(dec_send)
    dec_pack, lines, small = call(
        functools.partial(pack_kernel, rows.gain),
        "pack",
        [VMEM] * (1 + 2 * COLUMNS),
        [
            whole((COLUMNS, 256, width), bf16),
            whole((COLUMNS, 32, width)),
            (SMEM, jax.ShapeDtypeStruct((1,), jnp.int32)),
        ],
        [trunk_rows, *dec_blocks],
    )

    at = (column * plane + spot) * own
    ids = lax.dynamic_slice_in_dim(batch_ids, at, own).reshape(1, own)
    noise = lax.dynamic_slice_in_dim(noise_draw.T, at, own, axis=1)
    head_wide = jnp.pad(head_rows, ((0, 7), (0, 128 - 2 * latent)))
    decoded_low, saved, loss_tile = call(
        functools.partial(forward_kernel, len(pre_parts), latent, own),
        "forward",
        [VMEM] * (5 + len(pre_parts)),
        [whole((own, 128), bf16), whole((10, own, 128)), (VMEM, tile)],
        [masks, ids, noise, trunk_rows, head_wide, *pre_parts],
    )

    low_groups = gather_plane(decoded_low)
    sums = []
    back_parts = []
    for g in [*range(1, groups), 0]:
        early = back_parts[: (groups - 2) * each] if g == 0 else []
        *sums, back, loss_tile = call(
            functools.partial(decode_kernel, loss_scale, g, len(early)),
            "decode",
            [SMEM] + [VMEM] * (7 + len(sums) + len(early)),
            [
                whole((COLUMNS, 72, width)),
                whole((COLUMNS, 72, width)),
                whole((block, 128)),
                (VMEM, tile),
            ],
            [small, low_groups[g], masks, factors, dec_pack, lines, saved, loss_tile, *sums, *early],
            scratch=[
                pltpu.VMEM((block, width), f32),
                pltpu.VMEM((block, width), bf16),
                pltpu.VMEM((block, 256), bf16),
                pltpu.VMEM((144, block), bf16),
            ],
            aliases={8: 0, 9: 1} if sums else {},
        )
        if g == 0:
            back_parts = [back] + back_parts[len(early) :]
            if each > 1:
                back_parts += scatter_group(back, 0)[1:]
        else:
            back_parts += scatter_group(back, g)

    def send_sums(mine, other, name):
        other = over_dp(other)
        blocks = call(
            sum_kernel,
            name,
            [VMEM] * 2,
            [whole((80, width), bf16)] * (COLUMNS - 1),
            [mine, other],
        )
        return [mine, other] + [to_column(blocks[j - 1], j) for j in range(1, COLUMNS)]

    dec_parts = send_sums(*sums, "dec_sum")

    pre_low, trunk_mine, trunk_other = call(
        functools.partial(backward_kernel, len(back_parts), latent, loss_scale),
        "backward",
        [VMEM] * (4 + len(back_parts)),
        [whole((own, 128), bf16), whole((COLUMNS, PIECE, 128)), whole((COLUMNS, PIECE, 128))],
        [masks, trunk_rows, head_wide, saved, *back_parts],
        scratch=[pltpu.VMEM((320, 128), f32)],
    )

    pre_groups = gather_plane(pre_low)
    enc_mine, enc_other, loss_tile = call(
        functools.partial(encode_back_kernel, groups),
        "encode_back",
        [VMEM] * (5 + groups),
        [whole((COLUMNS, 72, width)), whole((COLUMNS, 72, width)), (VMEM, tile)],
        [masks, lines, loss_tile, trunk_mine, trunk_other, *pre_groups],
        scratch=[pltpu.VMEM((144, share), bf16)],
    )
    enc_parts = send_sums(enc_mine, enc_other, "enc_sum")

    like = lambda *arrays: [whole(x.shape) for x in arrays]
    dec_first_new, dec_second_new, dec_update, vec_first_new, vec_second_new, vec_update, dec_stats = call(
        functools.partial(dec_lamb_kernel, loss_scale),
        "dec_lamb",
        [VMEM] * (6 + len(dec_parts)),
        like(*[dec_weight] * 3, *[region_vecs] * 3) + [(VMEM, tile)],
        [dec_weight, dec_first, dec_second, region_vecs, vec_first, vec_second, *dec_parts],
    )
    stat_tiles = [dec_stats, loss_tile]
    enc_first_new, enc_second_new, enc_update, last = call(
        enc_lamb_kernel,
        "enc_lamb",
        [VMEM] * (4 + COLUMNS + len(stat_tiles)),
        like(*[enc_weight] * 3) + [whole((8 + PIECE, 128))],
        [enc_weight, enc_first, enc_second, *enc_parts, *stat_tiles],
    )
    beside = over_dp(last)
    last = jnp.concatenate([last[0:8] + beside[0:8], last[8:], beside[8:]], axis=0)
    last = last + sum(over_plane(last, k) for k in range(1, plane))
    last_parts = [last] + [from_column(last, j) for j in range(1, COLUMNS)]
    (
        loss,
        enc_new,
        enc_copy,
        dec_new,
        dec_copy,
        vecs_new,
        norms,
        trunk_new,
        trunk_first_new,
        trunk_second_new,
        head_new,
        head_first_new,
        head_second_new,
    ) = call(
        functools.partial(final_kernel, latent, loss_scale, all_cells),
        "final",
        [VMEM] * (COLUMNS + 12),
        [
            (SMEM, jax.ShapeDtypeStruct((2,), f32)),
            whole(enc_weight.shape),
            whole(enc_weight.shape, bf16),
            whole(dec_weight.shape),
            whole(dec_weight.shape, bf16),
            whole(region_vecs.shape),
            whole((2, 10)),
            *like(*[trunk_rows] * 3, *[head_across] * 3),
        ],
        [
            *last_parts,
            enc_weight,
            enc_update,
            dec_weight,
            dec_update,
            region_vecs,
            vec_update,
            trunk_rows,
            trunk_first,
            trunk_second,
            head_across,
            head_first,
            head_second,
        ],
        scratch=[pltpu.VMEM((2 * COLUMNS * PIECE, 128), f32)],
    )
    return (
        loss,
        enc_new.T,
        enc_first_new.T,
        enc_second_new.T,
        enc_copy.T,
        dec_new,
        dec_first_new,
        dec_second_new,
        dec_copy,
        vecs_new,
        vec_first_new,
        vec_second_new,
        trunk_new,
        trunk_first_new,
        trunk_second_new,
        head_new.T,
        head_first_new.T,
        head_second_new.T,
        norms,
    )


def solution(mesh):
    regions = mesh.shape["region"]
    devices = mesh.devices.reshape(mesh.shape["dp"], COLUMNS, regions // COLUMNS)
    inner = Mesh(devices, ("dp", "column", "plane"))
    across = ("column", "plane")
    by_row, by_line = P(across, "dp"), P("dp", across)
    return jax.shard_map(
        on_device,
        mesh=inner,
        in_specs=(P("dp"), P("dp"), P("dp"), P("dp", None), P("dp"))
        + (by_row,) * 3
        + (by_line,) * 6
        + (P(),) * 6,
        out_specs=(P(),) + (by_row,) * 4 + (by_line,) * 7 + (P(),) * 7,
        check_vma=False,
    )
```

```python
import functools

import jax
import jax.numpy as jnp
from jax import lax
from jax.experimental import pallas as pl
from jax.experimental.pallas import tpu as pltpu
from jax.sharding import Mesh
from jax.sharding import PartitionSpec as P

BATCHES = 8
COLUMNS = 4
PIECE = 40
SAFE = 40.0
HOT, NOISE, LEFT, CENTRE, LOG_VAR, SCALE = range(4, 10)
LOG2_E = 1.4426950408889634
LN_2 = 0.6931471805599453

norm_eps = 1e-05
leak_slope = 0.01
decay_rate = 0.5
weight_decay = 0.01
learn_rate = 0.5
lamb_eps = 1e-12

f32 = jnp.float32
bf16 = jnp.bfloat16
VMEM = pl.BlockSpec(memory_space=pltpu.VMEM)
SMEM = pl.BlockSpec(memory_space=pltpu.SMEM)
MEGA = 1024 * 1024


def params(mib=16):
    return pltpu.CompilerParams(vmem_limit_bytes=mib * MEGA)


def place():
    return tuple(lax.axis_index(name) for name in ("dp", "column", "plane"))


def exact(left, right, contract=((1,), (0,))):
    return lax.dot_general(
        left, right, (contract, ((), ())), precision=lax.Precision.HIGHEST, preferred_element_type=f32
    )


def wide(left, right, contract=((1,), (0,))):
    return lax.dot_general(left, right, (contract, ((), ())), preferred_element_type=f32)


def remainder(values, divisor):
    guess = jnp.floor(values.astype(f32) * (1.0 / divisor)).astype(jnp.int32)
    rest = values - guess * divisor
    rest = jnp.where(rest < 0, rest + divisor, rest)
    return jnp.where(rest >= divisor, rest - divisor, rest)


def turns(values, total):
    whole = 2**32 // total
    part = (2**32 % total) / total
    return values * whole + (values.astype(f32) * part + 0.5).astype(jnp.int32)


def mask_kernel(total, width, plane, own, in_order, counts_ref, seeds_ref, factors_ref, *refs):
    mask_ref, factor_ref, table_ref, held_ref = refs
    step = pl.program_id(0)
    lines_here = table_ref.shape[1]

    @pl.when(step == 0)
    def _():
        _, column, spot = place()
        if in_order:
            counts, seeds, factors = counts_ref[...], seeds_ref[...], factors_ref[...]
        else:
            each = own // 128
            starts = [
                (column * plane + (spot ^ k)) * each + i for k in range(plane) for i in range(each)
            ]
            counts, seeds, factors = (
                jnp.concatenate([ref[pl.ds(at, 1), :] for at in starts], axis=0)
                for ref in (counts_ref, seeds_ref, factors_ref)
            )
        stride = 6 * remainder(seeds, total // 6) + 1
        low_end = jnp.int32(-(2**31))
        half = jnp.int32(2**31 // total)
        for j in range(COLUMNS):
            base = (lax.rem(column + j, COLUMNS) * plane + spot) * width
            upper = remainder(stride * (base // 256), total)
            start = remainder(upper * 256 + stride * (base % 256) + seeds, total)
            table_ref[j] = turns(start, total) + (low_end + half)
        table_ref[4] = turns(stride, total)
        table_ref[5] = turns(remainder(stride * 128, total), total)
        table_ref[6] = turns(counts, total) + low_end
        cell = lax.broadcasted_iota(jnp.int32, (lines_here, 128), 0) * 128
        cell = cell + lax.broadcasted_iota(jnp.int32, (lines_here, 128), 1)
        known = jnp.where(cell < own, counts.astype(f32) * jnp.log(factors), 0.0)
        row = lax.broadcasted_iota(jnp.int32, (8, 128), 0)
        known = jnp.where(row == 0, jnp.sum(known, axis=0, keepdims=True), 0.0)
        factor_ref[128 * lines_here : 128 * lines_here + 8, :] = known
        held_ref[...] = factors

    at = pl.ds(step, 1)
    rows = [table_ref[j, at, :] for j in range(7)]
    table = jnp.concatenate(rows + rows[:1], axis=0).T
    factor_ref[pl.ds(pl.multiple_of(step * 128, 128), 128), :] = jnp.broadcast_to(held_ref[at, :], (128, 128)).T
    for part in range(4):
        lines = slice(part * 32, part * 32 + 32)
        shape = (32, 128)
        lane = lax.broadcasted_iota(jnp.int32, shape, 1)
        span = jnp.broadcast_to(table[lines, 4:5], shape) * lane
        advance = jnp.broadcast_to(table[lines, 5:6], shape)
        limit = jnp.broadcast_to(table[lines, 6:7], shape)
        for column in range(COLUMNS):
            value = jnp.broadcast_to(table[lines, column : column + 1], shape) + span
            for group in range(width // 128):
                here = column * width + group * 128
                mask_ref[lines, here : here + 128] = jnp.where(value < limit, 1.0, 0.0).astype(bf16)
                value = value + advance


def encode_kernel(width, group, mask_ref, *refs):
    out_ref = refs[-1]
    cells = out_ref.shape[0]
    lines = slice(group * cells, (group + 1) * cells)
    total = None
    for column in range(COLUMNS):
        block = jnp.concatenate([refs[2 * column][...], refs[2 * column + 1][...]], axis=0)
        term = wide(mask_ref[lines, column * width : (column + 1) * width], block, ((1,), (1,)))
        total = term if total is None else total + term
    out_ref[...] = total


def add_kernel(first_ref, *refs):
    out_ref = refs[-1]
    total = first_ref[0 : out_ref.shape[0]]
    for ref in refs[:-1]:
        total = total + ref[...]
    out_ref[...] = total


def pack_kernel(gain_row, trunk_ref, *refs):
    weight_ref, line_ref, small_ref = refs[-3:]
    is_first = place()[0] == 0
    longest = largest = jnp.zeros((1, 1), f32)
    for column in range(COLUMNS):
        mine = refs[2 * column][...]
        other = refs[2 * column + 1][...]
        mine_line = mine[64:80].astype(f32)[0:1]
        other_line = other[64:80].astype(f32)[0:1]
        bias = jnp.where(is_first, mine_line, other_line)
        logit = jnp.where(is_first, other_line, mine_line)
        width = mine.shape[1]
        row = lax.broadcasted_iota(jnp.int32, (16, width), 0)
        weight_ref[column, 0:64] = mine[0:64]
        weight_ref[column, 64:128] = other[0:64]
        weight_ref[column, 128:144] = jnp.where(row == 0, bias, 0.0).astype(bf16)
        weight_ref[column, 144:256] = jnp.zeros((112, width), bf16)
        spread = jnp.exp(-jnp.abs(logit))
        chance = jnp.where(logit >= 0, 1.0, spread) / (1.0 + spread)
        logs = jnp.minimum(logit, 0.0) - jnp.log(1.0 + spread)
        line_ref[column, 0:16] = jnp.broadcast_to(chance, (16, width))
        line_ref[column, 16:32] = jnp.broadcast_to(logs, (16, width))
        one, two = mine[0:64].astype(f32), other[0:64].astype(f32)
        squares = jnp.sum(one * one + two * two, axis=0, keepdims=True)
        longest = jnp.maximum(longest, jnp.max(squares, axis=1, keepdims=True))
        largest = jnp.maximum(largest, jnp.max(jnp.abs(bias), axis=1, keepdims=True))
    gain = jnp.max(jnp.abs(trunk_ref[gain_row + 3 : gain_row + 4, :]), axis=1, keepdims=True)
    shift = trunk_ref[gain_row + 7 : gain_row + 8, :]
    reach = gain * (128.0**0.5) + jnp.sqrt(jnp.sum(shift * shift, axis=1, keepdims=True))
    bound = 1.02 * reach * jnp.sqrt(longest) + largest
    small_ref[0] = jnp.sum(jnp.where(bound < SAFE, 1, 0))


def normalize(values):
    centre = values - jnp.mean(values, axis=-1, keepdims=True)
    spread = jnp.mean(centre * centre, axis=-1, keepdims=True)
    scale = lax.rsqrt(spread + norm_eps)
    return centre * scale, scale


def leaky(values):
    return jnp.where(values >= 0, values, leak_slope * values)


def swap_halves(values, is_first):
    return jnp.where(is_first, values, pltpu.roll(values, 64, 1))


class Rows:
    def __init__(self, hidden, latent):
        self.enc_two = BATCHES
        self.dec_one = BATCHES + hidden
        self.dec_two = 2 * BATCHES + hidden + latent
        self.gain = 2 * BATCHES + 2 * hidden + latent
        self.shift = self.gain + 4
        self.end = self.gain + 8


def turned_rows(values, own):
    rows, spare = values.shape[0], -values.shape[1] % 128
    if spare:
        values = jnp.concatenate([values, jnp.zeros((rows, spare), f32)], axis=1)
    if rows == 1:
        full = jnp.broadcast_to(values, (128, values.shape[1]))
    else:
        full = jnp.concatenate([values, jnp.zeros((128 - rows, values.shape[1]), f32)], axis=0)
    return full.T[0:own]


def forward_kernel(parts, latent, own, in_order, plane, *refs):
    ids_ref, noise_ref, trunk_ref, head_ref, *refs = refs
    part_refs = refs[:parts]
    low_ref, saved_ref, stat_ref, table_ref = refs[-4:]
    dp, own_column, spot = place()
    is_first = dp == 0
    rows = Rows(128, latent)
    total = part_refs[0][0:own]
    for ref in part_refs[1:]:
        total = total + ref[...]
    total = swap_halves(total, is_first)
    lane = lax.broadcasted_iota(jnp.int32, total.shape, 1)
    if in_order:
        ids, noise = ids_ref[...], noise_ref[...]
    else:
        line = (own_column * plane + spot) * (own // 128)
        ids = jnp.concatenate([ids_ref[pl.ds(line + i, 1), :] for i in range(own // 128)], axis=1)
        noise = noise_ref[:, pl.ds(pl.multiple_of(line * 128, 128), own)]
    ids = turned_rows(ids.astype(f32), own).astype(jnp.int32)
    noise = turned_rows(noise, own)
    saved_ref[NOISE] = noise
    hot = jnp.where(lane == ids, 1.0, 0.0)
    saved_ref[HOT] = hot
    gains = trunk_ref[rows.gain : rows.gain + 4, :]
    shifts = trunk_ref[rows.shift : rows.shift + 4, :]

    def act(index, values):
        normal, scale = normalize(values)
        saved_ref[index] = normal
        return leaky(normal * gains[index : index + 1] + shifts[index : index + 1]), scale

    first, scale0 = act(0, total + exact(hot, trunk_ref[0:128, :]))
    second, scale1 = act(1, exact(first, trunk_ref[rows.enc_two : rows.enc_two + 128, :]))
    size = 2 * latent
    table_ref[...] = jnp.zeros_like(table_ref)
    table_ref[0, 0:size] = head_ref[:, 0:128]
    table_ref[1, 0:size] = jnp.broadcast_to(head_ref[:, 128:129], (size, 128))
    moments = exact(second, table_ref[0], ((1,), (1,))) + table_ref[1].T[0:1]
    inside = lane < latent
    centre = jnp.where(inside, moments, 0.0)
    log_var = jnp.where(inside, pltpu.roll(moments, 128 - latent, 1), 0.0)
    sample = centre + jnp.exp(0.5 * log_var) * noise
    left = sample + jnp.where(lane == ids + latent, 1.0, 0.0)
    third, scale2 = act(2, exact(left, trunk_ref[rows.dec_one : rows.dec_one + 128, :]))
    fourth, scale3 = act(3, exact(third, trunk_ref[rows.dec_two : rows.dec_two + 128, :]))
    low_ref[...] = swap_halves(fourth, is_first).astype(bf16)
    saved_ref[LEFT] = left
    saved_ref[CENTRE] = centre
    saved_ref[LOG_VAR] = log_var
    saved_ref[SCALE] = jnp.where(
        lane == 0, scale0, jnp.where(lane == 1, scale1, jnp.where(lane == 2, scale2, scale3))
    )
    diverge = 0.5 * jnp.sum(jnp.exp(log_var) + centre * centre - 1.0 - log_var)
    stat_ref[...] = stat_tile([(9, diverge)])


def decode_kernel(loss_scale, group, parts, small_ref, low_ref, mask_ref, factor_ref, weight_ref, line_ref, *refs):
    saved_ref, loss_in, *refs = refs
    has_sum = group != 1
    if has_sum:
        refs = refs[2:]
    part_refs, refs = refs[:parts], refs[parts:]
    mine_ref, other_ref, back_ref, loss_ref, logit_ref, grad_ref, left_ref, turned_ref = refs
    cells, width = grad_ref.shape
    half = cells // 2
    halves = (slice(0, half), slice(half, cells))
    blocks = width // 128
    first_row = group * cells
    zero = jnp.zeros((8, 128), f32)

    low = low_ref[...]
    left_ref[:, 0:128] = low
    lane = lax.broadcasted_iota(jnp.int32, (cells, 128), 1)
    left_ref[:, 128:256] = jnp.where(lane == 0, 1.0, 0.0).astype(bf16)
    turned_ref[0:128, :] = low.astype(f32).T.astype(bf16)
    row = lax.broadcasted_iota(jnp.int32, (16, cells), 0)
    turned_ref[128:144, :] = jnp.where(row == 0, 1.0, 0.0).astype(bf16)
    back_ref[...] = jnp.zeros_like(back_ref)
    grad_ref[halves[1], :] = jnp.zeros((half, width), bf16)
    if not has_sum:
        mine_ref[...] = jnp.zeros_like(mine_ref)
        other_ref[...] = jnp.zeros_like(other_ref)

    def logits_of(lines, column):
        logit_ref[lines, :] = wide(left_ref[lines, :], weight_ref[column])

    def add_sums(lines, column):
        product = wide(turned_ref[:, lines], grad_ref[lines, :])
        tail = product[128:136]
        mine_ref[column, 0:72] += jnp.concatenate([product[0:64], tail], axis=0)
        other_ref[column, 0:72] += jnp.concatenate([product[64:128], tail], axis=0)

    def add_back(lines, column):
        back_ref[lines, :] += wide(grad_ref[lines, :], weight_ref[column, 0:128], ((1,), (1,)))

    def add_odds(column, odds):
        line = jnp.sum(jnp.concatenate(odds, axis=1), axis=0, keepdims=True)
        place = lax.broadcasted_iota(jnp.int32, (8, width), 0)
        line = jnp.where(place == 1, line * loss_scale, 0.0)
        mine_ref[column, 64:72] += line
        other_ref[column, 64:72] += line

    def finish(loss_sum):
        if group == 0:
            loss_sum = loss_sum + factor_ref[-8:, :]
        loss_ref[...] = loss_in[...] + stat_tile([(8, jnp.sum(loss_sum))])
        for ref in part_refs:
            back_ref[0 : ref.shape[0]] += ref[...]

    def quick(column, at, odds, loss_sum):
        factor = factor_ref[first_row + at : first_row + at + 16, :]
        held = None
        for block in range(blocks):
            lanes = slice(block * 128, block * 128 + 128)
            far = slice(column * width + block * 128, column * width + block * 128 + 128)
            ratio = jnp.exp2(logit_ref[at : at + 16, lanes] * -LOG2_E)
            whole = 1.0 + ratio
            chance = factor * line_ref[column, 0:16, lanes]
            opened = mask_ref[first_row + at : first_row + at + 16, far].astype(f32) > 0.5
            rest = jnp.where(opened, 1.0, whole - chance)
            inverse = pl.reciprocal(whole * rest)
            part = jnp.where(opened, -1.0, chance) * inverse
            grad_ref[at : at + 16, lanes] = ((ratio * part) * loss_scale).astype(bf16)
            odds[block] = odds[block] + part[0:8] + part[8:16]
            likely = rest * (rest * inverse)
            held = likely if held is None else held * likely
            if block % 2 == 1 or block == blocks - 1:
                logs = jnp.log2(held)
                loss_sum = loss_sum + logs[0:8] + logs[8:16]
                held = None
        return loss_sum

    @pl.when(small_ref[0] == 1)
    def _():
        logits_of(halves[0], 0)
        loss_sum = zero
        for column in range(COLUMNS):
            odds = [zero] * blocks
            for at in range(0, half, 16):
                loss_sum = quick(column, at, odds, loss_sum)
            logits_of(halves[1], column)
            if column > 0:
                add_sums(halves[1], column - 1)
                add_back(halves[1], column - 1)
            for at in range(half, cells, 16):
                loss_sum = quick(column, at, odds, loss_sum)
            if column + 1 < COLUMNS:
                logits_of(halves[0], column + 1)
            add_sums(halves[0], column)
            add_back(halves[0], column)
            add_odds(column, odds)
        add_sums(halves[1], COLUMNS - 1)
        add_back(halves[1], COLUMNS - 1)
        finish(loss_sum * LN_2)

    def steady(column, loss_sum):
        logits_of(slice(None), column)

        def step(index, carried):
            loss_sum, *odds = carried
            here = pl.multiple_of(index * 16, 16)
            at = pl.ds(here, 16)
            far_at = pl.ds(pl.multiple_of(first_row + here, 16), 16)
            factor = factor_ref[far_at, :]
            top = bottom = held = None
            for block in range(blocks):
                lanes = slice(block * 128, block * 128 + 128)
                far = pl.ds(pl.multiple_of(column * width + block * 128, 128), 128)
                logits = logit_ref[at, lanes]
                spread = jnp.exp(-jnp.abs(logits))
                whole = 1.0 + spread
                positive = logits >= 0
                chance = factor * line_ref[column, 0:16, lanes]
                taken = chance * jnp.where(positive, 1.0, spread)
                opened = mask_ref[far_at, far].astype(f32) > 0.5
                rest = jnp.where(opened, 1.0, whole - taken)
                inverse = pl.reciprocal(whole * rest)
                upper = jnp.where(opened, jnp.where(positive, -spread, -1.0), spread * chance)
                slope = upper * inverse
                grad_ref[at, lanes] = (slope * loss_scale).astype(bf16)
                part = jnp.where(opened, -1.0, taken * whole * inverse) - slope
                odds[block] = odds[block] + part[0:8] + part[8:16]
                likely = jnp.where(opened, jnp.minimum(logits, 0.0), 0.0)
                held = likely if held is None else held + likely
                top = rest if top is None else top * rest
                bottom = whole if bottom is None else bottom * whole
            held = held + (jnp.log(top) - jnp.log(bottom))
            return (loss_sum + held[0:8] + held[8:16], *odds)

        loss_sum, *odds = lax.fori_loop(0, cells // 16, step, (loss_sum,) + (zero,) * blocks)
        add_sums(slice(None), column)
        add_back(slice(None), column)
        add_odds(column, odds)
        return loss_sum

    @pl.when(small_ref[0] != 1)
    def _():
        finish(lax.fori_loop(0, COLUMNS, steady, zero))


def backward_kernel(parts, latent, loss_scale, _, trunk_ref, head_ref, saved_ref, *refs):
    part_refs = refs[:parts]
    low_ref, mine_ref, other_ref, sum_ref, table_ref = refs[parts:]
    table_ref[...] = jnp.zeros_like(table_ref)
    table_ref[0 : 2 * latent] = head_ref[:, 0:128]
    dp, own_column, _ = place()
    is_first = dp == 0
    own = low_ref.shape[0]
    rows = Rows(128, latent)
    total = part_refs[0][0:own]
    for ref in part_refs[1:]:
        total = total + ref[...]
    total = swap_halves(total, is_first)
    lane = lax.broadcasted_iota(jnp.int32, total.shape, 1)
    gains = trunk_ref[rows.gain : rows.gain + 4, :]
    shifts = trunk_ref[rows.shift : rows.shift + 4, :]
    sum_ref[...] = jnp.zeros_like(sum_ref)
    rows_in, rows_out = ((0,), (0,)), ((1,), (1,))

    def output(index):
        return leaky(saved_ref[index] * gains[index : index + 1] + shifts[index : index + 1])

    def pull(index, grad):
        normal = saved_ref[index]
        gain = gains[index : index + 1]
        before = normal * gain + shifts[index : index + 1]
        grad = jnp.where(before >= 0, grad, leak_slope * grad)
        at = rows.gain + index
        sum_ref[at : at + 1, :] = jnp.sum(grad * normal, axis=0, keepdims=True)
        at = rows.shift + index
        sum_ref[at : at + 1, :] = jnp.sum(grad, axis=0, keepdims=True)
        grad = grad * gain
        plain = jnp.mean(grad, axis=-1, keepdims=True)
        along = jnp.mean(grad * normal, axis=-1, keepdims=True)
        return (grad - plain - normal * along) * saved_ref[SCALE][:, index : index + 1]

    grad = pull(3, total)
    sum_ref[rows.dec_two : rows.dec_two + 128, :] = exact(output(2), grad, rows_in)
    grad = pull(2, exact(grad, trunk_ref[rows.dec_two : rows.dec_two + 128, :], rows_out))
    one = exact(saved_ref[LEFT], grad, rows_in)
    sum_ref[rows.dec_one : rows.dec_two, :] = one[0 : rows.dec_two - rows.dec_one]
    grad = exact(grad, trunk_ref[rows.dec_one : rows.dec_one + 128, :], rows_out)
    inside = lane < latent
    grad = jnp.where(inside, grad, 0.0)
    centre, log_var = saved_ref[CENTRE], saved_ref[LOG_VAR]
    grad_centre = grad + loss_scale * centre
    grad_log = grad * 0.5 * jnp.exp(0.5 * log_var) * saved_ref[NOISE] + (0.5 * loss_scale) * (
        jnp.exp(log_var) - 1.0
    )
    both = jnp.where(inside, grad_centre, pltpu.roll(jnp.where(inside, grad_log, 0.0), latent, 1))
    head = exact(both, output(1), rows_in)
    sum_ref[296 : 296 + 24, :] = head[0:24]
    sum_ref[296 + 2 * latent : 297 + 2 * latent, :] = jnp.sum(both, axis=0, keepdims=True)
    grad = pull(1, exact(both, table_ref[...]))
    sum_ref[rows.enc_two : rows.enc_two + 128, :] = exact(output(0), grad, rows_in)
    grad = pull(0, exact(grad, trunk_ref[rows.enc_two : rows.enc_two + 128, :], rows_out))
    low = grad.astype(bf16)
    hot = saved_ref[HOT].astype(bf16)
    sum_ref[0:BATCHES, :] = wide(hot, low, rows_in)[0:BATCHES]
    low_ref[...] = swap_halves(low.astype(f32), is_first).astype(bf16)
    for j in range(COLUMNS):
        start = lax.rem(own_column + j, COLUMNS) * PIECE
        for ref, half in ((mine_ref, dp), (other_ref, 1 - dp)):
            at = pl.multiple_of(half * (COLUMNS * PIECE) + start, 8)
            ref[j] = sum_ref[pl.ds(at, PIECE), :]


def encode_back_kernel(groups, mask_ref, line_ref, loss_in, trunk_mine_ref, trunk_other_ref, *refs):
    low_refs = refs[:groups]
    mine_ref, other_ref, known_ref, turned_ref = refs[groups:]
    cells = low_refs[0].shape[0]
    share = turned_ref.shape[1]
    width = mine_ref.shape[2]
    for group in range(groups):
        turned_ref[0:128, group * cells : (group + 1) * cells] = (
            low_refs[group][...].astype(f32).T.astype(bf16)
        )
    row = lax.broadcasted_iota(jnp.int32, (16, share), 0)
    turned_ref[128:144, :] = jnp.where(row == 0, 1.0, 0.0).astype(bf16)
    known = jnp.zeros((8, width), f32)
    for column in range(COLUMNS):
        product = wide(turned_ref[...], mask_ref[:, column * width : (column + 1) * width])
        mine_ref[column, 0:64] = product[0:64]
        other_ref[column, 0:64] = product[64:128]
        known = known + product[128:136] * line_ref[column, 16:24, :]
        for ref, trunk_ref in ((mine_ref, trunk_mine_ref), (other_ref, trunk_other_ref)):
            ref[column, 64:72] = jnp.zeros((8, width), f32)
            for part in range(PIECE // 8):
                lanes = slice(part * 128, part * 128 + 128)
                ref[column, 64:72, lanes] = trunk_ref[column, part * 8 : part * 8 + 8, :]
    known_ref[...] = loss_in[...] + stat_tile([(8, jnp.sum(known))])


def power_for(values):
    return 13.0 - jnp.floor(jnp.log2(jnp.maximum(values, 1e-30)))


def fold_tail(tail):
    row = lax.broadcasted_iota(jnp.int32, tail.shape, 0)
    lane = lax.broadcasted_iota(jnp.int32, tail.shape, 1)
    moved = pltpu.roll(pltpu.roll(tail, 2, 0), 128, 1)
    free = tail.shape[1] - 128
    moved = jnp.where((row == 2) | (row == 3), jnp.where(lane < 128, moved, 0.0), 0.0)
    return jnp.where((row < 2) & (lane < free), tail, moved)


def sum_kernel(folded, mine_ref, other_ref, *refs):
    width = mine_ref.shape[2]
    for j in range(1, COLUMNS):
        out_ref = refs[j - COLUMNS]
        total = mine_ref[j] + other_ref[j]
        main, tail = total[0:64], total[64:72]
        if folded:
            tail = fold_tail(tail)
        power = power_for(jnp.max(jnp.abs(main), axis=0, keepdims=True))
        out_ref[0:64] = jnp.round(main * jnp.exp2(power)).astype(jnp.int32).astype(jnp.int16)
        most = jnp.max(jnp.max(jnp.abs(tail), axis=0, keepdims=True), axis=1, keepdims=True)
        tail_power = power_for(most)
        tail = tail * jnp.exp2(tail_power)
        high = jnp.round(tail)
        low = jnp.round((tail - high) * 16384.0)
        row = lax.broadcasted_iota(jnp.int32, (8, 128), 0)
        note = jnp.where(row == 6, tail_power, 0.0)
        for i in range(width // 128):
            note = jnp.where(row == i, power[:, i * 128 : i * 128 + 128], note)
        high = jnp.concatenate([high[:, : width - 128], note], axis=1)
        out_ref[64:80] = jnp.concatenate([high, low], axis=0).astype(jnp.int32).astype(jnp.int16)


def received(ref):
    width = ref.shape[1]
    ends = ref[64:80].astype(jnp.int32).astype(f32)
    note = ends[0:8, width - 128 :]
    power = jnp.concatenate([note[i : i + 1] for i in range(width // 128)], axis=1)
    main = ref[0:64].astype(jnp.int32).astype(f32) * jnp.exp2(-power)
    tail = (ends[0:8] + ends[8:16] * (1.0 / 16384.0)) * jnp.exp2(-note[6:7, 0:1])
    return main, tail


def stat_tile(pairs):
    lane = lax.broadcasted_iota(jnp.int32, (8, 128), 1)
    row = lax.broadcasted_iota(jnp.int32, (8, 128), 0)
    tile = jnp.zeros((8, 128), f32)
    for index, value in pairs:
        tile = jnp.where(lane == index, value, tile)
    return jnp.where(row == 0, tile, 0.0)


def moments_of(weight, grad, first, second):
    first_new = decay_rate * first + (1.0 - decay_rate) * grad
    second_new = decay_rate * second + (1.0 - decay_rate) * grad * grad
    update = first_new / (jnp.sqrt(second_new) + lamb_eps) + weight_decay * weight
    return first_new, second_new, update


def enc_lamb_kernel(*refs):
    weight_ref, first_ref, second_ref, mine_ref, other_ref, *part_refs = refs[: 4 + COLUMNS]
    stat_refs = refs[4 + COLUMNS : -4]
    first_out, second_out, update_out, tile_out = refs[-4:]
    grad = mine_ref[0] + other_ref[0]
    tail = grad[64:72]
    grad = grad[0:64]
    for ref in part_refs:
        main, extra = received(ref)
        grad, tail = grad + main, tail + extra
    weight = weight_ref[...]
    first, second, update = moments_of(weight, grad, first_ref[...], second_ref[...])
    first_out[...] = first
    second_out[...] = second
    update_out[...] = update
    others = sum(ref[...] for ref in stat_refs)
    stats = stat_tile(
        [
            (0, jnp.sum(weight * weight)),
            (4, jnp.sum(update * update)),
        ]
    )
    tile_out[0:8] = stats + others
    for part in range(PIECE // 8):
        tile_out[8 + part * 8 : 16 + part * 8] = tail[:, part * 128 : part * 128 + 128]


def dec_lamb_kernel(loss_scale, *refs):
    weight_ref, first_ref, second_ref, vec_ref, vec_first_ref, vec_second_ref, mine_ref, other_ref = refs[:8]
    part_refs, refs = refs[8 : 7 + COLUMNS], refs[-7:]
    first_out, second_out, update_out, vec_first_out, vec_second_out, vec_update_out, stat_out = refs
    grad = mine_ref[0] + other_ref[0]
    tail = fold_tail(grad[64:72])
    grad = grad[0:64]
    for ref in part_refs:
        main, extra = received(ref)
        grad, tail = grad + main, tail + extra
    free = grad.shape[1] - 128
    tail = jnp.concatenate([tail[0:2, :free], tail[2:4, 0:128]], axis=1)
    weight = weight_ref[...]
    first, second, update = moments_of(weight, grad, first_ref[...], second_ref[...])
    first_out[...] = first
    second_out[...] = second
    update_out[...] = update
    is_first = place()[0] == 0
    vec = vec_ref[...]
    low = vec.astype(bf16).astype(f32)
    keep = 1.0 / (1.0 + jnp.exp(low))
    line = tail[0:1]
    line = jnp.where(is_first, line, keep * (tail[1:2] + line))
    vec_one, vec_two, vec_update = moments_of(vec, line, vec_first_ref[...], vec_second_ref[...])
    vec_first_out[...] = vec_one
    vec_second_out[...] = vec_two
    vec_update_out[...] = vec_update
    vec_square = jnp.sum(vec * vec)
    update_square = jnp.sum(vec_update * vec_update)
    stat_out[...] = stat_tile(
        [
            (1, jnp.sum(weight * weight)),
            (2, jnp.where(is_first, vec_square, 0.0)),
            (3, jnp.where(is_first, 0.0, vec_square)),
            (5, jnp.sum(update * update)),
            (6, jnp.where(is_first, update_square, 0.0)),
            (7, jnp.where(is_first, 0.0, update_square)),
        ]
    )


def trunk_lamb(latent, weight_refs, head_refs, outs, sum_ref):
    rows = Rows(128, latent)
    weight = weight_refs[0][...]
    count = weight.shape[0]
    first, second, update = moments_of(weight, sum_ref[0:count], weight_refs[1][...], weight_refs[2][...])
    outs[1][...] = first
    outs[2][...] = second
    edges = [0, rows.enc_two, rows.dec_one, rows.dec_two, rows.gain, rows.end]
    row = lax.broadcasted_iota(jnp.int32, (count, 1), 0)
    weight_lines = jnp.sum(weight * weight, axis=1, keepdims=True)
    update_lines = jnp.sum(update * update, axis=1, keepdims=True)
    ratio = jnp.zeros((count, 1), f32)
    norms = []
    for index in range(5):
        chosen = (row >= edges[index]) & (row < edges[index + 1])
        weight_norm = jnp.sqrt(jnp.sum(jnp.where(chosen, weight_lines, 0.0), keepdims=True))
        update_norm = jnp.sqrt(jnp.sum(jnp.where(chosen, update_lines, 0.0), keepdims=True))
        ratio = jnp.where(chosen, learn_rate * (weight_norm / update_norm), ratio)
        norms.append((weight_norm, update_norm))
    outs[0][...] = weight - ratio * update
    size = 2 * latent
    head = head_refs[0][...]
    bias = jnp.broadcast_to(sum_ref[296 + size : 297 + size, :], (128, 128)).T[0:size, 0:1]
    grad_head = jnp.concatenate([sum_ref[296 : 296 + size, :], bias], axis=1)
    first, second, update = moments_of(head, grad_head, head_refs[1][...], head_refs[2][...])
    outs[4][...] = first
    outs[5][...] = second
    weight_norm = jnp.sqrt(jnp.sum(head * head, keepdims=True))
    update_norm = jnp.sqrt(jnp.sum(update * update, keepdims=True))
    outs[3][...] = head - learn_rate * (weight_norm / update_norm) * update
    return norms + [(weight_norm, update_norm)]


def final_kernel(latent, loss_scale, all_cells, *refs):
    part_refs, refs = refs[:2], refs[2:]
    dp, own_column, _ = place()
    enc_ref, enc_update_ref, dec_ref, dec_update_ref, vec_ref, vec_update_ref = refs[:6]
    trunk_refs, head_refs = refs[6:9], refs[9:12]
    loss_out, enc_out, enc_copy, dec_out, dec_copy, vec_out, norm_out = refs[12:19]
    trunk_outs = refs[19:25]
    sum_ref = refs[25]
    stats = part_refs[0][0:8]
    for ref in part_refs[1:]:
        stats = stats + ref[0:8]
    roots = jnp.sqrt(jnp.abs(stats[0:1]))

    def ratio(index):
        return learn_rate * (roots[:, index : index + 1] / roots[:, index + 4 : index + 5])

    enc_new = enc_ref[...] - ratio(0) * enc_update_ref[...]
    enc_out[...] = enc_new
    enc_copy[...] = enc_new.astype(bf16)
    dec_new = dec_ref[...] - ratio(1) * dec_update_ref[...]
    dec_out[...] = dec_new
    dec_copy[...] = dec_new.astype(bf16)
    vec_ratio = jnp.where(dp == 0, ratio(2), ratio(3))
    vec_out[...] = vec_ref[...] - vec_ratio * vec_update_ref[...]
    for j in range(COLUMNS):
        start = lax.rem(own_column + j, COLUMNS) * PIECE
        for part, half in ((0, dp), (1, 1 - dp)):
            at = pl.multiple_of(half * (COLUMNS * PIECE) + start, 8)
            sum_ref[pl.ds(at, PIECE), :] = part_refs[part][8 + j * PIECE : 8 + (j + 1) * PIECE, :]
    norms = trunk_lamb(latent, trunk_refs, head_refs, trunk_outs, sum_ref)
    norm_out[0:1, 0:4] = roots[:, 0:4]
    norm_out[1:2, 0:4] = roots[:, 4:8]
    for index, (weight_norm, update_norm) in enumerate(norms):
        norm_out[0:1, 4 + index : 5 + index] = weight_norm
        norm_out[1:2, 4 + index : 5 + index] = update_norm
    lane = lax.broadcasted_iota(jnp.int32, (1, 128), 1)
    loss_out[0] = jnp.sum(jnp.where(lane == 8, -stats[0:1], 0.0)) * loss_scale
    loss_out[1] = jnp.sum(jnp.where(lane == 9, stats[0:1], 0.0)) / all_cells


def on_device(
    cell_counts,
    cell_seeds,
    batch_ids,
    noise_draw,
    cell_factor,
    enc_weight,
    enc_first,
    enc_second,
    dec_weight,
    dec_first,
    dec_second,
    region_vecs,
    vec_first,
    vec_second,
    trunk_rows,
    trunk_first,
    trunk_second,
    head_rows,
    head_first,
    head_second,
):
    cells_here = cell_counts.shape[0]
    enc_weight, enc_first, enc_second = enc_weight.T, enc_first.T, enc_second.T
    head_across, head_first, head_second = head_rows.T, head_first.T, head_second.T
    width = enc_weight.shape[1]
    latent = head_rows.shape[1] // 2
    plane = lax.axis_size("plane")
    total = width * COLUMNS * plane
    all_cells = cells_here * lax.axis_size("dp")
    loss_scale = 1.0 / (all_cells * total)
    share = cells_here // COLUMNS
    own = share // plane
    groups = min(4, plane)
    each = plane // groups
    block = own * each
    regions = COLUMNS * width
    rows = Rows(128, latent)
    column = lax.axis_index("column")
    spot = lax.axis_index("plane")
    tile = jax.ShapeDtypeStruct((8, 128), f32)

    def over_dp(value):
        return lax.ppermute(value, "dp", [(0, 1), (1, 0)])

    def from_column(value, j):
        return lax.ppermute(value, "column", [(i, (i - j) % COLUMNS) for i in range(COLUMNS)])

    def to_column(value, j):
        return lax.ppermute(value, "column", [(i, (i + j) % COLUMNS) for i in range(COLUMNS)])

    def over_plane(value, k):
        return lax.ppermute(value, "plane", [(i, i ^ k) for i in range(plane)])

    def gather_column(value, after=None):
        blocks = []
        for j in range(COLUMNS):
            mine = value if j == 0 else from_column(value, j)
            if j and after is not None:
                mine, _ = lax.optimization_barrier((mine, after))
            blocks += [mine, over_dp(mine)]
        return blocks

    def gather_plane(value):
        blocks = [value] + [over_plane(value, k) for k in range(1, plane)]
        if each == 1:
            return blocks
        return [jnp.concatenate(blocks[g * each : (g + 1) * each], axis=0) for g in range(groups)]

    def scatter_group(values, g):
        received = []
        for e in range(each):
            k = g * each + e
            piece = values if each == 1 else values[e * own : (e + 1) * own]
            received.append(piece if k == 0 else over_plane(piece, k))
        return received

    def call(kernel, name, ins, outs, args, mib=16, scratch=(), grid=(), aliases={}):
        return pl.pallas_call(
            kernel,
            grid=grid,
            in_specs=ins,
            out_specs=tuple(spec for spec, _ in outs),
            out_shape=tuple(shape for _, shape in outs),
            scratch_shapes=list(scratch),
            input_output_aliases=aliases,
            compiler_params=params(mib),
            name=name,
        )(*args)

    def whole(shape, kind=f32):
        return (VMEM, jax.ShapeDtypeStruct(shape, kind))

    in_order = own % 128 != 0
    per_cell = [cell_counts, cell_seeds, cell_factor]
    if in_order:
        per_cell = [
            jnp.concatenate(
                [
                    lax.dynamic_slice_in_dim(x, (column * plane + (spot ^ k)) * own, own)
                    for k in range(plane)
                ]
            )
            for x in per_cell
        ]
    per_cell = [x.reshape(-1, 128) for x in per_cell]
    batch_lines, noise = batch_ids.reshape(-1, 128), noise_draw.T
    if in_order:
        at = (column * plane + spot) * own
        batch_lines = lax.dynamic_slice_in_dim(batch_ids, at, own).reshape(1, own)
        noise = lax.dynamic_slice_in_dim(noise, at, own, axis=1)
    masks, factors = call(
        functools.partial(mask_kernel, total, width, plane, own, in_order),
        "masks",
        [pl.BlockSpec(x.shape, lambda i: (0, 0)) for x in per_cell],
        [
            (pl.BlockSpec((128, regions), lambda i: (i, 0)), jax.ShapeDtypeStruct((share, regions), bf16)),
            (pl.BlockSpec((share + 8, 128), lambda i: (0, 0)), jax.ShapeDtypeStruct((share + 8, 128), f32)),
        ],
        per_cell,
        scratch=[
            pltpu.VMEM((7, share // 128, 128), jnp.int32),
            pltpu.VMEM((share // 128, 128), f32),
        ],
        grid=(share // 128,),
    )

    enc_blocks = gather_column(enc_weight.astype(bf16), factors)
    partials = {}
    early, late = [], []
    for g in [*range(1, groups), 0]:
        (partials[g],) = call(
            functools.partial(encode_kernel, width, g),
            "encode",
            [VMEM] * (1 + 2 * COLUMNS),
            [whole((block, 128))],
            [masks, *enc_blocks],
        )
        if g:
            (late if g == 3 else early).extend(scatter_group(partials[g], g))
        elif each > 1:
            late += scatter_group(partials[0], 0)[1:]
    (partial,) = call(
        add_kernel, "add", [VMEM] * (1 + len(early)), [whole((own, 128))], [partials[0], *early]
    )
    pre_parts = [partial, *late]

    dec_send = jnp.concatenate(
        [dec_weight.astype(bf16), region_vecs.astype(bf16), jnp.zeros((15, width), bf16)], axis=0
    )
    dec_send, _ = lax.optimization_barrier((dec_send, partials[groups - 1]))
    dec_blocks = gather_column(dec_send)
    dec_pack, lines, small = call(
        functools.partial(pack_kernel, rows.gain),
        "pack",
        [VMEM] * (1 + 2 * COLUMNS),
        [
            whole((COLUMNS, 256, width), bf16),
            whole((COLUMNS, 32, width)),
            (SMEM, jax.ShapeDtypeStruct((1,), jnp.int32)),
        ],
        [trunk_rows, *dec_blocks],
    )

    decoded_low, saved, loss_tile = call(
        functools.partial(forward_kernel, len(pre_parts), latent, own, in_order, plane),
        "forward",
        [VMEM] * (4 + len(pre_parts) + 2),
        [whole((own, 128), bf16), whole((10, own, 128)), (VMEM, tile)],
        [batch_lines, noise, trunk_rows, head_across, *pre_parts, masks, lines],
        scratch=[pltpu.VMEM((2, 128, 128), f32)],
    )

    low_groups = gather_plane(decoded_low)
    sums = []
    back_parts = []
    for g in [*range(1, groups), 0]:
        early = back_parts[: (groups - 2) * each] if g == 0 else []
        *sums, back, loss_tile = call(
            functools.partial(decode_kernel, loss_scale, g, len(early)),
            "decode",
            [SMEM] + [VMEM] * (7 + len(sums) + len(early)),
            [
                whole((COLUMNS, 72, width)),
                whole((COLUMNS, 72, width)),
                whole((block, 128)),
                (VMEM, tile),
            ],
            [small, low_groups[g], masks, factors, dec_pack, lines, saved, loss_tile, *sums, *early],
            scratch=[
                pltpu.VMEM((block, width), f32),
                pltpu.VMEM((block, width), bf16),
                pltpu.VMEM((block, 256), bf16),
                pltpu.VMEM((144, block), bf16),
            ],
            aliases={8: 0, 9: 1} if sums else {},
        )
        if g == 0:
            back_parts = [back] + back_parts[len(early) :]
            if each > 1:
                back_parts += scatter_group(back, 0)[1:]
        else:
            back_parts += scatter_group(back, g)

    def send_sums(mine, other, name, after=()):
        other = over_dp(other)
        blocks = call(
            functools.partial(sum_kernel, name == "dec_sum"),
            name,
            [VMEM] * (2 + len(after)),
            [whole((80, width), jnp.int16)] * (COLUMNS - 1),
            [mine, other, *after],
        )
        return [mine, other] + [to_column(blocks[j - 1], j) for j in (2, 1, 3)]

    dec_parts = send_sums(*sums, "dec_sum")

    pre_low, trunk_mine, trunk_other = call(
        functools.partial(backward_kernel, len(back_parts), latent, loss_scale),
        "backward",
        [VMEM] * (4 + len(back_parts)),
        [whole((own, 128), bf16), whole((COLUMNS, PIECE, 128)), whole((COLUMNS, PIECE, 128))],
        [masks, trunk_rows, head_across, saved, *back_parts],
        scratch=[pltpu.VMEM((320, 128), f32), pltpu.VMEM((128, 128), f32)],
    )

    pre_groups = gather_plane(pre_low)
    enc_mine, enc_other, loss_tile = call(
        functools.partial(encode_back_kernel, groups),
        "encode_back",
        [VMEM] * (5 + groups),
        [whole((COLUMNS, 72, width)), whole((COLUMNS, 72, width)), (VMEM, tile)],
        [masks, lines, loss_tile, trunk_mine, trunk_other, *pre_groups],
        scratch=[pltpu.VMEM((144, share), bf16)],
    )
    like = lambda *arrays: [whole(x.shape) for x in arrays]
    dec_first_new, dec_second_new, dec_update, vec_first_new, vec_second_new, vec_update, dec_stats = call(
        functools.partial(dec_lamb_kernel, loss_scale),
        "dec_lamb",
        [VMEM] * (6 + len(dec_parts)),
        like(*[dec_weight] * 3, *[region_vecs] * 3) + [(VMEM, tile)],
        [dec_weight, dec_first, dec_second, region_vecs, vec_first, vec_second, *dec_parts],
    )
    enc_parts = send_sums(enc_mine, enc_other, "enc_sum")
    stat_tiles = [dec_stats, loss_tile]
    enc_first_new, enc_second_new, enc_update, last = call(
        enc_lamb_kernel,
        "enc_lamb",
        [VMEM] * (4 + COLUMNS + len(stat_tiles)),
        like(*[enc_weight] * 3) + [whole((8 + PIECE, 128))],
        [enc_weight, enc_first, enc_second, *enc_parts, *stat_tiles],
    )
    last = last + sum(over_plane(last, k) for k in range(1, plane))
    lasts = [last] + [from_column(last, j) for j in range(1, COLUMNS)]
    last = jnp.concatenate([sum(x[0:8] for x in lasts), *(x[8:] for x in lasts)], axis=0)
    last_parts = [last, over_dp(last)]
    (
        loss,
        enc_new,
        enc_copy,
        dec_new,
        dec_copy,
        vecs_new,
        norms,
        trunk_new,
        trunk_first_new,
        trunk_second_new,
        head_new,
        head_first_new,
        head_second_new,
    ) = call(
        functools.partial(final_kernel, latent, loss_scale, all_cells),
        "final",
        [VMEM] * (len(last_parts) + 12),
        [
            (SMEM, jax.ShapeDtypeStruct((2,), f32)),
            whole(enc_weight.shape),
            whole(enc_weight.shape, bf16),
            whole(dec_weight.shape),
            whole(dec_weight.shape, bf16),
            whole(region_vecs.shape),
            whole((2, 10)),
            *like(*[trunk_rows] * 3, *[head_across] * 3),
        ],
        [
            *last_parts,
            enc_weight,
            enc_update,
            dec_weight,
            dec_update,
            region_vecs,
            vec_update,
            trunk_rows,
            trunk_first,
            trunk_second,
            head_across,
            head_first,
            head_second,
        ],
        scratch=[pltpu.VMEM((2 * COLUMNS * PIECE, 128), f32)],
    )
    return (
        loss,
        enc_new.T,
        enc_first_new.T,
        enc_second_new.T,
        enc_copy.T,
        dec_new,
        dec_first_new,
        dec_second_new,
        dec_copy,
        vecs_new,
        vec_first_new,
        vec_second_new,
        trunk_new,
        trunk_first_new,
        trunk_second_new,
        head_new.T,
        head_first_new.T,
        head_second_new.T,
        norms,
    )


def solution(mesh):
    regions = mesh.shape["region"]
    devices = mesh.devices.reshape(mesh.shape["dp"], COLUMNS, regions // COLUMNS)
    inner = Mesh(devices, ("dp", "column", "plane"))
    across = ("column", "plane")
    by_row, by_line = P(across, "dp"), P("dp", across)
    return jax.shard_map(
        on_device,
        mesh=inner,
        in_specs=(P("dp"), P("dp"), P("dp"), P("dp", None), P("dp"))
        + (by_row,) * 3
        + (by_line,) * 6
        + (P(),) * 6,
        out_specs=(P(),) + (by_row,) * 4 + (by_line,) * 7 + (P(),) * 7,
        check_vma=False,
    )
```

```python
import functools

import jax
import jax.numpy as jnp
from jax import lax
from jax.experimental import pallas as pl
from jax.experimental.pallas import tpu as pltpu
from jax.sharding import Mesh
from jax.sharding import PartitionSpec as P

BATCHES = 8
COLUMNS = 4
HEIGHT = 512
PIECE = 40
SAFE = 40.0
HOT, NOISE, LEFT, CENTRE, LOG_VAR, SCALE = range(4, 10)
LOG2_E = 1.4426950408889634
LN_2 = 0.6931471805599453

norm_eps = 1e-05
leak_slope = 0.01
decay_rate = 0.5
weight_decay = 0.01
learn_rate = 0.5
lamb_eps = 1e-12

f32 = jnp.float32
bf16 = jnp.bfloat16
VMEM = pl.BlockSpec(memory_space=pltpu.VMEM)
SMEM = pl.BlockSpec(memory_space=pltpu.SMEM)
MEGA = 1024 * 1024


def params(mib=16):
    return pltpu.CompilerParams(vmem_limit_bytes=mib * MEGA)


def place():
    return tuple(lax.axis_index(name) for name in ("dp", "column", "plane"))


def exact(left, right, contract=((1,), (0,))):
    return lax.dot_general(
        left, right, (contract, ((), ())), precision=lax.Precision.HIGHEST, preferred_element_type=f32
    )


def wide(left, right, contract=((1,), (0,))):
    return lax.dot_general(left, right, (contract, ((), ())), preferred_element_type=f32)


def remainder(values, divisor):
    guess = jnp.floor(values.astype(f32) * (1.0 / divisor)).astype(jnp.int32)
    rest = values - guess * divisor
    rest = jnp.where(rest < 0, rest + divisor, rest)
    return jnp.where(rest >= divisor, rest - divisor, rest)


def turns(values, total):
    whole = 2**32 // total
    part = (2**32 % total) / total
    return values * whole + (values.astype(f32) * part + 0.5).astype(jnp.int32)


def mask_kernel(total, width, plane, own, in_order, counts_ref, seeds_ref, factors_ref, *refs):
    mask_ref, factor_ref, table_ref, held_ref = refs
    step = pl.program_id(0)
    lines_here = table_ref.shape[1]

    @pl.when(step == 0)
    def _():
        _, column, spot = place()
        if in_order:
            counts, seeds, factors = counts_ref[...], seeds_ref[...], factors_ref[...]
        else:
            each = own // 128
            starts = [
                (column * plane + (spot ^ k)) * each + i for k in range(plane) for i in range(each)
            ]
            counts, seeds, factors = (
                jnp.concatenate([ref[pl.ds(at, 1), :] for at in starts], axis=0)
                for ref in (counts_ref, seeds_ref, factors_ref)
            )
        stride = 6 * remainder(seeds, total // 6) + 1
        low_end = jnp.int32(-(2**31))
        half = jnp.int32(2**31 // total)
        for j in range(COLUMNS):
            base = (lax.rem(column + j, COLUMNS) * plane + spot) * width
            upper = remainder(stride * (base // 256), total)
            start = remainder(upper * 256 + stride * (base % 256) + seeds, total)
            table_ref[j] = turns(start, total) + (low_end + half)
        table_ref[4] = turns(stride, total)
        table_ref[5] = turns(remainder(stride * 128, total), total)
        table_ref[6] = turns(counts, total) + low_end
        cell = lax.broadcasted_iota(jnp.int32, (lines_here, 128), 0) * 128
        cell = cell + lax.broadcasted_iota(jnp.int32, (lines_here, 128), 1)
        known = jnp.where(cell < own, counts.astype(f32) * jnp.log(factors), 0.0)
        row = lax.broadcasted_iota(jnp.int32, (8, 128), 0)
        known = jnp.where(row == 0, jnp.sum(known, axis=0, keepdims=True), 0.0)
        factor_ref[128 * lines_here : 128 * lines_here + 8, :] = known
        held_ref[...] = factors

    height = mask_ref.shape[0] // 128
    for sub in range(height):
        line = step * height + sub
        at = pl.ds(line, 1)
        rows = [table_ref[j, at, :] for j in range(7)]
        table = jnp.concatenate(rows + rows[:1], axis=0).T
        factors = jnp.broadcast_to(held_ref[at, :], (8, 128)).T[:, 0:1]
        factor_ref[pl.ds(pl.multiple_of(line * 128, 128), 128), :] = jnp.broadcast_to(factors, (128, 128))
        for part in range(4):
            cells = slice(part * 32, part * 32 + 32)
            lines = slice(sub * 128 + part * 32, sub * 128 + part * 32 + 32)
            shape = (32, 128)
            lane = lax.broadcasted_iota(jnp.int32, shape, 1)
            span = jnp.broadcast_to(table[cells, 4:5], shape) * lane
            advance = jnp.broadcast_to(table[cells, 5:6], shape)
            limit = jnp.broadcast_to(table[cells, 6:7], shape)
            for column in range(COLUMNS):
                value = jnp.broadcast_to(table[cells, column : column + 1], shape) + span
                for group in range(width // 128):
                    here = column * width + group * 128
                    mask_ref[lines, here : here + 128] = jnp.where(value < limit, 1.0, 0.0).astype(bf16)
                    value = value + advance


def encode_kernel(width, group, mask_ref, *refs):
    out_ref = refs[-1]
    cells = out_ref.shape[0]
    lines = slice(group * cells, (group + 1) * cells)
    total = None
    for column in range(COLUMNS):
        block = jnp.concatenate([refs[2 * column][...], refs[2 * column + 1][...]], axis=0)
        term = wide(mask_ref[lines, column * width : (column + 1) * width], block, ((1,), (1,)))
        total = term if total is None else total + term
    out_ref[...] = total


def add_kernel(first_ref, *refs):
    out_ref = refs[-1]
    total = first_ref[0 : out_ref.shape[0]]
    for ref in refs[:-1]:
        total = total + ref[...]
    out_ref[...] = total


def pack_kernel(gain_row, trunk_ref, *refs):
    weight_ref, line_ref, small_ref = refs[-3:]
    is_first = place()[0] == 0
    longest = largest = jnp.zeros((1, 1), f32)
    for column in range(COLUMNS):
        mine = refs[2 * column][...]
        other = refs[2 * column + 1][...]
        mine_line = mine[64:80].astype(f32)[0:1]
        other_line = other[64:80].astype(f32)[0:1]
        bias = jnp.where(is_first, mine_line, other_line)
        logit = jnp.where(is_first, other_line, mine_line)
        width = mine.shape[1]
        row = lax.broadcasted_iota(jnp.int32, (16, width), 0)
        weight_ref[column, 0:64] = mine[0:64]
        weight_ref[column, 64:128] = other[0:64]
        weight_ref[column, 128:144] = jnp.where(row == 0, bias, 0.0).astype(bf16)
        weight_ref[column, 144:256] = jnp.zeros((112, width), bf16)
        spread = jnp.exp(-jnp.abs(logit))
        chance = jnp.where(logit >= 0, 1.0, spread) / (1.0 + spread)
        logs = jnp.minimum(logit, 0.0) - jnp.log(1.0 + spread)
        line_ref[column, 0:16] = jnp.broadcast_to(chance, (16, width))
        line_ref[column, 16:32] = jnp.broadcast_to(logs, (16, width))
        one, two = mine[0:64].astype(f32), other[0:64].astype(f32)
        squares = jnp.sum(one * one + two * two, axis=0, keepdims=True)
        longest = jnp.maximum(longest, jnp.max(squares, axis=1, keepdims=True))
        largest = jnp.maximum(largest, jnp.max(jnp.abs(bias), axis=1, keepdims=True))
    gain = jnp.max(jnp.abs(trunk_ref[gain_row + 3 : gain_row + 4, :]), axis=1, keepdims=True)
    shift = trunk_ref[gain_row + 7 : gain_row + 8, :]
    reach = gain * (128.0**0.5) + jnp.sqrt(jnp.sum(shift * shift, axis=1, keepdims=True))
    bound = 1.02 * reach * jnp.sqrt(longest) + largest
    small_ref[0] = jnp.sum(jnp.where(bound < SAFE, 1, 0))


def normalize(values):
    centre = values - jnp.mean(values, axis=-1, keepdims=True)
    spread = jnp.mean(centre * centre, axis=-1, keepdims=True)
    scale = lax.rsqrt(spread + norm_eps)
    return centre * scale, scale


def leaky(values):
    return jnp.where(values >= 0, values, leak_slope * values)


def swap_halves(values, is_first):
    return jnp.where(is_first, values, pltpu.roll(values, 64, 1))


class Rows:
    def __init__(self, hidden, latent):
        self.enc_two = BATCHES
        self.dec_one = BATCHES + hidden
        self.dec_two = 2 * BATCHES + hidden + latent
        self.gain = 2 * BATCHES + 2 * hidden + latent
        self.shift = self.gain + 4
        self.end = self.gain + 8


def turned_rows(values, own):
    rows, spare = values.shape[0], -values.shape[1] % 128
    if spare:
        values = jnp.concatenate([values, jnp.zeros((rows, spare), f32)], axis=1)
    if rows == 1:
        full = jnp.broadcast_to(values, (128, values.shape[1]))
    else:
        full = jnp.concatenate([values, jnp.zeros((128 - rows, values.shape[1]), f32)], axis=0)
    return full.T[0:own]


def forward_kernel(parts, latent, own, in_order, plane, *refs):
    ids_ref, noise_ref, trunk_ref, head_ref, *refs = refs
    part_refs = refs[:parts]
    low_ref, saved_ref, stat_ref, table_ref = refs[-4:]
    dp, own_column, spot = place()
    is_first = dp == 0
    rows = Rows(128, latent)
    total = part_refs[0][0:own]
    for ref in part_refs[1:]:
        total = total + ref[...]
    total = swap_halves(total, is_first)
    lane = lax.broadcasted_iota(jnp.int32, total.shape, 1)
    if in_order:
        ids, noise = ids_ref[...], noise_ref[...]
    else:
        line = (own_column * plane + spot) * (own // 128)
        ids = jnp.concatenate([ids_ref[pl.ds(line + i, 1), :] for i in range(own // 128)], axis=1)
        noise = noise_ref[:, pl.ds(pl.multiple_of(line * 128, 128), own)]
    ids = turned_rows(ids.astype(f32), own).astype(jnp.int32)
    noise = turned_rows(noise, own)
    saved_ref[NOISE] = noise
    hot = jnp.where(lane == ids, 1.0, 0.0)
    saved_ref[HOT] = hot
    gains = trunk_ref[rows.gain : rows.gain + 4, :]
    shifts = trunk_ref[rows.shift : rows.shift + 4, :]

    def act(index, values):
        normal, scale = normalize(values)
        saved_ref[index] = normal
        return leaky(normal * gains[index : index + 1] + shifts[index : index + 1]), scale

    first, scale0 = act(0, total + exact(hot, trunk_ref[0:128, :]))
    second, scale1 = act(1, exact(first, trunk_ref[rows.enc_two : rows.enc_two + 128, :]))
    size = 2 * latent
    table_ref[...] = jnp.zeros_like(table_ref)
    table_ref[0, 0:size] = head_ref[:, 0:128]
    table_ref[1, 0:size] = jnp.broadcast_to(head_ref[:, 128:129], (size, 128))
    moments = exact(second, table_ref[0], ((1,), (1,))) + table_ref[1].T[0:1]
    inside = lane < latent
    centre = jnp.where(inside, moments, 0.0)
    log_var = jnp.where(inside, pltpu.roll(moments, 128 - latent, 1), 0.0)
    sample = centre + jnp.exp(0.5 * log_var) * noise
    left = sample + jnp.where(lane == ids + latent, 1.0, 0.0)
    third, scale2 = act(2, exact(left, trunk_ref[rows.dec_one : rows.dec_one + 128, :]))
    fourth, scale3 = act(3, exact(third, trunk_ref[rows.dec_two : rows.dec_two + 128, :]))
    low_ref[...] = swap_halves(fourth, is_first).astype(bf16)
    saved_ref[LEFT] = left
    saved_ref[CENTRE] = centre
    saved_ref[LOG_VAR] = log_var
    saved_ref[SCALE] = jnp.where(
        lane == 0, scale0, jnp.where(lane == 1, scale1, jnp.where(lane == 2, scale2, scale3))
    )
    diverge = 0.5 * jnp.sum(jnp.exp(log_var) + centre * centre - 1.0 - log_var)
    stat_ref[...] = stat_tile([(9, diverge)])


def decode_kernel(loss_scale, group, parts, small_ref, low_ref, mask_ref, factor_ref, weight_ref, line_ref, *refs):
    saved_ref, loss_in, *refs = refs
    has_sum = group != 1
    if has_sum:
        refs = refs[2:]
    part_refs, refs = refs[:parts], refs[parts:]
    mine_ref, other_ref, back_ref, loss_ref, logit_ref, grad_ref, left_ref, turned_ref = refs
    cells, width = grad_ref.shape
    half = cells // 2
    halves = (slice(0, half), slice(half, cells))
    blocks = width // 128
    first_row = group * cells
    zero = jnp.zeros((8, 128), f32)

    low = low_ref[...]
    left_ref[:, 0:128] = low
    lane = lax.broadcasted_iota(jnp.int32, (cells, 128), 1)
    left_ref[:, 128:256] = jnp.where(lane == 0, 1.0, 0.0).astype(bf16)
    turned_ref[0:128, :] = low.astype(f32).T.astype(bf16)
    row = lax.broadcasted_iota(jnp.int32, (16, cells), 0)
    turned_ref[128:144, :] = jnp.where(row == 0, 1.0, 0.0).astype(bf16)
    back_ref[...] = jnp.zeros_like(back_ref)
    grad_ref[halves[1], :] = jnp.zeros((half, width), bf16)
    if not has_sum:
        mine_ref[...] = jnp.zeros_like(mine_ref)
        other_ref[...] = jnp.zeros_like(other_ref)

    def logits_of(lines, column):
        logit_ref[lines, :] = wide(left_ref[lines, :], weight_ref[column])

    def add_sums(lines, column):
        product = wide(turned_ref[:, lines], grad_ref[lines, :])
        tail = product[128:136]
        mine_ref[column, 0:72] += jnp.concatenate([product[0:64], tail], axis=0)
        other_ref[column, 0:72] += jnp.concatenate([product[64:128], tail], axis=0)

    def add_back(lines, column):
        back_ref[lines, :] += wide(grad_ref[lines, :], weight_ref[column, 0:128], ((1,), (1,)))

    def add_odds(column, odds):
        line = jnp.sum(jnp.concatenate(odds, axis=1), axis=0, keepdims=True)
        place = lax.broadcasted_iota(jnp.int32, (8, width), 0)
        line = jnp.where(place == 1, line * loss_scale, 0.0)
        mine_ref[column, 64:72] += line
        other_ref[column, 64:72] += line

    def finish(loss_sum):
        if group == 0:
            loss_sum = loss_sum + factor_ref[-8:, :]
        loss_ref[...] = loss_in[...] + stat_tile([(8, jnp.sum(loss_sum))])
        for ref in part_refs:
            back_ref[0 : ref.shape[0]] += ref[...]

    def quick(column, at, odds, loss_sum):
        factor = factor_ref[first_row + at : first_row + at + 16, :]
        held = None
        for block in range(blocks):
            lanes = slice(block * 128, block * 128 + 128)
            far = slice(column * width + block * 128, column * width + block * 128 + 128)
            ratio = jnp.exp2(logit_ref[at : at + 16, lanes] * -LOG2_E)
            whole = 1.0 + ratio
            chance = factor * line_ref[column, 0:16, lanes]
            opened = mask_ref[first_row + at : first_row + at + 16, far].astype(f32) > 0.5
            rest = jnp.where(opened, 1.0, whole - chance)
            inverse = pl.reciprocal(whole * rest)
            part = jnp.where(opened, -1.0, chance) * inverse
            grad_ref[at : at + 16, lanes] = ((ratio * part) * loss_scale).astype(bf16)
            odds[block] = odds[block] + part[0:8] + part[8:16]
            likely = rest * (rest * inverse)
            held = likely if held is None else held * likely
            if block % 2 == 1 or block == blocks - 1:
                logs = jnp.log2(held)
                loss_sum = loss_sum + logs[0:8] + logs[8:16]
                held = None
        return loss_sum

    @pl.when(small_ref[0] == 1)
    def _():
        logits_of(halves[0], 0)
        loss_sum = zero
        for column in range(COLUMNS):
            odds = [zero] * blocks
            for at in range(0, half, 16):
                loss_sum = quick(column, at, odds, loss_sum)
            logits_of(halves[1], column)
            if column > 0:
                add_sums(halves[1], column - 1)
                add_back(halves[1], column - 1)
            for at in range(half, cells, 16):
                loss_sum = quick(column, at, odds, loss_sum)
            if column + 1 < COLUMNS:
                logits_of(halves[0], column + 1)
            add_sums(halves[0], column)
            add_back(halves[0], column)
            add_odds(column, odds)
        add_sums(halves[1], COLUMNS - 1)
        add_back(halves[1], COLUMNS - 1)
        finish(loss_sum * LN_2)

    def steady(column, loss_sum):
        logits_of(slice(None), column)

        def step(index, carried):
            loss_sum, *odds = carried
            here = pl.multiple_of(index * 16, 16)
            at = pl.ds(here, 16)
            far_at = pl.ds(pl.multiple_of(first_row + here, 16), 16)
            factor = factor_ref[far_at, :]
            top = bottom = held = None
            for block in range(blocks):
                lanes = slice(block * 128, block * 128 + 128)
                far = pl.ds(pl.multiple_of(column * width + block * 128, 128), 128)
                logits = logit_ref[at, lanes]
                spread = jnp.exp(-jnp.abs(logits))
                whole = 1.0 + spread
                positive = logits >= 0
                chance = factor * line_ref[column, 0:16, lanes]
                taken = chance * jnp.where(positive, 1.0, spread)
                opened = mask_ref[far_at, far].astype(f32) > 0.5
                rest = jnp.where(opened, 1.0, whole - taken)
                inverse = pl.reciprocal(whole * rest)
                upper = jnp.where(opened, jnp.where(positive, -spread, -1.0), spread * chance)
                slope = upper * inverse
                grad_ref[at, lanes] = (slope * loss_scale).astype(bf16)
                part = jnp.where(opened, -1.0, taken * whole * inverse) - slope
                odds[block] = odds[block] + part[0:8] + part[8:16]
                likely = jnp.where(opened, jnp.minimum(logits, 0.0), 0.0)
                held = likely if held is None else held + likely
                top = rest if top is None else top * rest
                bottom = whole if bottom is None else bottom * whole
            held = held + (jnp.log(top) - jnp.log(bottom))
            return (loss_sum + held[0:8] + held[8:16], *odds)

        loss_sum, *odds = lax.fori_loop(0, cells // 16, step, (loss_sum,) + (zero,) * blocks)
        add_sums(slice(None), column)
        add_back(slice(None), column)
        add_odds(column, odds)
        return loss_sum

    @pl.when(small_ref[0] != 1)
    def _():
        finish(lax.fori_loop(0, COLUMNS, steady, zero))


def backward_kernel(parts, latent, loss_scale, _, trunk_ref, head_ref, saved_ref, *refs):
    part_refs = refs[:parts]
    low_ref, mine_ref, other_ref, sum_ref, table_ref = refs[parts:]
    table_ref[...] = jnp.zeros_like(table_ref)
    table_ref[0 : 2 * latent] = head_ref[:, 0:128]
    dp, own_column, _ = place()
    is_first = dp == 0
    own = low_ref.shape[0]
    rows = Rows(128, latent)
    total = part_refs[0][0:own]
    for ref in part_refs[1:]:
        total = total + ref[...]
    total = swap_halves(total, is_first)
    lane = lax.broadcasted_iota(jnp.int32, total.shape, 1)
    gains = trunk_ref[rows.gain : rows.gain + 4, :]
    shifts = trunk_ref[rows.shift : rows.shift + 4, :]
    sum_ref[...] = jnp.zeros_like(sum_ref)
    rows_in, rows_out = ((0,), (0,)), ((1,), (1,))

    def output(index):
        return leaky(saved_ref[index] * gains[index : index + 1] + shifts[index : index + 1])

    def pull(index, grad):
        normal = saved_ref[index]
        gain = gains[index : index + 1]
        before = normal * gain + shifts[index : index + 1]
        grad = jnp.where(before >= 0, grad, leak_slope * grad)
        at = rows.gain + index
        sum_ref[at : at + 1, :] = jnp.sum(grad * normal, axis=0, keepdims=True)
        at = rows.shift + index
        sum_ref[at : at + 1, :] = jnp.sum(grad, axis=0, keepdims=True)
        grad = grad * gain
        plain = jnp.mean(grad, axis=-1, keepdims=True)
        along = jnp.mean(grad * normal, axis=-1, keepdims=True)
        return (grad - plain - normal * along) * saved_ref[SCALE][:, index : index + 1]

    grad = pull(3, total)
    sum_ref[rows.dec_two : rows.dec_two + 128, :] = exact(output(2), grad, rows_in)
    grad = pull(2, exact(grad, trunk_ref[rows.dec_two : rows.dec_two + 128, :], rows_out))
    one = exact(saved_ref[LEFT], grad, rows_in)
    sum_ref[rows.dec_one : rows.dec_two, :] = one[0 : rows.dec_two - rows.dec_one]
    grad = exact(grad, trunk_ref[rows.dec_one : rows.dec_one + 128, :], rows_out)
    inside = lane < latent
    grad = jnp.where(inside, grad, 0.0)
    centre, log_var = saved_ref[CENTRE], saved_ref[LOG_VAR]
    grad_centre = grad + loss_scale * centre
    grad_log = grad * 0.5 * jnp.exp(0.5 * log_var) * saved_ref[NOISE] + (0.5 * loss_scale) * (
        jnp.exp(log_var) - 1.0
    )
    both = jnp.where(inside, grad_centre, pltpu.roll(jnp.where(inside, grad_log, 0.0), latent, 1))
    head = exact(both, output(1), rows_in)
    sum_ref[296 : 296 + 24, :] = head[0:24]
    sum_ref[296 + 2 * latent : 297 + 2 * latent, :] = jnp.sum(both, axis=0, keepdims=True)
    grad = pull(1, exact(both, table_ref[...]))
    sum_ref[rows.enc_two : rows.enc_two + 128, :] = exact(output(0), grad, rows_in)
    grad = pull(0, exact(grad, trunk_ref[rows.enc_two : rows.enc_two + 128, :], rows_out))
    low = grad.astype(bf16)
    hot = saved_ref[HOT].astype(bf16)
    sum_ref[0:BATCHES, :] = wide(hot, low, rows_in)[0:BATCHES]
    low_ref[...] = swap_halves(low.astype(f32), is_first).astype(bf16)
    for j in range(COLUMNS):
        start = lax.rem(own_column + j, COLUMNS) * PIECE
        for ref, half in ((mine_ref, dp), (other_ref, 1 - dp)):
            at = pl.multiple_of(half * (COLUMNS * PIECE) + start, 8)
            ref[j] = sum_ref[pl.ds(at, PIECE), :]


def encode_back_kernel(groups, mask_ref, line_ref, loss_in, trunk_mine_ref, trunk_other_ref, *refs):
    low_refs = refs[:groups]
    mine_ref, other_ref, known_ref, turned_ref = refs[groups:]
    cells = low_refs[0].shape[0]
    share = turned_ref.shape[1]
    width = mine_ref.shape[2]
    for group in range(groups):
        turned_ref[0:128, group * cells : (group + 1) * cells] = (
            low_refs[group][...].astype(f32).T.astype(bf16)
        )
    row = lax.broadcasted_iota(jnp.int32, (16, share), 0)
    turned_ref[128:144, :] = jnp.where(row == 0, 1.0, 0.0).astype(bf16)
    known = jnp.zeros((8, width), f32)
    for column in range(COLUMNS):
        product = wide(turned_ref[...], mask_ref[:, column * width : (column + 1) * width])
        mine_ref[column, 0:64] = product[0:64]
        other_ref[column, 0:64] = product[64:128]
        known = known + product[128:136] * line_ref[column, 16:24, :]
        for ref, trunk_ref in ((mine_ref, trunk_mine_ref), (other_ref, trunk_other_ref)):
            ref[column, 64:72] = jnp.zeros((8, width), f32)
            for part in range(PIECE // 8):
                lanes = slice(part * 128, part * 128 + 128)
                ref[column, 64:72, lanes] = trunk_ref[column, part * 8 : part * 8 + 8, :]
    known_ref[...] = loss_in[...] + stat_tile([(8, jnp.sum(known))])


def power_for(values):
    return 13.0 - jnp.floor(jnp.log2(jnp.maximum(values, 1e-30)))


def fold_tail(tail):
    row = lax.broadcasted_iota(jnp.int32, tail.shape, 0)
    lane = lax.broadcasted_iota(jnp.int32, tail.shape, 1)
    moved = pltpu.roll(pltpu.roll(tail, 2, 0), 128, 1)
    free = tail.shape[1] - 128
    moved = jnp.where((row == 2) | (row == 3), jnp.where(lane < 128, moved, 0.0), 0.0)
    return jnp.where((row < 2) & (lane < free), tail, moved)


def sum_kernel(folded, mine_ref, other_ref, *refs):
    width = mine_ref.shape[2]
    for j in range(1, COLUMNS):
        out_ref = refs[j - COLUMNS]
        total = mine_ref[j] + other_ref[j]
        main, tail = total[0:64], total[64:72]
        if folded:
            tail = fold_tail(tail)
        power = power_for(jnp.max(jnp.abs(main), axis=0, keepdims=True))
        out_ref[0:64] = jnp.round(main * jnp.exp2(power)).astype(jnp.int32).astype(jnp.int16)
        most = jnp.max(jnp.max(jnp.abs(tail), axis=0, keepdims=True), axis=1, keepdims=True)
        tail_power = power_for(most)
        tail = tail * jnp.exp2(tail_power)
        high = jnp.round(tail)
        low = jnp.round((tail - high) * 16384.0)
        row = lax.broadcasted_iota(jnp.int32, (8, 128), 0)
        note = jnp.where(row == 6, tail_power, 0.0)
        for i in range(width // 128):
            note = jnp.where(row == i, power[:, i * 128 : i * 128 + 128], note)
        high = jnp.concatenate([high[:, : width - 128], note], axis=1)
        out_ref[64:80] = jnp.concatenate([high, low], axis=0).astype(jnp.int32).astype(jnp.int16)


def received(ref):
    width = ref.shape[1]
    ends = ref[64:80].astype(jnp.int32).astype(f32)
    note = ends[0:8, width - 128 :]
    power = jnp.concatenate([note[i : i + 1] for i in range(width // 128)], axis=1)
    main = ref[0:64].astype(jnp.int32).astype(f32) * jnp.exp2(-power)
    tail = (ends[0:8] + ends[8:16] * (1.0 / 16384.0)) * jnp.exp2(-note[6:7, 0:1])
    return main, tail


def stat_tile(pairs):
    lane = lax.broadcasted_iota(jnp.int32, (8, 128), 1)
    row = lax.broadcasted_iota(jnp.int32, (8, 128), 0)
    tile = jnp.zeros((8, 128), f32)
    for index, value in pairs:
        tile = jnp.where(lane == index, value, tile)
    return jnp.where(row == 0, tile, 0.0)


def moments_of(weight, grad, first, second):
    first_new = decay_rate * first + (1.0 - decay_rate) * grad
    second_new = decay_rate * second + (1.0 - decay_rate) * grad * grad
    update = first_new / (jnp.sqrt(second_new) + lamb_eps) + weight_decay * weight
    return first_new, second_new, update


def enc_lamb_kernel(*refs):
    weight_ref, first_ref, second_ref, mine_ref, other_ref, *part_refs = refs[: 4 + COLUMNS]
    stat_refs = refs[4 + COLUMNS : -4]
    first_out, second_out, update_out, tile_out = refs[-4:]
    grad = mine_ref[0] + other_ref[0]
    tail = grad[64:72]
    grad = grad[0:64]
    for ref in part_refs:
        main, extra = received(ref)
        grad, tail = grad + main, tail + extra
    weight = weight_ref[...]
    first, second, update = moments_of(weight, grad, first_ref[...], second_ref[...])
    first_out[...] = first
    second_out[...] = second
    update_out[...] = update
    others = sum(ref[...] for ref in stat_refs)
    stats = stat_tile(
        [
            (0, jnp.sum(weight * weight)),
            (4, jnp.sum(update * update)),
        ]
    )
    tile_out[0:8] = stats + others
    for part in range(PIECE // 8):
        tile_out[8 + part * 8 : 16 + part * 8] = tail[:, part * 128 : part * 128 + 128]


def dec_lamb_kernel(loss_scale, *refs):
    weight_ref, first_ref, second_ref, vec_ref, vec_first_ref, vec_second_ref, mine_ref, other_ref = refs[:8]
    part_refs, refs = refs[8 : 7 + COLUMNS], refs[-7:]
    first_out, second_out, update_out, vec_first_out, vec_second_out, vec_update_out, stat_out = refs
    grad = mine_ref[0] + other_ref[0]
    tail = fold_tail(grad[64:72])
    grad = grad[0:64]
    for ref in part_refs:
        main, extra = received(ref)
        grad, tail = grad + main, tail + extra
    free = grad.shape[1] - 128
    tail = jnp.concatenate([tail[0:2, :free], tail[2:4, 0:128]], axis=1)
    weight = weight_ref[...]
    first, second, update = moments_of(weight, grad, first_ref[...], second_ref[...])
    first_out[...] = first
    second_out[...] = second
    update_out[...] = update
    is_first = place()[0] == 0
    vec = vec_ref[...]
    low = vec.astype(bf16).astype(f32)
    keep = 1.0 / (1.0 + jnp.exp(low))
    line = tail[0:1]
    line = jnp.where(is_first, line, keep * (tail[1:2] + line))
    vec_one, vec_two, vec_update = moments_of(vec, line, vec_first_ref[...], vec_second_ref[...])
    vec_first_out[...] = vec_one
    vec_second_out[...] = vec_two
    vec_update_out[...] = vec_update
    vec_square = jnp.sum(vec * vec)
    update_square = jnp.sum(vec_update * vec_update)
    stat_out[...] = stat_tile(
        [
            (1, jnp.sum(weight * weight)),
            (2, jnp.where(is_first, vec_square, 0.0)),
            (3, jnp.where(is_first, 0.0, vec_square)),
            (5, jnp.sum(update * update)),
            (6, jnp.where(is_first, update_square, 0.0)),
            (7, jnp.where(is_first, 0.0, update_square)),
        ]
    )


def trunk_lamb(latent, weight_refs, head_refs, outs, sum_ref):
    rows = Rows(128, latent)
    weight = weight_refs[0][...]
    count = weight.shape[0]
    first, second, update = moments_of(weight, sum_ref[0:count], weight_refs[1][...], weight_refs[2][...])
    outs[1][...] = first
    outs[2][...] = second
    edges = [0, rows.enc_two, rows.dec_one, rows.dec_two, rows.gain, rows.end]
    row = lax.broadcasted_iota(jnp.int32, (count, 1), 0)
    weight_lines = jnp.sum(weight * weight, axis=1, keepdims=True)
    update_lines = jnp.sum(update * update, axis=1, keepdims=True)
    ratio = jnp.zeros((count, 1), f32)
    norms = []
    for index in range(5):
        chosen = (row >= edges[index]) & (row < edges[index + 1])
        weight_norm = jnp.sqrt(jnp.sum(jnp.where(chosen, weight_lines, 0.0), keepdims=True))
        update_norm = jnp.sqrt(jnp.sum(jnp.where(chosen, update_lines, 0.0), keepdims=True))
        ratio = jnp.where(chosen, learn_rate * (weight_norm / update_norm), ratio)
        norms.append((weight_norm, update_norm))
    outs[0][...] = weight - ratio * update
    size = 2 * latent
    head = head_refs[0][...]
    bias = jnp.broadcast_to(sum_ref[296 + size : 297 + size, :], (128, 128)).T[0:size, 0:1]
    grad_head = jnp.concatenate([sum_ref[296 : 296 + size, :], bias], axis=1)
    first, second, update = moments_of(head, grad_head, head_refs[1][...], head_refs[2][...])
    outs[4][...] = first
    outs[5][...] = second
    weight_norm = jnp.sqrt(jnp.sum(head * head, keepdims=True))
    update_norm = jnp.sqrt(jnp.sum(update * update, keepdims=True))
    outs[3][...] = head - learn_rate * (weight_norm / update_norm) * update
    return norms + [(weight_norm, update_norm)]


def final_kernel(latent, loss_scale, all_cells, *refs):
    part_refs, refs = refs[:2], refs[2:]
    dp, own_column, _ = place()
    enc_ref, enc_update_ref, dec_ref, dec_update_ref, vec_ref, vec_update_ref = refs[:6]
    trunk_refs, head_refs = refs[6:9], refs[9:12]
    loss_out, enc_out, enc_copy, dec_out, dec_copy, vec_out, norm_out = refs[12:19]
    trunk_outs = refs[19:25]
    sum_ref = refs[25]
    stats = part_refs[0][0:8]
    for ref in part_refs[1:]:
        stats = stats + ref[0:8]
    roots = jnp.sqrt(jnp.abs(stats[0:1]))

    def ratio(index):
        return learn_rate * (roots[:, index : index + 1] / roots[:, index + 4 : index + 5])

    enc_new = enc_ref[...] - ratio(0) * enc_update_ref[...]
    enc_out[...] = enc_new
    enc_copy[...] = enc_new.astype(bf16)
    dec_new = dec_ref[...] - ratio(1) * dec_update_ref[...]
    dec_out[...] = dec_new
    dec_copy[...] = dec_new.astype(bf16)
    vec_ratio = jnp.where(dp == 0, ratio(2), ratio(3))
    vec_out[...] = vec_ref[...] - vec_ratio * vec_update_ref[...]
    for j in range(COLUMNS):
        start = lax.rem(own_column + j, COLUMNS) * PIECE
        for part, half in ((0, dp), (1, 1 - dp)):
            at = pl.multiple_of(half * (COLUMNS * PIECE) + start, 8)
            sum_ref[pl.ds(at, PIECE), :] = part_refs[part][8 + j * PIECE : 8 + (j + 1) * PIECE, :]
    norms = trunk_lamb(latent, trunk_refs, head_refs, trunk_outs, sum_ref)
    norm_out[0:1, 0:4] = roots[:, 0:4]
    norm_out[1:2, 0:4] = roots[:, 4:8]
    for index, (weight_norm, update_norm) in enumerate(norms):
        norm_out[0:1, 4 + index : 5 + index] = weight_norm
        norm_out[1:2, 4 + index : 5 + index] = update_norm
    lane = lax.broadcasted_iota(jnp.int32, (1, 128), 1)
    loss_out[0] = jnp.sum(jnp.where(lane == 8, -stats[0:1], 0.0)) * loss_scale
    loss_out[1] = jnp.sum(jnp.where(lane == 9, stats[0:1], 0.0)) / all_cells


def on_device(
    cell_counts,
    cell_seeds,
    batch_ids,
    noise_draw,
    cell_factor,
    enc_weight,
    enc_first,
    enc_second,
    dec_weight,
    dec_first,
    dec_second,
    region_vecs,
    vec_first,
    vec_second,
    trunk_rows,
    trunk_first,
    trunk_second,
    head_rows,
    head_first,
    head_second,
):
    cells_here = cell_counts.shape[0]
    enc_weight, enc_first, enc_second = enc_weight.T, enc_first.T, enc_second.T
    head_across, head_first, head_second = head_rows.T, head_first.T, head_second.T
    width = enc_weight.shape[1]
    latent = head_rows.shape[1] // 2
    plane = lax.axis_size("plane")
    total = width * COLUMNS * plane
    all_cells = cells_here * lax.axis_size("dp")
    loss_scale = 1.0 / (all_cells * total)
    share = cells_here // COLUMNS
    own = share // plane
    groups = min(4, plane)
    each = plane // groups
    block = own * each
    regions = COLUMNS * width
    rows = Rows(128, latent)
    column = lax.axis_index("column")
    spot = lax.axis_index("plane")
    tile = jax.ShapeDtypeStruct((8, 128), f32)

    def over_dp(value):
        return lax.ppermute(value, "dp", [(0, 1), (1, 0)])

    def from_column(value, j):
        return lax.ppermute(value, "column", [(i, (i - j) % COLUMNS) for i in range(COLUMNS)])

    def to_column(value, j):
        return lax.ppermute(value, "column", [(i, (i + j) % COLUMNS) for i in range(COLUMNS)])

    def over_plane(value, k):
        return lax.ppermute(value, "plane", [(i, i ^ k) for i in range(plane)])

    def gather_column(value, after=None):
        blocks = []
        for j in range(COLUMNS):
            mine = value if j == 0 else from_column(value, j)
            if j and after is not None:
                mine, _ = lax.optimization_barrier((mine, after))
            blocks += [mine, over_dp(mine)]
        return blocks

    def gather_plane(value):
        blocks = [value] + [over_plane(value, k) for k in range(1, plane)]
        if each == 1:
            return blocks
        return [jnp.concatenate(blocks[g * each : (g + 1) * each], axis=0) for g in range(groups)]

    def scatter_group(values, g):
        received = []
        for e in range(each):
            k = g * each + e
            piece = values if each == 1 else values[e * own : (e + 1) * own]
            received.append(piece if k == 0 else over_plane(piece, k))
        return received

    def call(kernel, name, ins, outs, args, mib=16, scratch=(), grid=(), aliases={}):
        return pl.pallas_call(
            kernel,
            grid=grid,
            in_specs=ins,
            out_specs=tuple(spec for spec, _ in outs),
            out_shape=tuple(shape for _, shape in outs),
            scratch_shapes=list(scratch),
            input_output_aliases=aliases,
            compiler_params=params(mib),
            name=name,
        )(*args)

    def whole(shape, kind=f32):
        return (VMEM, jax.ShapeDtypeStruct(shape, kind))

    in_order = own % 128 != 0
    per_cell = [cell_counts, cell_seeds, cell_factor]
    if in_order:
        per_cell = [
            jnp.concatenate(
                [
                    lax.dynamic_slice_in_dim(x, (column * plane + (spot ^ k)) * own, own)
                    for k in range(plane)
                ]
            )
            for x in per_cell
        ]
    per_cell = [x.reshape(-1, 128) for x in per_cell]
    batch_lines, noise = batch_ids.reshape(-1, 128), noise_draw.T
    if in_order:
        at = (column * plane + spot) * own
        batch_lines = lax.dynamic_slice_in_dim(batch_ids, at, own).reshape(1, own)
        noise = lax.dynamic_slice_in_dim(noise, at, own, axis=1)
    masks, factors = call(
        functools.partial(mask_kernel, total, width, plane, own, in_order),
        "masks",
        [pl.BlockSpec(x.shape, lambda i: (0, 0)) for x in per_cell],
        [
            (pl.BlockSpec((HEIGHT, regions), lambda i: (i, 0)), jax.ShapeDtypeStruct((share, regions), bf16)),
            (pl.BlockSpec((share + 8, 128), lambda i: (0, 0)), jax.ShapeDtypeStruct((share + 8, 128), f32)),
        ],
        per_cell,
        scratch=[
            pltpu.VMEM((7, share // 128, 128), jnp.int32),
            pltpu.VMEM((share // 128, 128), f32),
        ],
        grid=(share // HEIGHT,),
    )

    enc_blocks = gather_column(enc_weight.astype(bf16), factors)
    partials = {}
    early, late = [], []
    for g in [*range(1, groups), 0]:
        (partials[g],) = call(
            functools.partial(encode_kernel, width, g),
            "encode",
            [VMEM] * (1 + 2 * COLUMNS),
            [whole((block, 128))],
            [masks, *enc_blocks],
        )
        if g:
            (late if g == 3 else early).extend(scatter_group(partials[g], g))
        elif each > 1:
            late += scatter_group(partials[0], 0)[1:]
    (partial,) = call(
        add_kernel, "add", [VMEM] * (1 + len(early)), [whole((own, 128))], [partials[0], *early]
    )
    pre_parts = [partial, *late]

    dec_low, vec_low, _ = lax.optimization_barrier(
        (dec_weight, region_vecs, (early[0], partials[0]))
    )
    dec_send = jnp.concatenate([dec_low, vec_low, jnp.zeros((15, width), f32)], axis=0).astype(bf16)
    dec_blocks = gather_column(dec_send)
    dec_pack, lines, small = call(
        functools.partial(pack_kernel, rows.gain),
        "pack",
        [VMEM] * (1 + 2 * COLUMNS),
        [
            whole((COLUMNS, 256, width), bf16),
            whole((COLUMNS, 32, width)),
            (SMEM, jax.ShapeDtypeStruct((1,), jnp.int32)),
        ],
        [trunk_rows, *dec_blocks],
    )

    decoded_low, saved, loss_tile = call(
        functools.partial(forward_kernel, len(pre_parts), latent, own, in_order, plane),
        "forward",
        [VMEM] * (4 + len(pre_parts) + 1),
        [whole((own, 128), bf16), whole((10, own, 128)), (VMEM, tile)],
        [batch_lines, noise, trunk_rows, head_across, *pre_parts, masks],
        scratch=[pltpu.VMEM((2, 128, 128), f32)],
    )

    low_groups = gather_plane(decoded_low)
    sums = []
    back_parts = []
    for g in [*range(1, groups), 0]:
        early = back_parts[: (groups - 2) * each] if g == 0 else []
        *sums, back, loss_tile = call(
            functools.partial(decode_kernel, loss_scale, g, len(early)),
            "decode",
            [SMEM] + [VMEM] * (7 + len(sums) + len(early)),
            [
                whole((COLUMNS, 72, width)),
                whole((COLUMNS, 72, width)),
                whole((block, 128)),
                (VMEM, tile),
            ],
            [small, low_groups[g], masks, factors, dec_pack, lines, saved, loss_tile, *sums, *early],
            scratch=[
                pltpu.VMEM((block, width), f32),
                pltpu.VMEM((block, width), bf16),
                pltpu.VMEM((block, 256), bf16),
                pltpu.VMEM((144, block), bf16),
            ],
            aliases={8: 0, 9: 1} if sums else {},
        )
        if g == 0:
            back_parts = [back] + back_parts[len(early) :]
            if each > 1:
                back_parts += scatter_group(back, 0)[1:]
        else:
            back_parts += scatter_group(back, g)

    def send_sums(mine, other, name, after=()):
        other = over_dp(other)
        blocks = call(
            functools.partial(sum_kernel, name == "dec_sum"),
            name,
            [VMEM] * (2 + len(after)),
            [whole((80, width), jnp.int16)] * (COLUMNS - 1),
            [mine, other, *after],
        )
        return [mine, other] + [to_column(blocks[j - 1], j) for j in (2, 1, 3)]

    dec_parts = send_sums(*sums, "dec_sum")

    pre_low, trunk_mine, trunk_other = call(
        functools.partial(backward_kernel, len(back_parts), latent, loss_scale),
        "backward",
        [VMEM] * (4 + len(back_parts)),
        [whole((own, 128), bf16), whole((COLUMNS, PIECE, 128)), whole((COLUMNS, PIECE, 128))],
        [masks, trunk_rows, head_across, saved, *back_parts],
        scratch=[pltpu.VMEM((320, 128), f32), pltpu.VMEM((128, 128), f32)],
    )

    pre_groups = gather_plane(pre_low)
    enc_mine, enc_other, loss_tile = call(
        functools.partial(encode_back_kernel, groups),
        "encode_back",
        [VMEM] * (5 + groups),
        [whole((COLUMNS, 72, width)), whole((COLUMNS, 72, width)), (VMEM, tile)],
        [masks, lines, loss_tile, trunk_mine, trunk_other, *pre_groups],
        scratch=[pltpu.VMEM((144, share), bf16)],
    )
    like = lambda *arrays: [whole(x.shape) for x in arrays]
    dec_first_new, dec_second_new, dec_update, vec_first_new, vec_second_new, vec_update, dec_stats = call(
        functools.partial(dec_lamb_kernel, loss_scale),
        "dec_lamb",
        [VMEM] * (6 + len(dec_parts)),
        like(*[dec_weight] * 3, *[region_vecs] * 3) + [(VMEM, tile)],
        [dec_weight, dec_first, dec_second, region_vecs, vec_first, vec_second, *dec_parts],
    )
    enc_parts = send_sums(enc_mine, enc_other, "enc_sum")
    stat_tiles = [dec_stats, loss_tile]
    enc_first_new, enc_second_new, enc_update, last = call(
        enc_lamb_kernel,
        "enc_lamb",
        [VMEM] * (4 + COLUMNS + len(stat_tiles)),
        like(*[enc_weight] * 3) + [whole((8 + PIECE, 128))],
        [enc_weight, enc_first, enc_second, *enc_parts, *stat_tiles],
    )
    last = last + sum(over_plane(last, k) for k in range(1, plane))
    lasts = [last] + [from_column(last, j) for j in range(1, COLUMNS)]
    last = jnp.concatenate([sum(x[0:8] for x in lasts), *(x[8:] for x in lasts)], axis=0)
    last_parts = [last, over_dp(last)]
    (
        loss,
        enc_new,
        enc_copy,
        dec_new,
        dec_copy,
        vecs_new,
        norms,
        trunk_new,
        trunk_first_new,
        trunk_second_new,
        head_new,
        head_first_new,
        head_second_new,
    ) = call(
        functools.partial(final_kernel, latent, loss_scale, all_cells),
        "final",
        [VMEM] * (len(last_parts) + 12),
        [
            (SMEM, jax.ShapeDtypeStruct((2,), f32)),
            whole(enc_weight.shape),
            whole(enc_weight.shape, bf16),
            whole(dec_weight.shape),
            whole(dec_weight.shape, bf16),
            whole(region_vecs.shape),
            whole((2, 10)),
            *like(*[trunk_rows] * 3, *[head_across] * 3),
        ],
        [
            *last_parts,
            enc_weight,
            enc_update,
            dec_weight,
            dec_update,
            region_vecs,
            vec_update,
            trunk_rows,
            trunk_first,
            trunk_second,
            head_across,
            head_first,
            head_second,
        ],
        scratch=[pltpu.VMEM((2 * COLUMNS * PIECE, 128), f32)],
    )
    return (
        loss,
        enc_new.T,
        enc_first_new.T,
        enc_second_new.T,
        enc_copy.T,
        dec_new,
        dec_first_new,
        dec_second_new,
        dec_copy,
        vecs_new,
        vec_first_new,
        vec_second_new,
        trunk_new,
        trunk_first_new,
        trunk_second_new,
        head_new.T,
        head_first_new.T,
        head_second_new.T,
        norms,
    )


def solution(mesh):
    regions = mesh.shape["region"]
    devices = mesh.devices.reshape(mesh.shape["dp"], COLUMNS, regions // COLUMNS)
    inner = Mesh(devices, ("dp", "column", "plane"))
    across = ("column", "plane")
    by_row, by_line = P(across, "dp"), P("dp", across)
    return jax.shard_map(
        on_device,
        mesh=inner,
        in_specs=(P("dp"), P("dp"), P("dp"), P("dp", None), P("dp"))
        + (by_row,) * 3
        + (by_line,) * 6
        + (P(),) * 6,
        out_specs=(P(),) + (by_row,) * 4 + (by_line,) * 7 + (P(),) * 7,
        check_vma=False,
    )
```

```python
import functools

import jax
import jax.numpy as jnp
from jax import lax
from jax.experimental import pallas as pl
from jax.experimental.pallas import tpu as pltpu
from jax.sharding import Mesh
from jax.sharding import PartitionSpec as P

BATCHES = 8
COLUMNS = 4
HEIGHT = 512
PIECE = 40
SAFE = 40.0
HOT, NOISE, LEFT, CENTRE, LOG_VAR, SCALE = range(4, 10)
LOG2_E = 1.4426950408889634
LN_2 = 0.6931471805599453

norm_eps = 1e-05
leak_slope = 0.01
decay_rate = 0.5
weight_decay = 0.01
learn_rate = 0.5
lamb_eps = 1e-12

f32 = jnp.float32
bf16 = jnp.bfloat16
VMEM = pl.BlockSpec(memory_space=pltpu.VMEM)
SMEM = pl.BlockSpec(memory_space=pltpu.SMEM)
MEGA = 1024 * 1024


def params(mib=16):
    return pltpu.CompilerParams(vmem_limit_bytes=mib * MEGA)


def place():
    return tuple(lax.axis_index(name) for name in ("dp", "column", "plane"))


def exact(left, right, contract=((1,), (0,))):
    return lax.dot_general(
        left, right, (contract, ((), ())), precision=lax.Precision.HIGHEST, preferred_element_type=f32
    )


def wide(left, right, contract=((1,), (0,))):
    return lax.dot_general(left, right, (contract, ((), ())), preferred_element_type=f32)


def remainder(values, divisor):
    guess = jnp.floor(values.astype(f32) * (1.0 / divisor)).astype(jnp.int32)
    rest = values - guess * divisor
    rest = jnp.where(rest < 0, rest + divisor, rest)
    return jnp.where(rest >= divisor, rest - divisor, rest)


def turns(values, total):
    whole = 2**32 // total
    part = (2**32 % total) / total
    return values * whole + (values.astype(f32) * part + 0.5).astype(jnp.int32)


def mask_kernel(total, width, plane, own, in_order, cells_ref, factors_ref, *refs):
    mask_ref, factor_ref, table_ref, held_ref = refs
    step = pl.program_id(0)
    lines_here = table_ref.shape[1]

    @pl.when(step == 0)
    def _():
        _, column, spot = place()
        if in_order:
            counts, seeds, factors = cells_ref[0], cells_ref[1], factors_ref[...]
        else:
            each = own // 128
            starts = [
                (column * plane + (spot ^ k)) * each + i for k in range(plane) for i in range(each)
            ]
            counts, seeds, factors = (
                jnp.concatenate([ref[pl.ds(at, 1), :] for at in starts], axis=0)
                for ref in (cells_ref.at[0], cells_ref.at[1], factors_ref)
            )
        stride = 6 * remainder(seeds, total // 6) + 1
        low_end = jnp.int32(-(2**31))
        half = jnp.int32(2**31 // total)
        for j in range(COLUMNS):
            base = (lax.rem(column + j, COLUMNS) * plane + spot) * width
            upper = remainder(stride * (base // 256), total)
            start = remainder(upper * 256 + stride * (base % 256) + seeds, total)
            table_ref[j] = turns(start, total) + (low_end + half)
        table_ref[4] = turns(stride, total)
        table_ref[5] = turns(remainder(stride * 128, total), total)
        table_ref[6] = turns(counts, total) + low_end
        cell = lax.broadcasted_iota(jnp.int32, (lines_here, 128), 0) * 128
        cell = cell + lax.broadcasted_iota(jnp.int32, (lines_here, 128), 1)
        known = jnp.where(cell < own, counts.astype(f32) * jnp.log(factors), 0.0)
        row = lax.broadcasted_iota(jnp.int32, (8, 128), 0)
        known = jnp.where(row == 0, jnp.sum(known, axis=0, keepdims=True), 0.0)
        factor_ref[128 * lines_here : 128 * lines_here + 8, :] = known
        held_ref[...] = factors

    height = mask_ref.shape[0] // 128
    for sub in range(height):
        line = step * height + sub
        at = pl.ds(line, 1)
        rows = [table_ref[j, at, :] for j in range(7)]
        table = jnp.concatenate(rows + rows[:1], axis=0).T
        factors = jnp.broadcast_to(held_ref[at, :], (8, 128)).T[:, 0:1]
        factor_ref[pl.ds(pl.multiple_of(line * 128, 128), 128), :] = jnp.broadcast_to(factors, (128, 128))
        for part in range(4):
            cells = slice(part * 32, part * 32 + 32)
            lines = slice(sub * 128 + part * 32, sub * 128 + part * 32 + 32)
            shape = (32, 128)
            lane = lax.broadcasted_iota(jnp.int32, shape, 1)
            span = jnp.broadcast_to(table[cells, 4:5], shape) * lane
            advance = jnp.broadcast_to(table[cells, 5:6], shape)
            limit = jnp.broadcast_to(table[cells, 6:7], shape)
            for column in range(COLUMNS):
                value = jnp.broadcast_to(table[cells, column : column + 1], shape) + span
                for group in range(width // 128):
                    here = column * width + group * 128
                    mask_ref[lines, here : here + 128] = jnp.where(value < limit, 1.0, 0.0).astype(bf16)
                    value = value + advance


def encode_kernel(width, group, mask_ref, *refs):
    out_ref = refs[-1]
    cells = out_ref.shape[0]
    lines = slice(group * cells, (group + 1) * cells)
    total = None
    for column in range(COLUMNS):
        block = jnp.concatenate([refs[2 * column][...], refs[2 * column + 1][...]], axis=0)
        term = wide(mask_ref[lines, column * width : (column + 1) * width], block, ((1,), (1,)))
        total = term if total is None else total + term
    out_ref[...] = total


def add_kernel(first_ref, *refs):
    out_ref = refs[-1]
    total = first_ref[0 : out_ref.shape[0]]
    for ref in refs[:-1]:
        total = total + ref[...]
    out_ref[...] = total


def pack_kernel(gain_row, trunk_ref, *refs):
    weight_ref, line_ref, small_ref = refs[-3:]
    is_first = place()[0] == 0
    longest = largest = jnp.zeros((1, 1), f32)
    for column in range(COLUMNS):
        mine = refs[2 * column][...]
        other = refs[2 * column + 1][...]
        mine_line = mine[64:80].astype(f32)[0:1]
        other_line = other[64:80].astype(f32)[0:1]
        bias = jnp.where(is_first, mine_line, other_line)
        logit = jnp.where(is_first, other_line, mine_line)
        width = mine.shape[1]
        row = lax.broadcasted_iota(jnp.int32, (16, width), 0)
        weight_ref[column, 0:64] = mine[0:64]
        weight_ref[column, 64:128] = other[0:64]
        weight_ref[column, 128:144] = jnp.where(row == 0, bias, 0.0).astype(bf16)
        weight_ref[column, 144:256] = jnp.zeros((112, width), bf16)
        spread = jnp.exp(-jnp.abs(logit))
        chance = jnp.where(logit >= 0, 1.0, spread) / (1.0 + spread)
        logs = jnp.minimum(logit, 0.0) - jnp.log(1.0 + spread)
        line_ref[column, 0:16] = jnp.broadcast_to(chance, (16, width))
        line_ref[column, 16:32] = jnp.broadcast_to(logs, (16, width))
        one, two = mine[0:64].astype(f32), other[0:64].astype(f32)
        squares = jnp.sum(one * one + two * two, axis=0, keepdims=True)
        longest = jnp.maximum(longest, jnp.max(squares, axis=1, keepdims=True))
        largest = jnp.maximum(largest, jnp.max(jnp.abs(bias), axis=1, keepdims=True))
    gain = jnp.max(jnp.abs(trunk_ref[gain_row + 3 : gain_row + 4, :]), axis=1, keepdims=True)
    shift = trunk_ref[gain_row + 7 : gain_row + 8, :]
    reach = gain * (128.0**0.5) + jnp.sqrt(jnp.sum(shift * shift, axis=1, keepdims=True))
    bound = 1.02 * reach * jnp.sqrt(longest) + largest
    small_ref[0] = jnp.sum(jnp.where(bound < SAFE, 1, 0))


def normalize(values):
    centre = values - jnp.mean(values, axis=-1, keepdims=True)
    spread = jnp.mean(centre * centre, axis=-1, keepdims=True)
    scale = lax.rsqrt(spread + norm_eps)
    return centre * scale, scale


def leaky(values):
    return jnp.where(values >= 0, values, leak_slope * values)


def swap_halves(values, is_first):
    return jnp.where(is_first, values, pltpu.roll(values, 64, 1))


class Rows:
    def __init__(self, hidden, latent):
        self.enc_two = BATCHES
        self.dec_one = BATCHES + hidden
        self.dec_two = 2 * BATCHES + hidden + latent
        self.gain = 2 * BATCHES + 2 * hidden + latent
        self.shift = self.gain + 4
        self.end = self.gain + 8


def turned_rows(values, own):
    rows, spare = values.shape[0], -values.shape[1] % 128
    if spare:
        values = jnp.concatenate([values, jnp.zeros((rows, spare), f32)], axis=1)
    if rows == 1:
        full = jnp.broadcast_to(values, (128, values.shape[1]))
    else:
        full = jnp.concatenate([values, jnp.zeros((128 - rows, values.shape[1]), f32)], axis=0)
    return full.T[0:own]


def forward_kernel(parts, latent, own, in_order, plane, *refs):
    ids_ref, noise_ref, trunk_ref, head_ref, *refs = refs
    part_refs = refs[:parts]
    low_ref, saved_ref, stat_ref, table_ref = refs[-4:]
    dp, own_column, spot = place()
    is_first = dp == 0
    rows = Rows(128, latent)
    total = part_refs[0][0:own]
    for ref in part_refs[1:]:
        total = total + ref[...]
    total = swap_halves(total, is_first)
    lane = lax.broadcasted_iota(jnp.int32, total.shape, 1)
    if in_order:
        ids, noise = ids_ref[...], noise_ref[...]
    else:
        line = (own_column * plane + spot) * (own // 128)
        ids = jnp.concatenate([ids_ref[pl.ds(line + i, 1), :] for i in range(own // 128)], axis=1)
        noise = noise_ref[:, pl.ds(pl.multiple_of(line * 128, 128), own)]
    ids = turned_rows(ids.astype(f32), own).astype(jnp.int32)
    noise = turned_rows(noise, own)
    saved_ref[NOISE] = noise
    hot = jnp.where(lane == ids, 1.0, 0.0)
    saved_ref[HOT] = hot
    gains = trunk_ref[rows.gain : rows.gain + 4, :]
    shifts = trunk_ref[rows.shift : rows.shift + 4, :]

    def act(index, values):
        normal, scale = normalize(values)
        saved_ref[index] = normal
        return leaky(normal * gains[index : index + 1] + shifts[index : index + 1]), scale

    first, scale0 = act(0, total + exact(hot, trunk_ref[0:128, :]))
    second, scale1 = act(1, exact(first, trunk_ref[rows.enc_two : rows.enc_two + 128, :]))
    size = 2 * latent
    table_ref[...] = jnp.zeros_like(table_ref)
    table_ref[0, 0:size] = head_ref[:, 0:128]
    table_ref[1, 0:size] = jnp.broadcast_to(head_ref[:, 128:129], (size, 128))
    moments = exact(second, table_ref[0], ((1,), (1,))) + table_ref[1].T[0:1]
    inside = lane < latent
    centre = jnp.where(inside, moments, 0.0)
    log_var = jnp.where(inside, pltpu.roll(moments, 128 - latent, 1), 0.0)
    sample = centre + jnp.exp(0.5 * log_var) * noise
    left = sample + jnp.where(lane == ids + latent, 1.0, 0.0)
    third, scale2 = act(2, exact(left, trunk_ref[rows.dec_one : rows.dec_one + 128, :]))
    fourth, scale3 = act(3, exact(third, trunk_ref[rows.dec_two : rows.dec_two + 128, :]))
    low_ref[...] = swap_halves(fourth, is_first).astype(bf16)
    saved_ref[LEFT] = left
    saved_ref[CENTRE] = centre
    saved_ref[LOG_VAR] = log_var
    saved_ref[SCALE] = jnp.where(
        lane == 0, scale0, jnp.where(lane == 1, scale1, jnp.where(lane == 2, scale2, scale3))
    )
    diverge = 0.5 * jnp.sum(jnp.exp(log_var) + centre * centre - 1.0 - log_var)
    stat_ref[...] = stat_tile([(9, diverge)])


def decode_kernel(loss_scale, group, parts, small_ref, low_ref, mask_ref, factor_ref, weight_ref, line_ref, *refs):
    saved_ref, loss_in, *refs = refs
    has_sum = group != 1
    if has_sum:
        refs = refs[2:]
    part_refs, refs = refs[:parts], refs[parts:]
    mine_ref, other_ref, back_ref, loss_ref, logit_ref, grad_ref, left_ref, turned_ref = refs
    cells, width = grad_ref.shape
    half = cells // 2
    halves = (slice(0, half), slice(half, cells))
    blocks = width // 128
    first_row = group * cells
    zero = jnp.zeros((8, 128), f32)

    low = low_ref[...]
    left_ref[:, 0:128] = low
    lane = lax.broadcasted_iota(jnp.int32, (cells, 128), 1)
    left_ref[:, 128:256] = jnp.where(lane == 0, 1.0, 0.0).astype(bf16)
    turned_ref[0:128, :] = low.astype(f32).T.astype(bf16)
    row = lax.broadcasted_iota(jnp.int32, (16, cells), 0)
    turned_ref[128:144, :] = jnp.where(row == 0, 1.0, 0.0).astype(bf16)
    back_ref[...] = jnp.zeros_like(back_ref)
    grad_ref[halves[1], :] = jnp.zeros((half, width), bf16)
    if not has_sum:
        mine_ref[...] = jnp.zeros_like(mine_ref)
        other_ref[...] = jnp.zeros_like(other_ref)

    def logits_of(lines, column):
        logit_ref[lines, :] = wide(left_ref[lines, :], weight_ref[column])

    def add_sums(lines, column):
        product = wide(turned_ref[:, lines], grad_ref[lines, :])
        tail = product[128:136]
        mine_ref[column, 0:72] += jnp.concatenate([product[0:64], tail], axis=0)
        other_ref[column, 0:72] += jnp.concatenate([product[64:128], tail], axis=0)

    def add_back(lines, column):
        back_ref[lines, :] += wide(grad_ref[lines, :], weight_ref[column, 0:128], ((1,), (1,)))

    def add_odds(column, odds):
        line = jnp.sum(jnp.concatenate(odds, axis=1), axis=0, keepdims=True)
        place = lax.broadcasted_iota(jnp.int32, (8, width), 0)
        line = jnp.where(place == 1, line * loss_scale, 0.0)
        mine_ref[column, 64:72] += line
        other_ref[column, 64:72] += line

    def finish(loss_sum):
        if group == 0:
            loss_sum = loss_sum + factor_ref[-8:, :]
        loss_ref[...] = loss_in[...] + stat_tile([(8, jnp.sum(loss_sum))])
        for ref in part_refs:
            back_ref[0 : ref.shape[0]] += ref[...]

    def quick(column, at, odds, loss_sum):
        factor = factor_ref[first_row + at : first_row + at + 16, :]
        held = None
        for block in range(blocks):
            lanes = slice(block * 128, block * 128 + 128)
            far = slice(column * width + block * 128, column * width + block * 128 + 128)
            ratio = jnp.exp2(logit_ref[at : at + 16, lanes] * -LOG2_E)
            whole = 1.0 + ratio
            chance = factor * line_ref[column, 0:16, lanes]
            opened = mask_ref[first_row + at : first_row + at + 16, far].astype(f32) > 0.5
            rest = jnp.where(opened, 1.0, whole - chance)
            inverse = pl.reciprocal(whole * rest)
            part = jnp.where(opened, -1.0, chance) * inverse
            grad_ref[at : at + 16, lanes] = ((ratio * part) * loss_scale).astype(bf16)
            odds[block] = odds[block] + part[0:8] + part[8:16]
            likely = rest * (rest * inverse)
            held = likely if held is None else held * likely
            if block % 2 == 1 or block == blocks - 1:
                logs = jnp.log2(held)
                loss_sum = loss_sum + logs[0:8] + logs[8:16]
                held = None
        return loss_sum

    @pl.when(small_ref[0] == 1)
    def _():
        logits_of(halves[0], 0)
        loss_sum = zero
        for column in range(COLUMNS):
            odds = [zero] * blocks
            for at in range(0, half, 16):
                loss_sum = quick(column, at, odds, loss_sum)
            logits_of(halves[1], column)
            if column > 0:
                add_sums(halves[1], column - 1)
                add_back(halves[1], column - 1)
            for at in range(half, cells, 16):
                loss_sum = quick(column, at, odds, loss_sum)
            if column + 1 < COLUMNS:
                logits_of(halves[0], column + 1)
            add_sums(halves[0], column)
            add_back(halves[0], column)
            add_odds(column, odds)
        add_sums(halves[1], COLUMNS - 1)
        add_back(halves[1], COLUMNS - 1)
        finish(loss_sum * LN_2)

    def steady(column, loss_sum):
        logits_of(slice(None), column)

        def step(index, carried):
            loss_sum, *odds = carried
            here = pl.multiple_of(index * 16, 16)
            at = pl.ds(here, 16)
            far_at = pl.ds(pl.multiple_of(first_row + here, 16), 16)
            factor = factor_ref[far_at, :]
            top = bottom = held = None
            for block in range(blocks):
                lanes = slice(block * 128, block * 128 + 128)
                far = pl.ds(pl.multiple_of(column * width + block * 128, 128), 128)
                logits = logit_ref[at, lanes]
                spread = jnp.exp(-jnp.abs(logits))
                whole = 1.0 + spread
                positive = logits >= 0
                chance = factor * line_ref[column, 0:16, lanes]
                taken = chance * jnp.where(positive, 1.0, spread)
                opened = mask_ref[far_at, far].astype(f32) > 0.5
                rest = jnp.where(opened, 1.0, whole - taken)
                inverse = pl.reciprocal(whole * rest)
                upper = jnp.where(opened, jnp.where(positive, -spread, -1.0), spread * chance)
                slope = upper * inverse
                grad_ref[at, lanes] = (slope * loss_scale).astype(bf16)
                part = jnp.where(opened, -1.0, taken * whole * inverse) - slope
                odds[block] = odds[block] + part[0:8] + part[8:16]
                likely = jnp.where(opened, jnp.minimum(logits, 0.0), 0.0)
                held = likely if held is None else held + likely
                top = rest if top is None else top * rest
                bottom = whole if bottom is None else bottom * whole
            held = held + (jnp.log(top) - jnp.log(bottom))
            return (loss_sum + held[0:8] + held[8:16], *odds)

        loss_sum, *odds = lax.fori_loop(0, cells // 16, step, (loss_sum,) + (zero,) * blocks)
        add_sums(slice(None), column)
        add_back(slice(None), column)
        add_odds(column, odds)
        return loss_sum

    @pl.when(small_ref[0] != 1)
    def _():
        finish(lax.fori_loop(0, COLUMNS, steady, zero))


def backward_kernel(parts, latent, loss_scale, _, trunk_ref, head_ref, saved_ref, *refs):
    part_refs = refs[:parts]
    low_ref, mine_ref, other_ref, sum_ref, table_ref = refs[parts:]
    table_ref[...] = jnp.zeros_like(table_ref)
    table_ref[0 : 2 * latent] = head_ref[:, 0:128]
    dp, own_column, _ = place()
    is_first = dp == 0
    own = low_ref.shape[0]
    rows = Rows(128, latent)
    total = part_refs[0][0:own]
    for ref in part_refs[1:]:
        total = total + ref[...]
    total = swap_halves(total, is_first)
    lane = lax.broadcasted_iota(jnp.int32, total.shape, 1)
    gains = trunk_ref[rows.gain : rows.gain + 4, :]
    shifts = trunk_ref[rows.shift : rows.shift + 4, :]
    sum_ref[...] = jnp.zeros_like(sum_ref)
    rows_in, rows_out = ((0,), (0,)), ((1,), (1,))

    def output(index):
        return leaky(saved_ref[index] * gains[index : index + 1] + shifts[index : index + 1])

    def pull(index, grad):
        normal = saved_ref[index]
        gain = gains[index : index + 1]
        before = normal * gain + shifts[index : index + 1]
        grad = jnp.where(before >= 0, grad, leak_slope * grad)
        at = rows.gain + index
        sum_ref[at : at + 1, :] = jnp.sum(grad * normal, axis=0, keepdims=True)
        at = rows.shift + index
        sum_ref[at : at + 1, :] = jnp.sum(grad, axis=0, keepdims=True)
        grad = grad * gain
        plain = jnp.mean(grad, axis=-1, keepdims=True)
        along = jnp.mean(grad * normal, axis=-1, keepdims=True)
        return (grad - plain - normal * along) * saved_ref[SCALE][:, index : index + 1]

    grad = pull(3, total)
    sum_ref[rows.dec_two : rows.dec_two + 128, :] = exact(output(2), grad, rows_in)
    grad = pull(2, exact(grad, trunk_ref[rows.dec_two : rows.dec_two + 128, :], rows_out))
    one = exact(saved_ref[LEFT], grad, rows_in)
    sum_ref[rows.dec_one : rows.dec_two, :] = one[0 : rows.dec_two - rows.dec_one]
    grad = exact(grad, trunk_ref[rows.dec_one : rows.dec_one + 128, :], rows_out)
    inside = lane < latent
    grad = jnp.where(inside, grad, 0.0)
    centre, log_var = saved_ref[CENTRE], saved_ref[LOG_VAR]
    grad_centre = grad + loss_scale * centre
    grad_log = grad * 0.5 * jnp.exp(0.5 * log_var) * saved_ref[NOISE] + (0.5 * loss_scale) * (
        jnp.exp(log_var) - 1.0
    )
    both = jnp.where(inside, grad_centre, pltpu.roll(jnp.where(inside, grad_log, 0.0), latent, 1))
    head = exact(both, output(1), rows_in)
    sum_ref[296 : 296 + 24, :] = head[0:24]
    sum_ref[296 + 2 * latent : 297 + 2 * latent, :] = jnp.sum(both, axis=0, keepdims=True)
    grad = pull(1, exact(both, table_ref[...]))
    sum_ref[rows.enc_two : rows.enc_two + 128, :] = exact(output(0), grad, rows_in)
    grad = pull(0, exact(grad, trunk_ref[rows.enc_two : rows.enc_two + 128, :], rows_out))
    low = grad.astype(bf16)
    hot = saved_ref[HOT].astype(bf16)
    sum_ref[0:BATCHES, :] = wide(hot, low, rows_in)[0:BATCHES]
    low_ref[...] = swap_halves(low.astype(f32), is_first).astype(bf16)
    for j in range(COLUMNS):
        start = lax.rem(own_column + j, COLUMNS) * PIECE
        for ref, half in ((mine_ref, dp), (other_ref, 1 - dp)):
            at = pl.multiple_of(half * (COLUMNS * PIECE) + start, 8)
            ref[j] = sum_ref[pl.ds(at, PIECE), :]


def encode_back_kernel(groups, mask_ref, line_ref, loss_in, trunk_mine_ref, trunk_other_ref, *refs):
    low_refs = refs[:groups]
    mine_ref, other_ref, known_ref, turned_ref = refs[groups:]
    cells = low_refs[0].shape[0]
    share = turned_ref.shape[1]
    width = mine_ref.shape[2]
    for group in range(groups):
        turned_ref[0:128, group * cells : (group + 1) * cells] = (
            low_refs[group][...].astype(f32).T.astype(bf16)
        )
    row = lax.broadcasted_iota(jnp.int32, (16, share), 0)
    turned_ref[128:144, :] = jnp.where(row == 0, 1.0, 0.0).astype(bf16)
    known = jnp.zeros((8, width), f32)
    for column in range(COLUMNS):
        product = wide(turned_ref[...], mask_ref[:, column * width : (column + 1) * width])
        mine_ref[column, 0:64] = product[0:64]
        other_ref[column, 0:64] = product[64:128]
        known = known + product[128:136] * line_ref[column, 16:24, :]
        for ref, trunk_ref in ((mine_ref, trunk_mine_ref), (other_ref, trunk_other_ref)):
            ref[column, 64:72] = jnp.zeros((8, width), f32)
            for part in range(PIECE // 8):
                lanes = slice(part * 128, part * 128 + 128)
                ref[column, 64:72, lanes] = trunk_ref[column, part * 8 : part * 8 + 8, :]
    known_ref[...] = loss_in[...] + stat_tile([(8, jnp.sum(known))])


def power_for(values):
    return 13.0 - jnp.floor(jnp.log2(jnp.maximum(values, 1e-30)))


def fold_tail(tail):
    row = lax.broadcasted_iota(jnp.int32, tail.shape, 0)
    lane = lax.broadcasted_iota(jnp.int32, tail.shape, 1)
    moved = pltpu.roll(pltpu.roll(tail, 2, 0), 128, 1)
    free = tail.shape[1] - 128
    moved = jnp.where((row == 2) | (row == 3), jnp.where(lane < 128, moved, 0.0), 0.0)
    return jnp.where((row < 2) & (lane < free), tail, moved)


def sum_kernel(folded, mine_ref, other_ref, *refs):
    width = mine_ref.shape[2]
    for j in range(1, COLUMNS):
        out_ref = refs[j - COLUMNS]
        total = mine_ref[j] + other_ref[j]
        main, tail = total[0:64], total[64:72]
        if folded:
            tail = fold_tail(tail)
        power = power_for(jnp.max(jnp.abs(main), axis=0, keepdims=True))
        out_ref[0:64] = jnp.round(main * jnp.exp2(power)).astype(jnp.int32).astype(jnp.int16)
        most = jnp.max(jnp.max(jnp.abs(tail), axis=0, keepdims=True), axis=1, keepdims=True)
        tail_power = power_for(most)
        tail = tail * jnp.exp2(tail_power)
        high = jnp.round(tail)
        low = jnp.round((tail - high) * 16384.0)
        row = lax.broadcasted_iota(jnp.int32, (8, 128), 0)
        note = jnp.where(row == 6, tail_power, 0.0)
        for i in range(width // 128):
            note = jnp.where(row == i, power[:, i * 128 : i * 128 + 128], note)
        high = jnp.concatenate([high[:, : width - 128], note], axis=1)
        out_ref[64:80] = jnp.concatenate([high, low], axis=0).astype(jnp.int32).astype(jnp.int16)


def received(ref):
    width = ref.shape[1]
    ends = ref[64:80].astype(jnp.int32).astype(f32)
    note = ends[0:8, width - 128 :]
    power = jnp.concatenate([note[i : i + 1] for i in range(width // 128)], axis=1)
    main = ref[0:64].astype(jnp.int32).astype(f32) * jnp.exp2(-power)
    tail = (ends[0:8] + ends[8:16] * (1.0 / 16384.0)) * jnp.exp2(-note[6:7, 0:1])
    return main, tail


def stat_tile(pairs):
    lane = lax.broadcasted_iota(jnp.int32, (8, 128), 1)
    row = lax.broadcasted_iota(jnp.int32, (8, 128), 0)
    tile = jnp.zeros((8, 128), f32)
    for index, value in pairs:
        tile = jnp.where(lane == index, value, tile)
    return jnp.where(row == 0, tile, 0.0)


def moments_of(weight, grad, first, second):
    first_new = decay_rate * first + (1.0 - decay_rate) * grad
    second_new = decay_rate * second + (1.0 - decay_rate) * grad * grad
    update = first_new / (jnp.sqrt(second_new) + lamb_eps) + weight_decay * weight
    return first_new, second_new, update


def enc_lamb_kernel(*refs):
    weight_ref, first_ref, second_ref, mine_ref, other_ref, *part_refs = refs[: 4 + COLUMNS]
    stat_refs = refs[4 + COLUMNS : -4]
    first_out, second_out, update_out, tile_out = refs[-4:]
    grad = mine_ref[0] + other_ref[0]
    tail = grad[64:72]
    grad = grad[0:64]
    for ref in part_refs:
        main, extra = received(ref)
        grad, tail = grad + main, tail + extra
    weight = weight_ref[...]
    first, second, update = moments_of(weight, grad, first_ref[...], second_ref[...])
    first_out[...] = first
    second_out[...] = second
    update_out[...] = update
    others = sum(ref[...] for ref in stat_refs)
    stats = stat_tile(
        [
            (0, jnp.sum(weight * weight)),
            (4, jnp.sum(update * update)),
        ]
    )
    tile_out[0:8] = stats + others
    for part in range(PIECE // 8):
        tile_out[8 + part * 8 : 16 + part * 8] = tail[:, part * 128 : part * 128 + 128]


def dec_lamb_kernel(loss_scale, *refs):
    weight_ref, first_ref, second_ref, vec_ref, vec_first_ref, vec_second_ref, mine_ref, other_ref = refs[:8]
    part_refs, refs = refs[8 : 7 + COLUMNS], refs[-7:]
    first_out, second_out, update_out, vec_first_out, vec_second_out, vec_update_out, stat_out = refs
    grad = mine_ref[0] + other_ref[0]
    tail = fold_tail(grad[64:72])
    grad = grad[0:64]
    for ref in part_refs:
        main, extra = received(ref)
        grad, tail = grad + main, tail + extra
    free = grad.shape[1] - 128
    tail = jnp.concatenate([tail[0:2, :free], tail[2:4, 0:128]], axis=1)
    weight = weight_ref[...]
    first, second, update = moments_of(weight, grad, first_ref[...], second_ref[...])
    first_out[...] = first
    second_out[...] = second
    update_out[...] = update
    is_first = place()[0] == 0
    vec = vec_ref[...]
    low = vec.astype(bf16).astype(f32)
    keep = 1.0 / (1.0 + jnp.exp(low))
    line = tail[0:1]
    line = jnp.where(is_first, line, keep * (tail[1:2] + line))
    vec_one, vec_two, vec_update = moments_of(vec, line, vec_first_ref[...], vec_second_ref[...])
    vec_first_out[...] = vec_one
    vec_second_out[...] = vec_two
    vec_update_out[...] = vec_update
    vec_square = jnp.sum(vec * vec)
    update_square = jnp.sum(vec_update * vec_update)
    stat_out[...] = stat_tile(
        [
            (1, jnp.sum(weight * weight)),
            (2, jnp.where(is_first, vec_square, 0.0)),
            (3, jnp.where(is_first, 0.0, vec_square)),
            (5, jnp.sum(update * update)),
            (6, jnp.where(is_first, update_square, 0.0)),
            (7, jnp.where(is_first, 0.0, update_square)),
        ]
    )


def trunk_lamb(latent, weight_refs, head_refs, outs, sum_ref):
    rows = Rows(128, latent)
    weight = weight_refs[0][...]
    count = weight.shape[0]
    first, second, update = moments_of(weight, sum_ref[0:count], weight_refs[1][...], weight_refs[2][...])
    outs[1][...] = first
    outs[2][...] = second
    edges = [0, rows.enc_two, rows.dec_one, rows.dec_two, rows.gain, rows.end]
    row = lax.broadcasted_iota(jnp.int32, (count, 1), 0)
    weight_lines = jnp.sum(weight * weight, axis=1, keepdims=True)
    update_lines = jnp.sum(update * update, axis=1, keepdims=True)
    ratio = jnp.zeros((count, 1), f32)
    norms = []
    for index in range(5):
        chosen = (row >= edges[index]) & (row < edges[index + 1])
        weight_norm = jnp.sqrt(jnp.sum(jnp.where(chosen, weight_lines, 0.0), keepdims=True))
        update_norm = jnp.sqrt(jnp.sum(jnp.where(chosen, update_lines, 0.0), keepdims=True))
        ratio = jnp.where(chosen, learn_rate * (weight_norm / update_norm), ratio)
        norms.append((weight_norm, update_norm))
    outs[0][...] = weight - ratio * update
    size = 2 * latent
    head = head_refs[0][...]
    bias = jnp.broadcast_to(sum_ref[296 + size : 297 + size, :], (128, 128)).T[0:size, 0:1]
    grad_head = jnp.concatenate([sum_ref[296 : 296 + size, :], bias], axis=1)
    first, second, update = moments_of(head, grad_head, head_refs[1][...], head_refs[2][...])
    outs[4][...] = first
    outs[5][...] = second
    weight_norm = jnp.sqrt(jnp.sum(head * head, keepdims=True))
    update_norm = jnp.sqrt(jnp.sum(update * update, keepdims=True))
    outs[3][...] = head - learn_rate * (weight_norm / update_norm) * update
    return norms + [(weight_norm, update_norm)]


def final_kernel(latent, loss_scale, all_cells, *refs):
    part_refs, refs = refs[:2], refs[2:]
    dp, own_column, _ = place()
    enc_ref, enc_update_ref, dec_ref, dec_update_ref, vec_ref, vec_update_ref = refs[:6]
    trunk_refs, head_refs = refs[6:9], refs[9:12]
    loss_out, enc_out, enc_copy, dec_out, dec_copy, vec_out, norm_out = refs[12:19]
    trunk_outs = refs[19:25]
    sum_ref = refs[25]
    stats = part_refs[0][0:8]
    for ref in part_refs[1:]:
        stats = stats + ref[0:8]
    roots = jnp.sqrt(jnp.abs(stats[0:1]))

    def ratio(index):
        return learn_rate * (roots[:, index : index + 1] / roots[:, index + 4 : index + 5])

    enc_new = enc_ref[...] - ratio(0) * enc_update_ref[...]
    enc_out[...] = enc_new
    enc_copy[...] = enc_new.astype(bf16)
    dec_new = dec_ref[...] - ratio(1) * dec_update_ref[...]
    dec_out[...] = dec_new
    dec_copy[...] = dec_new.astype(bf16)
    vec_ratio = jnp.where(dp == 0, ratio(2), ratio(3))
    vec_out[...] = vec_ref[...] - vec_ratio * vec_update_ref[...]
    for j in range(COLUMNS):
        start = lax.rem(own_column + j, COLUMNS) * PIECE
        for part, half in ((0, dp), (1, 1 - dp)):
            at = pl.multiple_of(half * (COLUMNS * PIECE) + start, 8)
            sum_ref[pl.ds(at, PIECE), :] = part_refs[part][8 + j * PIECE : 8 + (j + 1) * PIECE, :]
    norms = trunk_lamb(latent, trunk_refs, head_refs, trunk_outs, sum_ref)
    norm_out[0:1, 0:4] = roots[:, 0:4]
    norm_out[1:2, 0:4] = roots[:, 4:8]
    for index, (weight_norm, update_norm) in enumerate(norms):
        norm_out[0:1, 4 + index : 5 + index] = weight_norm
        norm_out[1:2, 4 + index : 5 + index] = update_norm
    lane = lax.broadcasted_iota(jnp.int32, (1, 128), 1)
    loss_out[0] = jnp.sum(jnp.where(lane == 8, -stats[0:1], 0.0)) * loss_scale
    loss_out[1] = jnp.sum(jnp.where(lane == 9, stats[0:1], 0.0)) / all_cells


def on_device(
    cell_counts,
    cell_seeds,
    batch_ids,
    noise_draw,
    cell_factor,
    enc_weight,
    enc_first,
    enc_second,
    dec_weight,
    dec_first,
    dec_second,
    region_vecs,
    vec_first,
    vec_second,
    trunk_rows,
    trunk_first,
    trunk_second,
    head_rows,
    head_first,
    head_second,
):
    cells_here = cell_counts.shape[0]
    enc_weight, enc_first, enc_second = enc_weight.T, enc_first.T, enc_second.T
    head_across, head_first, head_second = head_rows.T, head_first.T, head_second.T
    width = enc_weight.shape[1]
    latent = head_rows.shape[1] // 2
    plane = lax.axis_size("plane")
    total = width * COLUMNS * plane
    all_cells = cells_here * lax.axis_size("dp")
    loss_scale = 1.0 / (all_cells * total)
    share = cells_here // COLUMNS
    own = share // plane
    groups = min(4, plane)
    each = plane // groups
    block = own * each
    regions = COLUMNS * width
    rows = Rows(128, latent)
    column = lax.axis_index("column")
    spot = lax.axis_index("plane")
    tile = jax.ShapeDtypeStruct((8, 128), f32)

    def over_dp(value):
        return lax.ppermute(value, "dp", [(0, 1), (1, 0)])

    def from_column(value, j):
        return lax.ppermute(value, "column", [(i, (i - j) % COLUMNS) for i in range(COLUMNS)])

    def to_column(value, j):
        return lax.ppermute(value, "column", [(i, (i + j) % COLUMNS) for i in range(COLUMNS)])

    def over_plane(value, k):
        return lax.ppermute(value, "plane", [(i, i ^ k) for i in range(plane)])

    def gather_column(value, after=None):
        blocks = []
        for j in range(COLUMNS):
            mine = value if j == 0 else from_column(value, j)
            if j and after is not None:
                mine, _ = lax.optimization_barrier((mine, after))
            blocks += [mine, over_dp(mine)]
        return blocks

    def gather_plane(value):
        blocks = [value] + [over_plane(value, k) for k in range(1, plane)]
        if each == 1:
            return blocks
        return [jnp.concatenate(blocks[g * each : (g + 1) * each], axis=0) for g in range(groups)]

    def scatter_group(values, g):
        received = []
        for e in range(each):
            k = g * each + e
            piece = values if each == 1 else values[e * own : (e + 1) * own]
            received.append(piece if k == 0 else over_plane(piece, k))
        return received

    def call(kernel, name, ins, outs, args, mib=16, scratch=(), grid=(), aliases={}):
        return pl.pallas_call(
            kernel,
            grid=grid,
            in_specs=ins,
            out_specs=tuple(spec for spec, _ in outs),
            out_shape=tuple(shape for _, shape in outs),
            scratch_shapes=list(scratch),
            input_output_aliases=aliases,
            compiler_params=params(mib),
            name=name,
        )(*args)

    def whole(shape, kind=f32):
        return (VMEM, jax.ShapeDtypeStruct(shape, kind))

    in_order = own % 128 != 0
    per_cell = [cell_counts, cell_seeds, cell_factor]
    if in_order:
        per_cell = [
            jnp.concatenate(
                [
                    lax.dynamic_slice_in_dim(x, (column * plane + (spot ^ k)) * own, own)
                    for k in range(plane)
                ]
            )
            for x in per_cell
        ]
    per_cell = [jnp.stack(per_cell[:2]).reshape(2, -1, 128), per_cell[2].reshape(-1, 128)]
    batch_lines, noise = batch_ids.reshape(-1, 128), noise_draw.T
    if in_order:
        at = (column * plane + spot) * own
        batch_lines = lax.dynamic_slice_in_dim(batch_ids, at, own).reshape(1, own)
        noise = lax.dynamic_slice_in_dim(noise, at, own, axis=1)
    masks, factors = call(
        functools.partial(mask_kernel, total, width, plane, own, in_order),
        "masks",
        [
            pl.BlockSpec(per_cell[0].shape, lambda i: (0, 0, 0)),
            pl.BlockSpec(per_cell[1].shape, lambda i: (0, 0)),
        ],
        [
            (pl.BlockSpec((HEIGHT, regions), lambda i: (i, 0)), jax.ShapeDtypeStruct((share, regions), bf16)),
            (pl.BlockSpec((share + 8, 128), lambda i: (0, 0)), jax.ShapeDtypeStruct((share + 8, 128), f32)),
        ],
        per_cell,
        scratch=[
            pltpu.VMEM((7, share // 128, 128), jnp.int32),
            pltpu.VMEM((share // 128, 128), f32),
        ],
        grid=(share // HEIGHT,),
    )

    enc_blocks = gather_column(enc_weight.astype(bf16), factors)
    partials = {}
    early, late = [], []
    for g in [*range(1, groups), 0]:
        (partials[g],) = call(
            functools.partial(encode_kernel, width, g),
            "encode",
            [VMEM] * (1 + 2 * COLUMNS),
            [whole((block, 128))],
            [masks, *enc_blocks],
        )
        if g:
            (late if g == 3 else early).extend(scatter_group(partials[g], g))
        elif each > 1:
            late += scatter_group(partials[0], 0)[1:]
    (partial,) = call(
        add_kernel, "add", [VMEM] * (1 + len(early)), [whole((own, 128))], [partials[0], *early]
    )
    pre_parts = [partial, *late]

    dec_low, vec_low, _ = lax.optimization_barrier(
        (dec_weight, region_vecs, (early[0], partials[0]))
    )
    dec_send = jnp.concatenate([dec_low, vec_low, jnp.zeros((15, width), f32)], axis=0).astype(bf16)
    dec_blocks = gather_column(dec_send)
    dec_pack, lines, small = call(
        functools.partial(pack_kernel, rows.gain),
        "pack",
        [VMEM] * (1 + 2 * COLUMNS),
        [
            whole((COLUMNS, 256, width), bf16),
            whole((COLUMNS, 32, width)),
            (SMEM, jax.ShapeDtypeStruct((1,), jnp.int32)),
        ],
        [trunk_rows, *dec_blocks],
    )

    decoded_low, saved, loss_tile = call(
        functools.partial(forward_kernel, len(pre_parts), latent, own, in_order, plane),
        "forward",
        [VMEM] * (4 + len(pre_parts) + 1),
        [whole((own, 128), bf16), whole((10, own, 128)), (VMEM, tile)],
        [batch_lines, noise, trunk_rows, head_across, *pre_parts, masks],
        scratch=[pltpu.VMEM((2, 128, 128), f32)],
    )

    low_groups = gather_plane(decoded_low)
    sums = []
    back_parts = []
    for g in [*range(1, groups), 0]:
        early = back_parts[: (groups - 2) * each] if g == 0 else []
        *sums, back, loss_tile = call(
            functools.partial(decode_kernel, loss_scale, g, len(early)),
            "decode",
            [SMEM] + [VMEM] * (7 + len(sums) + len(early)),
            [
                whole((COLUMNS, 72, width)),
                whole((COLUMNS, 72, width)),
                whole((block, 128)),
                (VMEM, tile),
            ],
            [small, low_groups[g], masks, factors, dec_pack, lines, saved, loss_tile, *sums, *early],
            scratch=[
                pltpu.VMEM((block, width), f32),
                pltpu.VMEM((block, width), bf16),
                pltpu.VMEM((block, 256), bf16),
                pltpu.VMEM((144, block), bf16),
            ],
            aliases={8: 0, 9: 1} if sums else {},
        )
        if g == 0:
            back_parts = [back] + back_parts[len(early) :]
            if each > 1:
                back_parts += scatter_group(back, 0)[1:]
        else:
            back_parts += scatter_group(back, g)

    def send_sums(mine, other, name, after=()):
        other = over_dp(other)
        blocks = call(
            functools.partial(sum_kernel, name == "dec_sum"),
            name,
            [VMEM] * (2 + len(after)),
            [whole((80, width), jnp.int16)] * (COLUMNS - 1),
            [mine, other, *after],
        )
        return [mine, other] + [to_column(blocks[j - 1], j) for j in (2, 1, 3)]

    dec_parts = send_sums(*sums, "dec_sum")

    pre_low, trunk_mine, trunk_other = call(
        functools.partial(backward_kernel, len(back_parts), latent, loss_scale),
        "backward",
        [VMEM] * (4 + len(back_parts)),
        [whole((own, 128), bf16), whole((COLUMNS, PIECE, 128)), whole((COLUMNS, PIECE, 128))],
        [masks, trunk_rows, head_across, saved, *back_parts],
        scratch=[pltpu.VMEM((320, 128), f32), pltpu.VMEM((128, 128), f32)],
    )

    pre_groups = gather_plane(pre_low)
    enc_mine, enc_other, loss_tile = call(
        functools.partial(encode_back_kernel, groups),
        "encode_back",
        [VMEM] * (5 + groups),
        [whole((COLUMNS, 72, width)), whole((COLUMNS, 72, width)), (VMEM, tile)],
        [masks, lines, loss_tile, trunk_mine, trunk_other, *pre_groups],
        scratch=[pltpu.VMEM((144, share), bf16)],
    )
    like = lambda *arrays: [whole(x.shape) for x in arrays]
    dec_first_new, dec_second_new, dec_update, vec_first_new, vec_second_new, vec_update, dec_stats = call(
        functools.partial(dec_lamb_kernel, loss_scale),
        "dec_lamb",
        [VMEM] * (6 + len(dec_parts)),
        like(*[dec_weight] * 3, *[region_vecs] * 3) + [(VMEM, tile)],
        [dec_weight, dec_first, dec_second, region_vecs, vec_first, vec_second, *dec_parts],
    )
    enc_parts = send_sums(enc_mine, enc_other, "enc_sum")
    stat_tiles = [dec_stats, loss_tile]
    enc_first_new, enc_second_new, enc_update, last = call(
        enc_lamb_kernel,
        "enc_lamb",
        [VMEM] * (4 + COLUMNS + len(stat_tiles)),
        like(*[enc_weight] * 3) + [whole((8 + PIECE, 128))],
        [enc_weight, enc_first, enc_second, *enc_parts, *stat_tiles],
    )
    last = last + sum(over_plane(last, k) for k in range(1, plane))
    lasts = [last] + [from_column(last, j) for j in range(1, COLUMNS)]
    last = jnp.concatenate([sum(x[0:8] for x in lasts), *(x[8:] for x in lasts)], axis=0)
    last_parts = [last, over_dp(last)]
    (
        loss,
        enc_new,
        enc_copy,
        dec_new,
        dec_copy,
        vecs_new,
        norms,
        trunk_new,
        trunk_first_new,
        trunk_second_new,
        head_new,
        head_first_new,
        head_second_new,
    ) = call(
        functools.partial(final_kernel, latent, loss_scale, all_cells),
        "final",
        [VMEM] * (len(last_parts) + 12),
        [
            (SMEM, jax.ShapeDtypeStruct((2,), f32)),
            whole(enc_weight.shape),
            whole(enc_weight.shape, bf16),
            whole(dec_weight.shape),
            whole(dec_weight.shape, bf16),
            whole(region_vecs.shape),
            whole((2, 10)),
            *like(*[trunk_rows] * 3, *[head_across] * 3),
        ],
        [
            *last_parts,
            enc_weight,
            enc_update,
            dec_weight,
            dec_update,
            region_vecs,
            vec_update,
            trunk_rows,
            trunk_first,
            trunk_second,
            head_across,
            head_first,
            head_second,
        ],
        scratch=[pltpu.VMEM((2 * COLUMNS * PIECE, 128), f32)],
    )
    return (
        loss,
        enc_new.T,
        enc_first_new.T,
        enc_second_new.T,
        enc_copy.T,
        dec_new,
        dec_first_new,
        dec_second_new,
        dec_copy,
        vecs_new,
        vec_first_new,
        vec_second_new,
        trunk_new,
        trunk_first_new,
        trunk_second_new,
        head_new.T,
        head_first_new.T,
        head_second_new.T,
        norms,
    )


def solution(mesh):
    regions = mesh.shape["region"]
    devices = mesh.devices.reshape(mesh.shape["dp"], COLUMNS, regions // COLUMNS)
    inner = Mesh(devices, ("dp", "column", "plane"))
    across = ("column", "plane")
    by_row, by_line = P(across, "dp"), P("dp", across)
    return jax.shard_map(
        on_device,
        mesh=inner,
        in_specs=(P("dp"), P("dp"), P("dp"), P("dp", None), P("dp"))
        + (by_row,) * 3
        + (by_line,) * 6
        + (P(),) * 6,
        out_specs=(P(),) + (by_row,) * 4 + (by_line,) * 7 + (P(),) * 7,
        check_vma=False,
    )
```
